32 devices in a mesh: section: 2 (over core), dp: 4 (over z), group: 4 (over y, x).
Axes of the slice: x: 2, y: 2, z: 4, core: 2. Of those that a mesh axis runs over, the one named last changes fastest.
Arguments:
- tokens: bfloat16 [8192, 1024], P(('dp', 'group')), may hold values from -6 to 6
- cotangent: bfloat16 [8192, 1024], P(('dp', 'group')), may hold values from -6 to 6
- mem_keys: bfloat16 [32, 256, 1024], P(('dp', 'group')), may hold values from -6 to 6
- mem_values: bfloat16 [32, 256, 1024], P(('dp', 'group')), may hold values from -6 to 6
- mem_index: int32 [32, 128], P(('dp', 'group')), may hold values from 0 to 255, all different within a row
- mem_flags: int32 [32], P(('dp', 'group')), may hold values 0 or 1
- norm_attn: bfloat16 [2, 1024], P('section'), may hold values from 0.5 to 1.5
- w_qkv: bfloat16 [2, 1024, 3072], P('section'), may hold values from -0.1875 to 0.1875
- w_out: bfloat16 [2, 1024, 1024], P('section'), may hold values from -0.75 to 0.75
- norm_ffn: bfloat16 [2, 1024], P('section'), may hold values from 0.5 to 1.5
- w_gate_up: bfloat16 [2, 1024, 5632], P('section'), may hold values from -0.1875 to 0.1875
- w_down: bfloat16 [2, 2816, 1024], P('section'), may hold values from -0.109375 to 0.109375
Outputs:
- activations: bfloat16 [2, 8192, 1024], P('section', ('dp', 'group'))
- input_grads: bfloat16 [2, 8192, 1024], P('section', ('dp', 'group'))
- grad_norm_attn: float32 [2, 1024], P('section', 'dp')
- grad_w_qkv: float32 [2, 1024, 3072], P('section', 'dp')
- grad_w_out: float32 [2, 1024, 1024], P('section', 'dp')
- grad_norm_ffn: float32 [2, 1024], P('section', 'dp')
- grad_w_gate_up: float32 [2, 1024, 5632], P('section', 'dp')
- grad_w_down: float32 [2, 2816, 1024], P('section', 'dp')
The draws below stay inside these ranges and needn't reach their ends.
Inputs may be any that keep to these rules, and one draw needn't show every extreme that they name: `mem_index`: each row names 128 different memory rows.
All inputs are finite; a program needn't handle non-finite values. No bound on the sum of `mem_flags` on one device may be relied on, other than what follows from the above.
Results may differ from the reference program's by a relative error of at most 0.03.
Values may be sent and summed in bfloat16 or wider, within the bound.
A program may use at most 256 MiB of HBM per device.

```python
import jax
import jax.numpy as jnp
from jax import lax

D = 1024
HEADS = 8
HEAD_DIM = 128
FF = 2816
SEG = 256
MEM = 256
TOPM = 128
TOKENS = 8192
SEGS = 32


def touch_ends(drawn, rng, smallest, largest):
    index_at = [jax.random.randint(jax.random.fold_in(rng, axis), (), 0, length) for axis, length in enumerate(drawn.shape)]
    main_axis = drawn.shape.index(max(drawn.shape))
    next_to = index_at[:main_axis] + [(index_at[main_axis] + 1) % drawn.shape[main_axis]] + index_at[main_axis + 1:]
    return drawn.at[tuple(index_at)].set(smallest).at[tuple(next_to)].set(largest)


def strengthened(values, key, source, target, blocks, factor):
    def block_of(dim):
        return (jnp.arange(values.shape[dim]) // (values.shape[dim] // blocks)).reshape((-1,) + (1,) * (values.ndim - 1 - dim))

    one_side = jax.random.permutation(key, blocks)[block_of(target)]
    far = (block_of(target) + blocks // 2) % blocks
    return jnp.where((block_of(source) == one_side) | (block_of(source) == far), factor * values, values)


def block_scale(rng, extent, shards, low, largest):
    def one(position, shards_of):
        heights = jax.random.uniform(jax.random.fold_in(jax.random.fold_in(rng, 6), position), (shards_of,), jnp.float32, low / len(shards), largest / len(shards))
        return jnp.repeat(jnp.exp(heights), extent[position] // shards_of).reshape((-1,) + (1,) * (len(extent) - position - 1))

    factor_of = one(*shards[0])
    for cut in shards[1:]:
        factor_of = factor_of * one(*cut)
    return factor_of


def distinct(key, rows, count, top, lift):
    ranking = jax.random.permutation(jax.random.fold_in(key, 1), count)
    pull = ranking
    for power in range(3):
        pull = pull * pull // count
    pull = pull * lift // count
    chance = jax.random.randint(jax.random.fold_in(key, 2), (rows, count), 0, 4096) + pull
    holders = jax.random.permutation(jax.random.fold_in(key, 3), rows)[jnp.arange(count) % rows]
    chance = jnp.where(jnp.arange(rows)[:, None] == holders[None, :], 1 << 14, chance)
    priority = chance * count + jnp.arange(count)
    return lax.top_k(priority.astype(jnp.int32), top)[1].astype(jnp.int32)


def centred(rng, dims, scale, reach, pieces=(), kind=jnp.bfloat16):
    gain = block_scale(rng, dims, pieces, -0.22, 0.18) if pieces else 1.0
    entries = jax.random.normal(rng, dims, jnp.float32) * scale * gain
    return jnp.minimum(jnp.maximum(entries, -reach), reach).astype(kind)


def noise_with(stream_key, shape, spread, limit, shards, heavy, held_as=jnp.bfloat16):
    entries = spread * jax.random.normal(stream_key, shape, jnp.float32)
    if shards:
        entries = entries * block_scale(stream_key, shape, shards, -0.22, 0.18)
    return jnp.clip(strengthened(entries, jax.random.fold_in(stream_key, 3), *heavy), -limit, limit).astype(held_as)


def setup_inputs(seed: int = 0) -> dict:
    keys = jax.random.split(jax.random.key(seed), 13)
    tokens = centred(keys[0], (TOKENS, D), 1.0, 6.0, ((0, 16),))
    cotangent = noise_with(keys[1], (TOKENS, D), 1.0, 6.0, ((0, 16),), (0, 1, 16, 2.0))
    mem_keys = centred(keys[2], (SEGS, MEM, D), 1.0, 6.0, ((0, 16),))
    mem_values = centred(keys[3], (SEGS, MEM, D), 1.0, 6.0, ((0, 16),))
    mem_index = distinct(keys[4], SEGS, MEM, TOPM, 0)
    mem_flags = touch_ends((jax.random.randint(keys[5], (SEGS,), 0, 2) < 1).astype(jnp.int32), jax.random.fold_in(keys[5], 1), 0, 1)
    norm_attn = jnp.clip(1.0 + 0.1 * jax.random.normal(keys[6], (2, D), jnp.float32), 0.5, 1.5).astype(jnp.bfloat16)
    w_qkv = centred(keys[7], (2, D, 3 * D), D ** -0.5, 0.1875, ((0, 2),))
    w_out = centred(keys[8], (2, D, D), (D // 16) ** -0.5, 0.75, ((0, 2),))
    norm_ffn = jnp.clip(1.0 + 0.1 * jax.random.normal(keys[9], (2, D), jnp.float32), 0.5, 1.5).astype(jnp.bfloat16)
    w_gate_up = centred(keys[10], (2, D, 2 * FF), D ** -0.5, 0.1875, ((0, 2),))
    w_down = centred(keys[11], (2, FF, D), FF ** -0.5, 0.109375, ((0, 2),))
    return dict(tokens=tokens, cotangent=cotangent, mem_keys=mem_keys, mem_values=mem_values, mem_index=mem_index, mem_flags=mem_flags, norm_attn=norm_attn, w_qkv=w_qkv, w_out=w_out, norm_ffn=norm_ffn, w_gate_up=w_gate_up, w_down=w_down)


@jax.custom_vjp
def low(v):
    return lax.optimization_barrier(v.astype(jnp.bfloat16)).astype(jnp.float32)

@jax.custom_vjp
def low_back(v):
    return v

def low_keep(v):
    return (low(v), None)

def low_pass(kept, grad):
    return (grad,)

def back_keep(v):
    return (v, None)

def back_low(kept, grad):
    return (low(grad),)
low.defvjp(low_keep, low_pass)
low_back.defvjp(back_keep, back_low)
EPS = 1e-05
NEG = -1e+30
HIGH = lax.Precision.HIGHEST

def matmul(left, right):
    return jnp.dot(left, right, precision=HIGH, preferred_element_type=jnp.float32)

def rotary_tables(length, size):
    half = size // 2
    freqs = jnp.exp(-jnp.log(10000.0) * jnp.arange(half, dtype=jnp.float32) * 2.0 / size)
    angles = jnp.arange(length, dtype=jnp.float32)[:, None] * freqs[None, :]
    cosine = jnp.concatenate([jnp.cos(angles), jnp.cos(angles)], axis=1)
    sine = jnp.concatenate([jnp.sin(angles), jnp.sin(angles)], axis=1)
    return (cosine, sine)

def rotate(values, cosine, sine):
    half = values.shape[-1] // 2
    turned = jnp.concatenate([-values[..., half:], values[..., :half]], axis=-1)
    return values * cosine[:, None, :] + turned * sine[:, None, :]

def attend_segment(query, key_rot, values_loc, mem_key, mem_value, flag):
    scale = HEAD_DIM ** (-0.5)
    length = query.shape[0]
    causal = jnp.arange(length)[:, None] >= jnp.arange(length)[None, :]
    local = low_back(jnp.einsum('qhe,khe->hqk', query, key_rot, precision=HIGH) * scale)
    scores = jnp.where(causal[None], local, NEG)
    if mem_key is not None:
        remote = low_back(jnp.einsum('qhe,mhe->hqm', query, mem_key, precision=HIGH) * scale)
        remote = jnp.where(flag > 0, remote, NEG)
        scores = jnp.concatenate([scores, remote], axis=-1)
    peak_score = lax.optimization_barrier(jnp.max(scores, axis=-1, keepdims=True))
    weights = jnp.exp(scores - peak_score)
    probs = low(weights / lax.optimization_barrier(jnp.sum(weights, axis=-1, keepdims=True)))
    result = jnp.einsum('hqk,khe->qhe', probs[..., :length], values_loc, precision=HIGH)
    if mem_key is not None:
        result = result + jnp.einsum('hqm,mhe->qhe', probs[..., length:], mem_value, precision=HIGH)
    return result

def select_rows(cache, indices):
    return jax.vmap(lambda table_rows, picked: jnp.take(table_rows, picked, axis=0))(cache, indices)

def layer(inputs, params, memory):
    gain_attn, weight_qkv, weight_out, gain_ffn, weight_gu, weight_down = params
    row_count = inputs.shape[0]
    segments = row_count // SEG
    normed = low(inputs * lax.rsqrt(lax.optimization_barrier(jnp.mean(inputs * inputs, axis=-1, keepdims=True)) + EPS) * gain_attn)
    mixed = low_back(matmul(normed, weight_qkv)).reshape(segments, SEG, 3, HEADS, HEAD_DIM)
    cosine, sine = rotary_tables(SEG, HEAD_DIM)
    query = low(rotate(mixed[:, :, 0], cosine, sine))
    key_rot = low(rotate(mixed[:, :, 1], cosine, sine))
    values_loc = low(mixed[:, :, 2])
    if memory is None:

        def plain_block(blocks):
            return attend_segment(blocks[0], blocks[1], blocks[2], None, None, None)
        attended = lax.map(jax.checkpoint(plain_block), (query, key_rot, values_loc))
    else:
        cache_keys, cache_values, indices, flags = memory
        chosen_keys = select_rows(cache_keys, indices).reshape(segments, TOPM, HEADS, HEAD_DIM)
        chosen_values = select_rows(cache_values, indices).reshape(segments, TOPM, HEADS, HEAD_DIM)

        def memory_block(blocks):
            return attend_segment(blocks[0], blocks[1], blocks[2], blocks[3], blocks[4], blocks[5])
        attended = lax.map(jax.checkpoint(memory_block), (query, key_rot, values_loc, chosen_keys, chosen_values, flags))
    attended = low(low_back(attended.reshape(row_count, D)))
    resid = inputs + low_back(matmul(attended, weight_out))
    normed_ffn = low(resid * lax.rsqrt(lax.optimization_barrier(jnp.mean(resid * resid, axis=-1, keepdims=True)) + EPS) * gain_ffn)
    gate_up = low_back(matmul(normed_ffn, weight_gu))
    hidden = low(jax.nn.silu(gate_up[:, :FF]) * gate_up[:, FF:])
    return resid + low_back(matmul(hidden, weight_down))

def reference(tokens, cotangent, mem_keys, mem_values, mem_index, mem_flags, norm_attn, w_qkv, w_out, norm_ffn, w_gate_up, w_down):
    weights = (norm_attn, w_qkv, w_out, norm_ffn, w_gate_up, w_down)
    lower_params = tuple((item[0].astype(jnp.float32) for item in weights))
    upper_params = tuple((item[1].astype(jnp.float32) for item in weights))
    segments = TOKENS // SEG
    per_step = max((count_try for count_try in (8, 4, 2, 1) if segments % count_try == 0))
    steps_total = segments // per_step

    def blocked(array):
        return array.reshape((steps_total, -1) + array.shape[1:])
    blocks = (blocked(tokens.astype(jnp.float32)), blocked(cotangent.astype(jnp.float32)), blocked(mem_keys.astype(jnp.float32)), blocked(mem_values.astype(jnp.float32)), blocked(mem_index), blocked(mem_flags))

    def step(carry, block):
        inputs, grad_top, cache_keys, cache_values, indices, flags = block

        def lower(lower_in, params):
            return low(low_back(layer(lower_in, params, None)))

        def upper(upper_in, params):
            return layer(upper_in, params, (cache_keys, cache_values, indices, flags))
        middle, lower_vjp = jax.vjp(lower, inputs, lower_params)
        top, upper_vjp = jax.vjp(upper, middle, upper_params)
        grad_middle, grad_upper = upper_vjp(grad_top)
        grad_inputs, grad_lower = lower_vjp(grad_middle)
        sums_lower = tuple((left + right for left, right in zip(carry[0], grad_lower)))
        sums_upper = tuple((left + right for left, right in zip(carry[1], grad_upper)))
        return ((sums_lower, sums_upper), (middle, top, grad_inputs, grad_middle))
    zeros = tuple((jnp.zeros_like(item) for item in lower_params))
    (sums_lower, sums_upper), (middles, tops, grads_in, grads_mid) = lax.scan(step, (zeros, zeros), blocks)
    activations = jnp.stack([middles.reshape(TOKENS, D), tops.reshape(TOKENS, D)]).astype(jnp.bfloat16)
    input_grads = jnp.stack([grads_in.reshape(TOKENS, D), grads_mid.reshape(TOKENS, D)]).astype(jnp.bfloat16)
    stacked = tuple((jnp.stack([left, right]) for left, right in zip(sums_lower, sums_upper)))
    return (activations, input_grads, stacked[0], stacked[1], stacked[2], stacked[3], stacked[4], stacked[5])
```

```python
import functools

import jax
import jax.numpy as jnp
from jax import lax
from jax.experimental import pallas as pl
from jax.experimental.pallas import tpu as pltpu
from jax.sharding import PartitionSpec as P

D = 1024
HEADS = 8
HEAD_DIM = 128
FF = 2816
SEG = 256
TOPM = 128
MICRO = 2


EPS = 1e-05
NEG = -1e30
MESH = pl.DeviceIdType.MESH


def from_behind(block, axis, distance):
    devices = range(lax.axis_size(axis))
    route = [(i - distance, i) for i in devices if i - distance in devices]
    return lax.ppermute(block, axis, route)


def rotary_tables(length, size):
    half = size // 2
    freqs = jnp.exp(-jnp.log(10000.0) * jnp.arange(half, dtype=jnp.float32) * 2.0 / size)
    angles = jnp.arange(length, dtype=jnp.float32)[:, None] * freqs[None, :]
    cosine = jnp.concatenate([jnp.cos(angles), jnp.cos(angles)], axis=1)
    sine = jnp.concatenate([jnp.sin(angles), jnp.sin(angles)], axis=1)
    return (cosine, sine)


def rotate(values, cosine, sine):
    half = values.shape[-1] // 2
    turned = jnp.concatenate([-values[..., half:], values[..., :half]], axis=-1)
    return values * cosine[:, None, :] + turned * sine[:, None, :]


def rotate_back(grads, cosine, sine):
    half = grads.shape[-1] // 2
    moved = grads * sine[:, None, :]
    return grads * cosine[:, None, :] + jnp.concatenate(
        [moved[..., half:], -moved[..., :half]], axis=-1
    )


def contract_cols(left, right):
    return lax.dot_general(
        left, right, (((1,), (1,)), ((), ())), preferred_element_type=jnp.float32
    )


def score_blocks(query, key_rot, keys_mem, flags):
    scale = HEAD_DIM ** (-0.5)
    causal = jnp.arange(SEG)[:, None] >= jnp.arange(SEG)[None, :]
    local = (
        jnp.einsum("gqhe,gkhe->ghqk", query, key_rot, preferred_element_type=jnp.float32) * scale
    )
    local = jnp.where(causal, local, NEG)
    remote = (
        jnp.einsum("gqhe,gmhe->ghqm", query, keys_mem, preferred_element_type=jnp.float32) * scale
    )
    remote = jnp.where(flags[:, None, None, None] > 0, remote, NEG)
    return (local, remote)


def forward_layer(layer_input, params, memory):
    gain_attn, weight_qkv, weight_out, gain_ffn, weight_gu, weight_down = params
    keys_mem, values_mem, flags = memory
    row_count = layer_input.shape[0]
    segments = row_count // SEG
    inputs_f = layer_input.astype(jnp.float32)
    first_scale = lax.rsqrt(jnp.mean(inputs_f * inputs_f, axis=-1, keepdims=True) + EPS)
    normed_attn = (inputs_f * first_scale * gain_attn.astype(jnp.float32)).astype(jnp.bfloat16)
    mixed = jnp.dot(normed_attn, weight_qkv, preferred_element_type=jnp.float32)
    mixed = mixed.reshape(segments, SEG, 3, HEADS, HEAD_DIM)
    cosine, sine = rotary_tables(SEG, HEAD_DIM)
    query = rotate(mixed[:, :, 0], cosine, sine).astype(jnp.bfloat16)
    key_rot = rotate(mixed[:, :, 1], cosine, sine).astype(jnp.bfloat16)
    values_loc = mixed[:, :, 2].astype(jnp.bfloat16)
    local, remote = score_blocks(query, key_rot, keys_mem, flags)
    peak_score = jnp.maximum(jnp.max(local, axis=-1), jnp.max(remote, axis=-1))
    totals = jnp.sum(jnp.exp(local - peak_score[..., None]), axis=-1) + jnp.sum(
        jnp.exp(remote - peak_score[..., None]), axis=-1
    )
    log_total = peak_score + jnp.log(totals)
    prob_local = jnp.exp(local - log_total[..., None]).astype(jnp.bfloat16)
    prob_remote = jnp.exp(remote - log_total[..., None]).astype(jnp.bfloat16)
    attended = jnp.einsum(
        "ghqk,gkhe->gqhe", prob_local, values_loc, preferred_element_type=jnp.float32
    )
    attended = attended + jnp.einsum(
        "ghqm,gmhe->gqhe", prob_remote, values_mem, preferred_element_type=jnp.float32
    )
    attended = attended.reshape(row_count, D).astype(jnp.bfloat16)
    resid = inputs_f + jnp.dot(attended, weight_out, preferred_element_type=jnp.float32)
    second_scale = lax.rsqrt(jnp.mean(resid * resid, axis=-1, keepdims=True) + EPS)
    normed_ffn = (resid * second_scale * gain_ffn.astype(jnp.float32)).astype(jnp.bfloat16)
    gate_up = jnp.dot(normed_ffn, weight_gu, preferred_element_type=jnp.float32)
    hidden = (jax.nn.silu(gate_up[:, :FF]) * gate_up[:, FF:]).astype(jnp.bfloat16)
    output = resid + jnp.dot(hidden, weight_down, preferred_element_type=jnp.float32)
    kept = (
        first_scale,
        normed_attn,
        query,
        key_rot,
        values_loc,
        log_total,
        attended,
        resid,
        second_scale,
        normed_ffn,
        gate_up,
        hidden,
    )
    return (output, kept)


def backward_inputs(layer_input, grad_out, kept, params, memory):
    gain_attn, weight_qkv, weight_out, gain_ffn, weight_gu, weight_down = params
    keys_mem, values_mem, flags = memory
    (
        first_scale,
        normed_attn,
        query,
        key_rot,
        values_loc,
        log_total,
        attended,
        resid,
        second_scale,
        normed_ffn,
        gate_up,
        hidden,
    ) = kept
    row_count = layer_input.shape[0]
    segments = row_count // SEG
    inputs_f = layer_input.astype(jnp.float32)
    grad_branch = grad_out.astype(jnp.bfloat16)
    grad_hidden = contract_cols(grad_branch, weight_down)
    gate_part = gate_up[:, :FF]
    up_part = gate_up[:, FF:]
    sigmoid_gate = jax.nn.sigmoid(gate_part)
    grad_gate = grad_hidden * up_part * sigmoid_gate * (1.0 + gate_part * (1.0 - sigmoid_gate))
    grad_up = grad_hidden * gate_part * sigmoid_gate
    grad_gu = jnp.concatenate([grad_gate, grad_up], axis=1).astype(jnp.bfloat16)
    grad_normed = contract_cols(grad_gu, weight_gu)
    scaled_ffn = grad_normed * gain_ffn.astype(jnp.float32)
    grad_gain_ffn = jnp.sum(grad_normed * resid * second_scale, axis=0)
    grad_resid = (
        grad_out
        + second_scale * scaled_ffn
        - resid * second_scale**3 * jnp.mean(scaled_ffn * resid, axis=-1, keepdims=True)
    )
    grad_attn_out = grad_resid.astype(jnp.bfloat16)
    grad_attended = (
        contract_cols(grad_attn_out, weight_out)
        .astype(jnp.bfloat16)
        .reshape(segments, SEG, HEADS, HEAD_DIM)
    )
    local, remote = score_blocks(query, key_rot, keys_mem, flags)
    prob_local = jnp.exp(local - log_total[..., None])
    prob_remote = jnp.exp(remote - log_total[..., None])
    grad_values = jnp.einsum(
        "ghqk,gqhe->gkhe",
        prob_local.astype(jnp.bfloat16),
        grad_attended,
        preferred_element_type=jnp.float32,
    )
    grad_plocal = jnp.einsum(
        "gqhe,gkhe->ghqk", grad_attended, values_loc, preferred_element_type=jnp.float32
    )
    grad_premote = jnp.einsum(
        "gqhe,gmhe->ghqm", grad_attended, values_mem, preferred_element_type=jnp.float32
    )
    centre = jnp.sum(prob_local * grad_plocal, axis=-1) + jnp.sum(
        prob_remote * grad_premote, axis=-1
    )
    grad_slocal = (prob_local * (grad_plocal - centre[..., None])).astype(jnp.bfloat16)
    grad_sremote = (prob_remote * (grad_premote - centre[..., None])).astype(jnp.bfloat16)
    scale = HEAD_DIM ** (-0.5)
    grad_query = scale * (
        jnp.einsum("ghqk,gkhe->gqhe", grad_slocal, key_rot, preferred_element_type=jnp.float32)
        + jnp.einsum("ghqm,gmhe->gqhe", grad_sremote, keys_mem, preferred_element_type=jnp.float32)
    )
    grad_key = scale * jnp.einsum(
        "ghqk,gqhe->gkhe", grad_slocal, query, preferred_element_type=jnp.float32
    )
    cosine, sine = rotary_tables(SEG, HEAD_DIM)
    grad_mixed = jnp.stack(
        [rotate_back(grad_query, cosine, sine), rotate_back(grad_key, cosine, sine), grad_values],
        axis=2,
    )
    grad_mixed = grad_mixed.reshape(row_count, 3 * D).astype(jnp.bfloat16)
    grad_normed_attn = contract_cols(grad_mixed, weight_qkv)
    scaled_attn = grad_normed_attn * gain_attn.astype(jnp.float32)
    grad_gain_attn = jnp.sum(grad_normed_attn * inputs_f * first_scale, axis=0)
    grad_input = (
        grad_resid
        + first_scale * scaled_attn
        - inputs_f * first_scale**3 * jnp.mean(scaled_attn * inputs_f, axis=-1, keepdims=True)
    )
    pending = (
        grad_gain_attn,
        grad_gain_ffn,
        hidden,
        grad_branch,
        normed_ffn,
        grad_gu,
        attended,
        grad_attn_out,
        normed_attn,
        grad_mixed,
    )
    return (grad_input, pending)


BLOCK = 256
LAG = 2


def flip(value, mask):
    return value + mask * (1 - 2 * ((value // mask) % 2))


def summed(left, right):
    return (left.astype(jnp.float32) + right.astype(jnp.float32)).astype(jnp.bfloat16)


def reduce_kernel(extra, *refs):
    n_extra = len(extra)
    (nf_t, na_t, o_t, z_t, dgu, dm, f_cols, e_cols, gains) = refs[:9]
    (out_sq, out_d, out_gains) = refs[9:12]
    refs = refs[12:]
    (a_own, a_in, z_own, z_in, b_own, b_in, e_own, e_in) = refs[:8]
    (g_sq, q0, q1, q2, g_d, d0, d1, d2, gain_out, gain_in) = refs[8:18]
    refs = refs[18:]
    x_sq, x_d = refs[:2]
    (sem_load, sem_bload, sem_asend, sem_arecv, sem_bsend, sem_brecv) = refs[2:8]
    (sem_send, sem_recv, sem_copy, gain_send, gain_recv) = refs[8:13]

    section, dpi, group = (lax.axis_index(name) for name in ("section", "dp", "group"))
    mask1 = 1 + section
    mask2 = 2 - section
    half = (group // mask1) % 2
    low2 = (group // mask2) % 2
    bit0 = dpi % 2
    bit1 = (dpi // 2) % 2
    first = (section, dpi, flip(group, mask1))
    second = (section, dpi, flip(group, mask2))
    near = (section, flip(dpi, 1), group)
    far = (section, flip(dpi, 2), group)
    others = [(section, dpi, flip(group, mask)) for mask in extra]
    partners = [first, second, near, far] + others

    barrier = pltpu.get_barrier_semaphore()
    for partner in partners:
        pl.semaphore_signal(barrier, inc=1, device_id=partner, device_id_type=MESH)
    pl.semaphore_wait(barrier, len(partners))

    def remote(src, dst, send, recv, device):
        return pltpu.make_async_remote_copy(
            src_ref=src, dst_ref=dst, send_sem=send, recv_sem=recv, device_id=device, device_id_type=MESH
        )

    def load_a(slot):
        src = (nf_t, o_t, na_t)[slot]
        return pltpu.make_async_copy(src, a_own.at[slot], sem_load.at[slot])

    def load_z():
        return pltpu.make_async_copy(z_t.at[pl.ds(0, 4), half], z_own, sem_load.at[3])

    def b_src(index, part):
        if index[0] == 0:
            return dgu.at[part * 11 + index[1]]
        if index[0] == 1:
            return f_cols.at[part * 2 + index[1]]
        return dm.at[part * 6 + index[1]]

    def load_b(kind, i, slot):
        return pltpu.make_async_copy(b_src((kind, i), half), b_own.at[slot], sem_bload.at[slot])

    def load_e(k):
        return pltpu.make_async_copy(e_cols.at[k], e_own.at[k], sem_bload.at[19 + k])

    def send_a(slot):
        src = (nf_t, o_t, na_t)[slot]
        return remote(src, a_in.at[slot], sem_asend.at[slot], sem_arecv.at[slot], first)

    def send_z():
        return remote(z_t.at[pl.ds(0, 4), 1 - half], z_in, sem_asend.at[3], sem_arecv.at[3], first)

    def send_b(kind, i, slot):
        return remote(b_src((kind, i), 1 - half), b_in.at[slot], sem_bsend.at[slot], sem_brecv.at[slot], first)

    def send_e(k):
        return remote(e_cols.at[k], e_in.at[k], sem_bsend.at[19 + k], sem_brecv.at[19 + k], first)

    kinds = ((0, 0, 11), (1, 11, 2), (2, 13, 6))
    load_z().start()
    send_z().start()

    @pl.loop(0, 4)
    def _(k):
        load_e(k).start()
        send_e(k).start()

    for kind, base, count in kinds:
        load_a(kind).start()
        send_a(kind).start()

        @pl.loop(0, count)
        def _(i):
            load_b(kind, i, base + i).start()
            send_b(kind, i, base + i).start()

    class Square:
        base, rows = 4, 256
        partial, recv0, recv1, recv2, xs, out = g_sq, q0, q1, q2, x_sq, out_sq

    class Down:
        base, rows = 0, 352
        partial, recv0, recv1, recv2, xs, out = g_d, d0, d1, d2, x_d, out_d

    def to_near(cls, c):
        k = cls.base + c
        return remote(cls.partial.at[c, pl.ds(0, 2), 1 - bit0], cls.recv0.at[c], sem_send.at[0, k], sem_recv.at[0, k], near)

    def to_far(cls, c):
        k = cls.base + c
        return remote(cls.recv0.at[c, 1 - bit1], cls.recv1.at[c], sem_send.at[1, k], sem_recv.at[1, k], far)

    def rows_at(cls, part):
        size = cls.rows // 2
        return pl.ds(pl.multiple_of(part * size, 16), size)

    def to_second(cls, c):
        k = cls.base + c
        return remote(cls.recv1.at[c, rows_at(cls, 1 - low2)], cls.recv2.at[c], sem_send.at[2, k], sem_recv.at[2, k], second)

    def to_extra(cls, c, i):
        k = cls.base + c
        src = cls.recv2.at[c] if i == 0 else cls.xs.at[i - 1, c]
        return remote(src, cls.xs.at[i, c], sem_send.at[6 + i, k], sem_recv.at[6 + i, k], others[i])

    def final(cls, c):
        return cls.recv2.at[c] if n_extra == 0 else cls.xs.at[n_extra - 1, c]

    def share_second(cls, c):
        k = cls.base + c
        return remote(final(cls, c), cls.out.at[half, c, rows_at(cls, low2)], sem_send.at[3, k], sem_recv.at[3, k], second)

    def share_first(cls, c):
        k = cls.base + c
        return remote(final(cls, c), cls.out.at[half, c, rows_at(cls, low2)], sem_send.at[4, k], sem_recv.at[4, k], first)

    def pass_on(cls, c):
        k = cls.base + c
        block = cls.out.at[half, c, rows_at(cls, 1 - low2)]
        return remote(block, block, sem_send.at[5, k], sem_recv.at[5, k], first)

    def keep(cls, c):
        return pltpu.make_async_copy(final(cls, c), cls.out.at[half, c, rows_at(cls, low2)], sem_copy.at[cls.base + c])

    def multiply(left, right, left2, right2):
        total = jnp.dot(left, right, preferred_element_type=jnp.float32)
        total += jnp.dot(left2, right2, preferred_element_type=jnp.float32)
        return total.astype(jnp.bfloat16)

    def partial_square(c):
        for kind, base, count in kinds:

            @pl.when(c == base)
            def _():
                load_a(kind).wait()
                send_a(kind).wait_recv()

        load_b(0, 0, c).wait()
        send_b(0, 0, c).wait_recv()
        for kind, base, count in kinds:

            @pl.when((c >= base) & (c < base + count))
            def _():
                for j in range(4):
                    rows = pl.ds(j * 256, 256)
                    g_sq[c, j // 2, j % 2] = multiply(
                        a_own[kind, rows, :], b_own[c], a_in[kind, rows, :], b_in[c]
                    )

        to_near(Square, c).start()

    def partial_down(c):
        @pl.when(c == 0)
        def _():
            load_z().wait()
            send_z().wait_recv()

        load_e(c).wait()
        send_e(c).wait_recv()
        for j in range(4):
            g_d[c, j // 2, j % 2] = multiply(z_own[j], e_own[c], z_in[j], e_in[c])
        to_near(Down, c).start()

    def stage_near(cls, c):
        to_near(cls, c).wait_recv()
        for i in range(2):
            cls.recv0[c, i] = summed(cls.partial[c, i, bit0], cls.recv0[c, i])
        to_far(cls, c).start()

    def stage_far(cls, c):
        to_far(cls, c).wait_recv()
        cls.recv1[c] = summed(cls.recv0[c, bit1], cls.recv1[c])
        to_second(cls, c).start()

    def share(cls, c):
        share_second(cls, c).start()
        share_first(cls, c).start()
        keep(cls, c).start()

    def stage_second(cls, c):
        to_second(cls, c).wait_recv()
        cls.recv2[c] = summed(cls.recv1[c, rows_at(cls, low2)], cls.recv2[c])
        if n_extra:
            to_extra(cls, c, 0).start()
        else:
            share(cls, c)

    def stage_extra(cls, c, i):
        to_extra(cls, c, i).wait()
        mine = cls.recv2[c] if i == 0 else cls.xs[i - 1, c]
        cls.xs[i, c] = summed(mine, cls.xs[i, c])
        if i + 1 < n_extra:
            to_extra(cls, c, i + 1).start()
        else:
            share(cls, c)

    def stage_pass(cls, c):
        share_second(cls, c).wait_recv()
        pass_on(cls, c).start()

    def partial(cls, c):
        (partial_square if cls is Square else partial_down)(c)

    stages = [partial, stage_near, stage_far, stage_second]
    stages += [functools.partial(lambda i, cls, c: stage_extra(cls, c, i), i) for i in range(n_extra)]
    stages += [stage_pass]

    def gain_exchange(i):
        return remote(gain_out.at[i], gain_in.at[i], gain_send.at[i], gain_recv.at[i], partners[i])

    steps = 23 + LAG * (len(stages) - 1)

    @pl.loop(0, steps)
    def _(t):
        for i, stage in enumerate(stages):
            c = t - LAG * i

            @pl.when((c >= 0) & (c < 4))
            def _():
                stage(Down, c)

            @pl.when((c >= 4) & (c < 23))
            def _():
                stage(Square, c - 4)

        for i in range(len(partners)):

            @pl.when(t == 3 * i + 2)
            def _():
                if i == 0:
                    gain_out[0] = gains[...]
                else:
                    gain_exchange(i - 1).wait()
                    gain_out[i] = gain_out[i - 1] + gain_in[i - 1]
                gain_exchange(i).start()

    last = len(partners) - 1
    gain_exchange(last).wait()
    out_gains[...] = gain_out[last] + gain_in[last]

    send_z().wait_send()
    for kind, base, count in kinds:
        send_a(kind).wait_send()

    def finish(cls, c):
        to_near(cls, c).wait_send()
        to_far(cls, c).wait_send()
        to_second(cls, c).wait_send()
        share_second(cls, c).wait_send()
        share_first(cls, c).wait()
        pass_on(cls, c).wait()
        keep(cls, c).wait()

    @pl.loop(0, 4)
    def _(c):
        send_e(c).wait_send()
        finish(Down, c)

    @pl.loop(0, 19)
    def _(c):
        send_b(0, 0, c).wait_send()
        finish(Square, c)


def reduce_gradients(group_size, nf_t, na_t, o_t, z_t, dgu, dm, f_cols, e_cols, gains):
    extra = []
    mask = 4
    while mask < group_size:
        extra.append(mask)
        mask *= 2
    n_extra = len(extra)
    low = jnp.bfloat16
    tokens = nf_t.shape[1]
    scratch = [
        pltpu.VMEM((3, D, tokens), low),
        pltpu.VMEM((3, D, tokens), low),
        pltpu.VMEM((4, 352, tokens), low),
        pltpu.VMEM((4, 352, tokens), low),
        pltpu.VMEM((19, tokens, BLOCK), low),
        pltpu.VMEM((19, tokens, BLOCK), low),
        pltpu.VMEM((4, tokens, BLOCK), low),
        pltpu.VMEM((4, tokens, BLOCK), low),
        pltpu.VMEM((19, 2, 2, 256, BLOCK), low),
        pltpu.VMEM((19, 2, 256, BLOCK), low),
        pltpu.VMEM((19, 256, BLOCK), low),
        pltpu.VMEM((19, 128, BLOCK), low),
        pltpu.VMEM((4, 2, 2, 352, BLOCK), low),
        pltpu.VMEM((4, 2, 352, BLOCK), low),
        pltpu.VMEM((4, 352, BLOCK), low),
        pltpu.VMEM((4, 176, BLOCK), low),
        pltpu.VMEM((4 + n_extra, 8, D), jnp.float32),
        pltpu.VMEM((4 + n_extra, 8, D), jnp.float32),
        pltpu.VMEM((max(n_extra, 1), 19 if n_extra else 1, 128, BLOCK), low),
        pltpu.VMEM((max(n_extra, 1), 4 if n_extra else 1, 176, BLOCK), low),
        pltpu.SemaphoreType.DMA((4,)),
        pltpu.SemaphoreType.DMA((23,)),
        pltpu.SemaphoreType.DMA((4,)),
        pltpu.SemaphoreType.DMA((4,)),
        pltpu.SemaphoreType.DMA((23,)),
        pltpu.SemaphoreType.DMA((23,)),
        pltpu.SemaphoreType.DMA((6 + n_extra, 23)),
        pltpu.SemaphoreType.DMA((6 + n_extra, 23)),
        pltpu.SemaphoreType.DMA((23,)),
        pltpu.SemaphoreType.DMA((4 + n_extra,)),
        pltpu.SemaphoreType.DMA((4 + n_extra,)),
    ]
    anywhere = pl.BlockSpec(memory_space=pl.ANY)
    near_by = pl.BlockSpec(memory_space=pltpu.VMEM)
    return pl.pallas_call(
        functools.partial(reduce_kernel, tuple(extra)),
        out_shape=(
            jax.ShapeDtypeStruct((2, 19, 256, BLOCK), low),
            jax.ShapeDtypeStruct((2, 4, 352, BLOCK), low),
            jax.ShapeDtypeStruct((8, D), jnp.float32),
        ),
        in_specs=[anywhere] * 8 + [near_by],
        out_specs=(anywhere, anywhere, near_by),
        scratch_shapes=scratch,
        compiler_params=pltpu.CompilerParams(
            collective_id=0, has_side_effects=True, vmem_limit_bytes=58 * 2**20
        ),
        cost_estimate=pl.CostEstimate(flops=13 * 10**9, bytes_accessed=30 * 10**6, transcendentals=0),
        name="reduce_gradients",
    )(nf_t, na_t, o_t, z_t, dgu, dm, f_cols, e_cols, gains)


def column_blocks(array):
    return array.reshape(array.shape[0], -1, BLOCK).transpose(1, 0, 2)


def unblock(blocks):
    blocks = blocks.reshape(-1, *blocks.shape[-2:])
    return blocks.transpose(1, 0, 2).reshape(blocks.shape[1], -1).astype(jnp.float32)[None]


def unpack_gradients(out_sq, out_d, out_gains):
    start = lax.axis_index("dp") * BLOCK
    gains = lax.dynamic_slice(out_gains, (0, start), (2, BLOCK))
    down = out_d.transpose(0, 2, 1, 3).reshape(704, D).astype(jnp.float32)[None]
    return (
        gains[0:1],
        unblock(out_sq[:, 13:19]),
        unblock(out_sq[:, 11:13]),
        gains[1:2],
        unblock(out_sq[:, :11]),
        down,
    )


def body(
    group_size,
    tokens,
    cotangent,
    mem_keys,
    mem_values,
    mem_index,
    mem_flags,
    norm_attn,
    w_qkv,
    w_out,
    norm_ffn,
    w_gate_up,
    w_down,
):
    params = (norm_attn[0], w_qkv[0], w_out[0], norm_ffn[0], w_gate_up[0], w_down[0])
    upper_section = lax.axis_index("section") == 1
    mb_rows = tokens.shape[0] // MICRO
    mb_segs = mem_flags.shape[0] // MICRO
    picked_keys = jax.vmap(lambda table_rows, picked: jnp.take(table_rows, picked, axis=0))(
        mem_keys, mem_index
    )
    picked_values = jax.vmap(lambda table_rows, picked: jnp.take(table_rows, picked, axis=0))(
        mem_values, mem_index
    )
    picked_keys = picked_keys.reshape(-1, TOPM, HEADS, HEAD_DIM)
    picked_values = picked_values.reshape(-1, TOPM, HEADS, HEAD_DIM)
    live_flags = mem_flags * upper_section.astype(jnp.int32)

    def memory_for(micro):
        start = micro * mb_segs
        return (
            picked_keys[start : start + mb_segs],
            picked_values[start : start + mb_segs],
            live_flags[start : start + mb_segs],
        )

    def rows_of(array, micro):
        return array[micro * mb_rows : (micro + 1) * mb_rows]

    def pick(upper_tree, lower_tree):
        return jax.tree.map(
            lambda upper_leaf, lower_leaf: jnp.where(upper_section, upper_leaf, lower_leaf),
            upper_tree,
            lower_tree,
        )

    def forward_active(operands):
        return forward_layer(operands[0], params, operands[1])

    def forward_spare(operands):
        return jax.tree.map(jnp.zeros_like, forward_active(operands))

    received = jnp.zeros((mb_rows, D), jnp.bfloat16)
    tick_outputs = []
    tick_kept = []
    tick_inputs = []
    for tick_index in range(MICRO + 1):
        lower_micro = min(tick_index, MICRO - 1)
        upper_micro = max(tick_index - 1, 0)
        layer_input = jnp.where(upper_section, received, rows_of(tokens, lower_micro))
        memory = pick(memory_for(upper_micro), memory_for(lower_micro))
        busy = jnp.where(
            upper_section, jnp.asarray(tick_index >= 1), jnp.asarray(tick_index < MICRO)
        )
        output, kept = lax.cond(busy, forward_active, forward_spare, (layer_input, memory))
        output_low = output.astype(jnp.bfloat16)
        if tick_index < MICRO:
            received = from_behind(output_low, "section", 1)
        tick_outputs.append(output_low)
        tick_kept.append(kept)
        tick_inputs.append(layer_input)
    micro_outputs = [pick(tick_outputs[micro + 1], tick_outputs[micro]) for micro in range(MICRO)]

    def backward_active(operands):
        layer_input, grad_out, kept, memory = operands
        grad_input, pending = backward_inputs(layer_input, grad_out, kept, params, memory)
        return (grad_input, pending)

    def backward_spare(operands):
        return jax.tree.map(jnp.zeros_like, backward_active(operands))

    sent_back = jnp.zeros((mb_rows, D), jnp.bfloat16)
    tick_grads = []
    tick_results = []
    for tick_index in range(MICRO + 1):
        upper_micro = min(tick_index, MICRO - 1)
        lower_micro = max(tick_index - 1, 0)
        grad_out = jnp.where(
            upper_section,
            rows_of(cotangent, upper_micro).astype(jnp.float32),
            sent_back.astype(jnp.float32),
        )
        layer_input = pick(tick_inputs[upper_micro + 1], tick_inputs[lower_micro])
        memory = pick(memory_for(upper_micro), memory_for(lower_micro))
        kept = pick(tick_kept[upper_micro + 1], tick_kept[lower_micro])
        busy = jnp.where(
            upper_section, jnp.asarray(tick_index < MICRO), jnp.asarray(tick_index >= 1)
        )
        grad_input, result = lax.cond(
            busy, backward_active, backward_spare, (layer_input, grad_out, kept, memory)
        )
        grad_low = grad_input.astype(jnp.bfloat16)
        if tick_index < MICRO:
            sent_back = from_behind(grad_low, "section", -1)
        tick_grads.append(grad_low)
        tick_results.append(result)
    micro_results = [pick(tick_results[micro], tick_results[micro + 1]) for micro in range(MICRO)]
    gain_attn_sum = micro_results[0][0]
    gain_ffn_sum = micro_results[0][1]
    micro = 1
    gain_attn_sum = gain_attn_sum + micro_results[micro][0]
    gain_ffn_sum = gain_ffn_sum + micro_results[micro][1]
    joined = tuple(
        (jnp.concatenate([item[slot] for item in micro_results], axis=0) for slot in range(2, 10))
    )
    hidden, grad_branch, normed_ffn, grad_gu, attended, grad_attn_out, normed_attn, grad_mixed = joined
    gains = jnp.zeros((8, D), jnp.float32).at[0].set(gain_attn_sum).at[1].set(gain_ffn_sum)
    reduced = reduce_gradients(
        group_size,
        normed_ffn.T,
        normed_attn.T,
        attended.T,
        hidden.T.reshape(4, 2, 352, -1),
        column_blocks(grad_gu),
        column_blocks(grad_mixed),
        column_blocks(grad_attn_out),
        column_blocks(grad_branch),
        gains,
    )
    totals = unpack_gradients(*reduced)
    micro_grads = [pick(tick_grads[micro], tick_grads[micro + 1]) for micro in range(MICRO)]
    activations = jnp.concatenate(micro_outputs, axis=0)[None]
    input_grads = jnp.concatenate(micro_grads, axis=0)[None]
    return (
        activations,
        input_grads,
        totals[0],
        totals[1],
        totals[2],
        totals[3],
        totals[4],
        totals[5],
    )


def solution(mesh):
    placed = (
        P(("dp", "group"), None),
        P(("dp", "group"), None),
        P(("dp", "group"), None, None),
        P(("dp", "group"), None, None),
        P(("dp", "group"), None),
        P(("dp", "group")),
        P("section", None),
        P("section", None, None),
        P("section", None, None),
        P("section", None),
        P("section", None, None),
        P("section", None, None),
    )
    return jax.shard_map(
        functools.partial(body, mesh.shape["group"]),
        mesh=mesh,
        in_specs=placed,
        out_specs=(
            P("section", ("dp", "group"), None),
            P("section", ("dp", "group"), None),
            P("section", "dp"),
            P("section", "dp", None),
            P("section", "dp", None),
            P("section", "dp"),
            P("section", "dp", None),
            P("section", "dp", None),
        ),
        check_vma=False,
    )
```

```python
import functools

import jax
import jax.numpy as jnp
import numpy as np
from jax import lax
from jax.experimental import pallas as pl
from jax.experimental.pallas import tpu as pltpu
from jax.sharding import PartitionSpec as P

D = 1024
HEADS = 8
HEAD_DIM = 128
FF = 2816
SEG = 256
TOPM = 128
MICRO = 2
EPS = 1e-05
NEG = -1e30
MESH = pl.DeviceIdType.MESH
BLOCK = 256
LAG = 2


def flip(value, mask):
    return value + mask * (1 - 2 * ((value // mask) % 2))


def summed(left, right):
    return (left.astype(jnp.float32) + right.astype(jnp.float32)).astype(jnp.bfloat16)


def reduce_kernel(extra, *refs):
    n_extra = len(extra)
    (nf_t, na_t, o_t, z_t, dgu, dm, f_cols, e_cols, gains) = refs[:9]
    (out_sq, out_d, out_gains) = refs[9:12]
    refs = refs[12:]
    (a_own, a_in, z_own, z_in, b_own, b_in, e_own, e_in) = refs[:8]
    (g_sq, q0, q1, q2, g_d, d0, d1, d2, gain_out, gain_in) = refs[8:18]
    refs = refs[18:]
    x_sq, x_d = refs[:2]
    (sem_load, sem_bload, sem_asend, sem_arecv, sem_bsend, sem_brecv) = refs[2:8]
    (sem_send, sem_recv, sem_copy, gain_send, gain_recv) = refs[8:13]

    section, dpi, group = (lax.axis_index(name) for name in ("section", "dp", "group"))
    mask1 = 1 + section
    mask2 = 2 - section
    half = (group // mask1) % 2
    low2 = (group // mask2) % 2
    bit0 = dpi % 2
    bit1 = (dpi // 2) % 2
    first = (section, dpi, flip(group, mask1))
    second = (section, dpi, flip(group, mask2))
    near = (section, flip(dpi, 1), group)
    far = (section, flip(dpi, 2), group)
    others = [(section, dpi, flip(group, mask)) for mask in extra]
    partners = [first, second, near, far] + others

    barrier = pltpu.get_barrier_semaphore()
    for partner in partners:
        pl.semaphore_signal(barrier, inc=1, device_id=partner, device_id_type=MESH)
    pl.semaphore_wait(barrier, len(partners))

    def remote(src, dst, send, recv, device):
        return pltpu.make_async_remote_copy(
            src_ref=src, dst_ref=dst, send_sem=send, recv_sem=recv, device_id=device, device_id_type=MESH
        )

    def load_a(slot):
        src = (nf_t, o_t, na_t)[slot]
        return pltpu.make_async_copy(src, a_own.at[slot], sem_load.at[slot])

    def load_z():
        return pltpu.make_async_copy(z_t.at[pl.ds(0, 4), half], z_own, sem_load.at[3])

    def b_src(index, part):
        if index[0] == 0:
            return dgu.at[part * 11 + index[1]]
        if index[0] == 1:
            return f_cols.at[part * 2 + index[1]]
        return dm.at[part * 6 + index[1]]

    def load_b(kind, i, slot):
        return pltpu.make_async_copy(b_src((kind, i), half), b_own.at[slot], sem_bload.at[slot])

    def load_e(k):
        return pltpu.make_async_copy(e_cols.at[k], e_own.at[k], sem_bload.at[19 + k])

    def send_a(slot):
        src = (nf_t, o_t, na_t)[slot]
        return remote(src, a_in.at[slot], sem_asend.at[slot], sem_arecv.at[slot], first)

    def send_z():
        return remote(z_t.at[pl.ds(0, 4), 1 - half], z_in, sem_asend.at[3], sem_arecv.at[3], first)

    def send_b(kind, i, slot):
        return remote(b_src((kind, i), 1 - half), b_in.at[slot], sem_bsend.at[slot], sem_brecv.at[slot], first)

    def send_e(k):
        return remote(e_cols.at[k], e_in.at[k], sem_bsend.at[19 + k], sem_brecv.at[19 + k], first)

    kinds = ((0, 0, 11), (1, 11, 2), (2, 13, 6))
    load_z().start()
    send_z().start()

    @pl.loop(0, 4)
    def _(k):
        load_e(k).start()
        send_e(k).start()

    for kind, base, count in kinds:
        load_a(kind).start()
        send_a(kind).start()

        @pl.loop(0, count)
        def _(i):
            load_b(kind, i, base + i).start()
            send_b(kind, i, base + i).start()

    class Square:
        base, rows = 4, 256
        partial, recv0, recv1, recv2, xs, out = g_sq, q0, q1, q2, x_sq, out_sq

    class Down:
        base, rows = 0, 352
        partial, recv0, recv1, recv2, xs, out = g_d, d0, d1, d2, x_d, out_d

    def to_near(cls, c):
        k = cls.base + c
        return remote(cls.partial.at[c, pl.ds(0, 2), 1 - bit0], cls.recv0.at[c], sem_send.at[0, k], sem_recv.at[0, k], near)

    def to_far(cls, c):
        k = cls.base + c
        return remote(cls.recv0.at[c, 1 - bit1], cls.recv1.at[c], sem_send.at[1, k], sem_recv.at[1, k], far)

    def rows_at(cls, part):
        size = cls.rows // 2
        return pl.ds(pl.multiple_of(part * size, 16), size)

    def to_second(cls, c):
        k = cls.base + c
        return remote(cls.recv1.at[c, rows_at(cls, 1 - low2)], cls.recv2.at[c], sem_send.at[2, k], sem_recv.at[2, k], second)

    def to_extra(cls, c, i):
        k = cls.base + c
        src = cls.recv2.at[c] if i == 0 else cls.xs.at[i - 1, c]
        return remote(src, cls.xs.at[i, c], sem_send.at[6 + i, k], sem_recv.at[6 + i, k], others[i])

    def final(cls, c):
        return cls.recv2.at[c] if n_extra == 0 else cls.xs.at[n_extra - 1, c]

    def share_second(cls, c):
        k = cls.base + c
        return remote(final(cls, c), cls.out.at[half, c, rows_at(cls, low2)], sem_send.at[3, k], sem_recv.at[3, k], second)

    def share_first(cls, c):
        k = cls.base + c
        return remote(final(cls, c), cls.out.at[half, c, rows_at(cls, low2)], sem_send.at[4, k], sem_recv.at[4, k], first)

    def pass_on(cls, c):
        k = cls.base + c
        block = cls.out.at[half, c, rows_at(cls, 1 - low2)]
        return remote(block, block, sem_send.at[5, k], sem_recv.at[5, k], first)

    def keep(cls, c):
        return pltpu.make_async_copy(final(cls, c), cls.out.at[half, c, rows_at(cls, low2)], sem_copy.at[cls.base + c])

    def multiply(left, right, left2, right2):
        total = jnp.dot(left, right, preferred_element_type=jnp.float32)
        total += jnp.dot(left2, right2, preferred_element_type=jnp.float32)
        return total.astype(jnp.bfloat16)

    def partial_square(c):
        for kind, base, count in kinds:

            @pl.when(c == base)
            def _():
                load_a(kind).wait()
                send_a(kind).wait_recv()

        load_b(0, 0, c).wait()
        send_b(0, 0, c).wait_recv()
        for kind, base, count in kinds:

            @pl.when((c >= base) & (c < base + count))
            def _():
                for j in range(4):
                    rows = pl.ds(j * 256, 256)
                    g_sq[c, j // 2, j % 2] = multiply(
                        a_own[kind, rows, :], b_own[c], a_in[kind, rows, :], b_in[c]
                    )

        to_near(Square, c).start()

    def partial_down(c):
        @pl.when(c == 0)
        def _():
            load_z().wait()
            send_z().wait_recv()

        load_e(c).wait()
        send_e(c).wait_recv()
        for j in range(4):
            g_d[c, j // 2, j % 2] = multiply(z_own[j], e_own[c], z_in[j], e_in[c])
        to_near(Down, c).start()

    def stage_near(cls, c):
        to_near(cls, c).wait_recv()
        for i in range(2):
            cls.recv0[c, i] = summed(cls.partial[c, i, bit0], cls.recv0[c, i])
        to_far(cls, c).start()

    def stage_far(cls, c):
        to_far(cls, c).wait_recv()
        cls.recv1[c] = summed(cls.recv0[c, bit1], cls.recv1[c])
        to_second(cls, c).start()

    def share(cls, c):
        share_second(cls, c).start()
        share_first(cls, c).start()
        keep(cls, c).start()

    def stage_second(cls, c):
        to_second(cls, c).wait_recv()
        cls.recv2[c] = summed(cls.recv1[c, rows_at(cls, low2)], cls.recv2[c])
        if n_extra:
            to_extra(cls, c, 0).start()
        else:
            share(cls, c)

    def stage_extra(cls, c, i):
        to_extra(cls, c, i).wait()
        mine = cls.recv2[c] if i == 0 else cls.xs[i - 1, c]
        cls.xs[i, c] = summed(mine, cls.xs[i, c])
        if i + 1 < n_extra:
            to_extra(cls, c, i + 1).start()
        else:
            share(cls, c)

    def stage_pass(cls, c):
        share_second(cls, c).wait_recv()
        pass_on(cls, c).start()

    def partial(cls, c):
        (partial_square if cls is Square else partial_down)(c)

    stages = [partial, stage_near, stage_far, stage_second]
    stages += [functools.partial(lambda i, cls, c: stage_extra(cls, c, i), i) for i in range(n_extra)]
    stages += [stage_pass]

    def gain_exchange(i):
        return remote(gain_out.at[i], gain_in.at[i], gain_send.at[i], gain_recv.at[i], partners[i])

    steps = 23 + LAG * (len(stages) - 1)

    @pl.loop(0, steps)
    def _(t):
        for i, stage in enumerate(stages):
            c = t - LAG * i

            @pl.when((c >= 0) & (c < 4))
            def _():
                stage(Down, c)

            @pl.when((c >= 4) & (c < 23))
            def _():
                stage(Square, c - 4)

        for i in range(len(partners)):

            @pl.when(t == 3 * i + 2)
            def _():
                if i == 0:
                    gain_out[0] = gains[...]
                else:
                    gain_exchange(i - 1).wait()
                    gain_out[i] = gain_out[i - 1] + gain_in[i - 1]
                gain_exchange(i).start()

    last = len(partners) - 1
    gain_exchange(last).wait()
    out_gains[...] = gain_out[last] + gain_in[last]

    send_z().wait_send()
    for kind, base, count in kinds:
        send_a(kind).wait_send()

    def finish(cls, c):
        to_near(cls, c).wait_send()
        to_far(cls, c).wait_send()
        to_second(cls, c).wait_send()
        share_second(cls, c).wait_send()
        share_first(cls, c).wait()
        pass_on(cls, c).wait()
        keep(cls, c).wait()

    @pl.loop(0, 4)
    def _(c):
        send_e(c).wait_send()
        finish(Down, c)

    @pl.loop(0, 19)
    def _(c):
        send_b(0, 0, c).wait_send()
        finish(Square, c)


def reduce_gradients(group_size, nf_t, na_t, o_t, z_t, dgu, dm, f_cols, e_cols, gains):
    extra = []
    mask = 4
    while mask < group_size:
        extra.append(mask)
        mask *= 2
    n_extra = len(extra)
    low = jnp.bfloat16
    tokens = nf_t.shape[1]
    scratch = [
        pltpu.VMEM((3, D, tokens), low),
        pltpu.VMEM((3, D, tokens), low),
        pltpu.VMEM((4, 352, tokens), low),
        pltpu.VMEM((4, 352, tokens), low),
        pltpu.VMEM((19, tokens, BLOCK), low),
        pltpu.VMEM((19, tokens, BLOCK), low),
        pltpu.VMEM((4, tokens, BLOCK), low),
        pltpu.VMEM((4, tokens, BLOCK), low),
        pltpu.VMEM((19, 2, 2, 256, BLOCK), low),
        pltpu.VMEM((19, 2, 256, BLOCK), low),
        pltpu.VMEM((19, 256, BLOCK), low),
        pltpu.VMEM((19, 128, BLOCK), low),
        pltpu.VMEM((4, 2, 2, 352, BLOCK), low),
        pltpu.VMEM((4, 2, 352, BLOCK), low),
        pltpu.VMEM((4, 352, BLOCK), low),
        pltpu.VMEM((4, 176, BLOCK), low),
        pltpu.VMEM((4 + n_extra, 8, D), jnp.float32),
        pltpu.VMEM((4 + n_extra, 8, D), jnp.float32),
        pltpu.VMEM((max(n_extra, 1), 19 if n_extra else 1, 128, BLOCK), low),
        pltpu.VMEM((max(n_extra, 1), 4 if n_extra else 1, 176, BLOCK), low),
        pltpu.SemaphoreType.DMA((4,)),
        pltpu.SemaphoreType.DMA((23,)),
        pltpu.SemaphoreType.DMA((4,)),
        pltpu.SemaphoreType.DMA((4,)),
        pltpu.SemaphoreType.DMA((23,)),
        pltpu.SemaphoreType.DMA((23,)),
        pltpu.SemaphoreType.DMA((6 + n_extra, 23)),
        pltpu.SemaphoreType.DMA((6 + n_extra, 23)),
        pltpu.SemaphoreType.DMA((23,)),
        pltpu.SemaphoreType.DMA((4 + n_extra,)),
        pltpu.SemaphoreType.DMA((4 + n_extra,)),
    ]
    anywhere = pl.BlockSpec(memory_space=pl.ANY)
    near_by = pl.BlockSpec(memory_space=pltpu.VMEM)
    return pl.pallas_call(
        functools.partial(reduce_kernel, tuple(extra)),
        out_shape=(
            jax.ShapeDtypeStruct((2, 19, 256, BLOCK), low),
            jax.ShapeDtypeStruct((2, 4, 352, BLOCK), low),
            jax.ShapeDtypeStruct((8, D), jnp.float32),
        ),
        in_specs=[anywhere] * 8 + [near_by],
        out_specs=(anywhere, anywhere, near_by),
        scratch_shapes=scratch,
        compiler_params=pltpu.CompilerParams(
            collective_id=0, has_side_effects=True, vmem_limit_bytes=58 * 2**20
        ),
        cost_estimate=pl.CostEstimate(flops=13 * 10**9, bytes_accessed=30 * 10**6, transcendentals=0),
        name="reduce_gradients",
    )(nf_t, na_t, o_t, z_t, dgu, dm, f_cols, e_cols, gains)


def to_f32(value):
    return value.astype(jnp.float32)


def to_low(value):
    return value.astype(jnp.bfloat16)


def by_rows(left, right):
    return lax.dot_general(left, right, (((1,), (1,)), ((), ())), preferred_element_type=jnp.float32)


def by_tokens(left, right):
    return lax.dot_general(left, right, (((0,), (0,)), ((), ())), preferred_element_type=jnp.float32)


def times(left, right):
    return jnp.dot(left, right, preferred_element_type=jnp.float32)


def cols(index, size=BLOCK, base=0):
    return pl.ds(pl.multiple_of(base + index * size, 128), size)


def inverse_rms(values):
    return lax.rsqrt(jnp.mean(values * values, axis=-1, keepdims=True) + EPS)


def layer_kernel(*refs):
    (tokens, cotangent, mem_k, mem_v, index, bias, cosine, sine, gain_a, gain_f) = refs[:10]
    (w_qkv_hbm, w_o_hbm, w_gu_hbm, w_d_hbm) = refs[10:14]
    (act, igrad, na_t, nf_t, o_t, z_t, dgu, dm, f_cols, e_cols, gains) = refs[14:25]
    refs = refs[25:]
    (w_qkv, w_o, w_gu, w_d, xs, qkv, probs, resid, factors, grads, picked_k, picked_v) = refs[:12]
    (raw, normed, attended, hidden, turned, hidden_t, y_low, wide, dh, f_low, d_att, gx) = refs[12:24]
    (sem_w, sem_in, sem_mem, sem_t, sem_out, sem_send, sem_recv) = refs[24:31]

    section, dpi, group = (lax.axis_index(name) for name in ("section", "dp", "group"))
    twin = (1 - section, dpi, group)
    is_lower = section == 0
    is_upper = section == 1
    scale = HEAD_DIM ** (-0.5)

    weights = []
    for i, (src, dst, pieces) in enumerate(
        ((w_qkv_hbm, w_qkv, 4), (w_o_hbm, w_o, 1), (w_gu_hbm, w_gu, 4), (w_d_hbm, w_d, 2))
    ):
        size = src.shape[0] // pieces
        weights.append(
            [
                pltpu.make_async_copy(src.at[pl.ds(p * size, size)], dst.at[pl.ds(p * size, size)], sem_w.at[i, p])
                for p in range(pieces)
            ]
        )

    def rows(m):
        return pl.ds(m * SEG, SEG)

    def load_tokens(m):
        return pltpu.make_async_copy(tokens.at[rows(m)], xs.at[m], sem_in.at[0, m])

    def load_cotangent(m):
        return pltpu.make_async_copy(cotangent.at[rows(m)], grads.at[m], sem_in.at[1, m])

    def send_up(m):
        return pltpu.make_async_remote_copy(
            src_ref=y_low.at[m], dst_ref=xs.at[m], send_sem=sem_send.at[0, m], recv_sem=sem_recv.at[0, m],
            device_id=twin, device_id_type=MESH,
        )

    def send_down(m):
        return pltpu.make_async_remote_copy(
            src_ref=gx.at[m], dst_ref=grads.at[m], send_sem=sem_send.at[1, m], recv_sem=sem_recv.at[1, m],
            device_id=twin, device_id_type=MESH,
        )

    @pl.when(is_lower)
    def _():
        load_tokens(0).start()

    for copy in weights[0]:
        copy.start()

    @pl.when(is_lower)
    def _():
        load_tokens(1).start()

    memory_in = [
        pltpu.make_async_copy(src, raw.at[i], sem_mem.at[i]) for i, src in enumerate((mem_k, mem_v))
    ]

    @pl.when(is_upper)
    def _():
        for copy in memory_in:
            copy.start()
        for m in range(MICRO):
            load_cotangent(m).start()

    for group_copies in weights[1:]:
        for copy in group_copies:
            copy.start()

    barrier = pltpu.get_barrier_semaphore()
    pl.semaphore_signal(barrier, inc=1, device_id=twin, device_id_type=MESH)
    pl.semaphore_wait(barrier, 1)

    @pl.when(is_lower)
    def _():
        picked_k[...] = jnp.zeros_like(picked_k)
        picked_v[...] = jnp.zeros_like(picked_v)

    @pl.when(is_upper)
    def _():
        for copy in memory_in:
            copy.wait()
        places = lax.broadcasted_iota(jnp.int32, (TOPM, SEG), 1)
        for m in range(MICRO):
            chosen = to_low(to_f32(index[m] == places))
            for n in range(4):
                picked_k[m, :, cols(n)] = to_low(times(chosen, raw[0, m, :, cols(n)]))
                picked_v[m, :, cols(n)] = to_low(times(chosen, raw[1, m, :, cols(n)]))

    eye = to_low(
        to_f32(
            lax.broadcasted_iota(jnp.int32, (BLOCK, BLOCK), 0) == lax.broadcasted_iota(jnp.int32, (BLOCK, BLOCK), 1)
        )
    )
    turned_copies = {}

    def turn(src, width, dst, slot, out, sem, m):
        if m:
            turned_copies[sem].wait()

        def step(j, _):
            dst[slot + (pl.ds(pl.multiple_of(j * BLOCK, BLOCK), BLOCK), slice(None))] = to_low(
                by_rows(eye, src[:, cols(j)])
            )
            return 0

        lax.fori_loop(0, width // BLOCK, step, 0, unroll=True)
        view = dst.at[slot[0]] if slot else dst
        turned_copies[sem] = pltpu.make_async_copy(view, out.at[:, cols(m)], sem_t.at[sem])
        turned_copies[sem].start()

    def forward(m):
        @pl.when(is_lower)
        def _():
            load_tokens(m).wait()

        @pl.when(is_upper)
        def _():
            send_up(m).wait_recv()

        x = to_f32(xs[m])
        normed[...] = to_low(x * inverse_rms(x) * gain_a[...])
        if m == 0:
            for copy in weights[0]:
                copy.wait()

        def rotated(j, _):
            block = times(normed[...], w_qkv[:, cols(j)])
            for p in range(2):
                part = block[:, p * HEAD_DIM : (p + 1) * HEAD_DIM]
                part = part * cosine[...] + pltpu.roll(part, HEAD_DIM // 2, 1) * sine[...]
                qkv[m, :, cols(2 * j + p, HEAD_DIM)] = to_low(part)
            return 0

        lax.fori_loop(0, 8, rotated, 0, unroll=4)

        def plain(j, _):
            qkv[m, :, cols(j, BLOCK, 2 * D)] = to_low(times(normed[...], w_qkv[:, cols(j, BLOCK, 2 * D)]))
            return 0

        lax.fori_loop(0, 4, plain, 0, unroll=True)
        turn(normed, D, turned, (0,), na_t, 0, m)
        causal = lax.broadcasted_iota(jnp.int32, (SEG, SEG), 0) >= lax.broadcasted_iota(jnp.int32, (SEG, SEG), 1)

        def head(h, _):
            query = qkv[m, :, cols(h, HEAD_DIM)]
            local = by_rows(query, qkv[m, :, cols(h, HEAD_DIM, D)]) * scale
            local = jnp.where(causal, local, NEG)
            remote = by_rows(query, picked_k[m, :, cols(h, HEAD_DIM)]) * scale + bias[m]
            peak = jnp.maximum(
                jnp.max(local, axis=-1, keepdims=True), jnp.max(remote, axis=-1, keepdims=True)
            )
            local = jnp.exp(local - peak)
            remote = jnp.exp(remote - peak)
            share = 1.0 / (jnp.sum(local, axis=-1, keepdims=True) + jnp.sum(remote, axis=-1, keepdims=True))
            local = to_low(local * share)
            remote = to_low(remote * share)
            probs[m, h, :, :SEG] = local
            probs[m, h, :, SEG:] = remote
            result = times(local, qkv[m, :, cols(h, HEAD_DIM, 2 * D)])
            result += times(remote, picked_v[m, :, cols(h, HEAD_DIM)])
            attended[:, cols(h, HEAD_DIM)] = to_low(result)
            return 0

        lax.fori_loop(0, HEADS, head, 0, unroll=4)
        if m == 0:
            weights[1][0].wait()

        def project(n, _):
            resid[m, :, cols(n)] = to_f32(xs[m, :, cols(n)]) + times(attended[...], w_o[:, cols(n)])
            return 0

        lax.fori_loop(0, 4, project, 0, unroll=True)
        turn(attended, D, turned, (1,), o_t, 1, m)
        h = resid[m]
        normed[...] = to_low(h * inverse_rms(h) * gain_f[...])
        if m == 0:
            for copy in weights[2]:
                copy.wait()

        def gate(j, _):
            a = times(normed[...], w_gu[:, cols(j)])
            u = times(normed[...], w_gu[:, cols(j, BLOCK, FF)])
            sg = jax.nn.sigmoid(a)
            silu = a * sg
            hidden[:, cols(j)] = to_low(silu * u)
            factors[m, :, cols(j)] = to_low(u * sg * (1.0 + a * (1.0 - sg)))
            factors[m, :, cols(j, BLOCK, FF)] = to_low(silu)
            return 0

        lax.fori_loop(0, FF // BLOCK, gate, 0, unroll=4)
        if m == 0:
            for copy in weights[3]:
                copy.wait()

        def down(n, _):
            y_low[m, :, cols(n)] = to_low(resid[m, :, cols(n)] + times(hidden[...], w_d[:, cols(n)]))
            return 0

        lax.fori_loop(0, 4, down, 0, unroll=2)

        @pl.when(is_lower)
        def _():
            send_up(m).start()

        write_out(y_low.at[m], act.at[rows(m)], 0, m).start()
        turn(normed, D, turned, (2,), nf_t, 2, m)
        turn(hidden, FF, hidden_t, (), z_t, 3, m)

    def write_out(src, dst, kind, m):
        return pltpu.make_async_copy(src, dst, sem_out.at[kind, m])

    def block_out(src, dst, kind, m, i):
        return write_out(src.at[m, :, cols(i)], dst.at[i, rows(m)], kind, m)

    block_sets = ((grads, e_cols, 2, 4), (factors, dgu, 3, 22), (f_low, f_cols, 4, 4), (qkv, dm, 5, 12))

    def start_blocks(which, m):
        src, dst, kind, count = block_sets[which]
        for i in range(count):
            block_out(src, dst, kind, m, i).start()

    def wait_blocks(which, m):
        src, dst, kind, count = block_sets[which]
        whole = dst.at[:, rows(m)]
        pltpu.make_async_copy(whole, whole, sem_out.at[kind, m]).wait()

    def norm_back(d_normed, values, gain, incoming):
        inverse = inverse_rms(values)
        scaled = d_normed * gain
        column = jnp.sum(d_normed * (values * inverse), axis=0, keepdims=True)
        centre = jnp.mean(scaled * values, axis=-1, keepdims=True)
        return incoming + inverse * scaled - values * (inverse * inverse * inverse * centre), column

    def backward(m):
        @pl.when(is_upper)
        def _():
            load_cotangent(m).wait()

        @pl.when(is_lower)
        def _():
            send_down(m).wait_recv()

        start_blocks(0, m)

        def gate_back(j, _):
            dz = by_rows(grads[m], w_d[pl.ds(pl.multiple_of(j * BLOCK, BLOCK), BLOCK), :])
            factors[m, :, cols(j)] = to_low(dz * to_f32(factors[m, :, cols(j)]))
            factors[m, :, cols(j, BLOCK, FF)] = to_low(dz * to_f32(factors[m, :, cols(j, BLOCK, FF)]))
            return 0

        lax.fori_loop(0, FF // BLOCK, gate_back, 0, unroll=4)
        start_blocks(1, m)

        def gate_up_back(n, _):
            wide[:, cols(n)] = by_rows(factors[m], w_gu[pl.ds(pl.multiple_of(n * BLOCK, BLOCK), BLOCK), :])
            return 0

        lax.fori_loop(0, 4, gate_up_back, 0)
        result, column = norm_back(wide[...], resid[m], gain_f[...], to_f32(grads[m]))
        dh[...] = result
        f_low[m] = to_low(result)
        gains[1:2, :] = column if m == 0 else gains[1:2, :] + column
        start_blocks(2, m)

        def out_back(n, _):
            d_att[:, cols(n)] = to_low(by_rows(f_low[m], w_o[pl.ds(pl.multiple_of(n * BLOCK, BLOCK), BLOCK), :]))
            return 0

        lax.fori_loop(0, 4, out_back, 0, unroll=True)

        def rotate_back(part):
            return part * cosine[...] - pltpu.roll(part, HEAD_DIM // 2, 1) * sine[...]

        def head_back(h, _):
            at_q, at_k, at_v = (cols(h, HEAD_DIM, base) for base in (0, D, 2 * D))
            query, key, value = qkv[m, :, at_q], qkv[m, :, at_k], qkv[m, :, at_v]
            d_out = d_att[:, cols(h, HEAD_DIM)]
            p_local = probs[m, h, :, :SEG]
            p_remote = probs[m, h, :, SEG:]
            d_local = by_rows(d_out, value)
            d_remote = by_rows(d_out, picked_v[m, :, cols(h, HEAD_DIM)])
            wide_local, wide_remote = to_f32(p_local), to_f32(p_remote)
            centre = jnp.sum(wide_local * d_local, axis=-1, keepdims=True) + jnp.sum(
                wide_remote * d_remote, axis=-1, keepdims=True
            )
            d_local = to_low(wide_local * (d_local - centre))
            d_remote = to_low(wide_remote * (d_remote - centre))
            d_query = (times(d_local, key) + times(d_remote, picked_k[m, :, cols(h, HEAD_DIM)])) * scale
            d_key = by_tokens(d_local, query) * scale
            qkv[m, :, at_v] = to_low(by_tokens(p_local, d_out))
            qkv[m, :, at_q] = to_low(rotate_back(d_query))
            qkv[m, :, at_k] = to_low(rotate_back(d_key))
            return 0

        lax.fori_loop(0, HEADS, head_back, 0, unroll=2)
        start_blocks(3, m)

        def qkv_back(n, _):
            wide[:, cols(n)] = by_rows(qkv[m], w_qkv[pl.ds(pl.multiple_of(n * BLOCK, BLOCK), BLOCK), :])
            return 0

        lax.fori_loop(0, 4, qkv_back, 0)
        result, column = norm_back(wide[...], to_f32(xs[m]), gain_a[...], dh[...])
        gx[m] = to_low(result)
        gains[0:1, :] = column if m == 0 else gains[0:1, :] + column

        @pl.when(is_upper)
        def _():
            send_down(m).start()

        write_out(gx.at[m], igrad.at[rows(m)], 1, m).start()

    gains[...] = jnp.zeros_like(gains)
    for m in range(MICRO):
        forward(m)
    for m in range(MICRO):
        backward(m)

    for m in range(MICRO):
        write_out(y_low.at[m], act.at[rows(m)], 0, m).wait()
        write_out(gx.at[m], igrad.at[rows(m)], 1, m).wait()
        for which in range(4):
            wait_blocks(which, m)
    for copy in turned_copies.values():
        copy.wait()

    @pl.when(is_lower)
    def _():
        for m in range(MICRO):
            send_up(m).wait_send()

    @pl.when(is_upper)
    def _():
        for m in range(MICRO):
            send_down(m).wait_send()


def rotary_constants():
    half = HEAD_DIM // 2
    freqs = np.exp(-np.log(10000.0) * np.arange(half) * 2.0 / HEAD_DIM)
    angles = np.arange(SEG)[:, None] * freqs[None, :]
    cosine = np.concatenate([np.cos(angles), np.cos(angles)], axis=1)
    sine = np.concatenate([-np.sin(angles), np.sin(angles)], axis=1)
    return cosine.astype(np.float32), sine.astype(np.float32)


def run_layers(tokens, cotangent, mem_keys, mem_values, index, bias, gain_a, gain_f, w_qkv, w_o, w_gu, w_d):
    cosine, sine = rotary_constants()
    count = tokens.shape[0]
    low, wide = jnp.bfloat16, jnp.float32
    anywhere = pl.BlockSpec(memory_space=pl.ANY)
    near_by = pl.BlockSpec(memory_space=pltpu.VMEM)
    shape = jax.ShapeDtypeStruct
    outs = (
        shape((count, D), low),
        shape((count, D), low),
        shape((D, count), low),
        shape((D, count), low),
        shape((D, count), low),
        shape((FF, count), low),
        shape((22, count, BLOCK), low),
        shape((12, count, BLOCK), low),
        shape((4, count, BLOCK), low),
        shape((4, count, BLOCK), low),
        shape((8, D), wide),
    )
    scratch = [
        pltpu.VMEM((D, 3 * D), low),
        pltpu.VMEM((D, D), low),
        pltpu.VMEM((D, 2 * FF), low),
        pltpu.VMEM((FF, D), low),
        pltpu.VMEM((MICRO, SEG, D), low),
        pltpu.VMEM((MICRO, SEG, 3 * D), low),
        pltpu.VMEM((MICRO, HEADS, SEG, SEG + TOPM), low),
        pltpu.VMEM((MICRO, SEG, D), wide),
        pltpu.VMEM((MICRO, SEG, 2 * FF), low),
        pltpu.VMEM((MICRO, SEG, D), low),
        pltpu.VMEM((MICRO, TOPM, D), low),
        pltpu.VMEM((MICRO, TOPM, D), low),
        pltpu.VMEM((2, MICRO, SEG, D), low),
        pltpu.VMEM((SEG, D), low),
        pltpu.VMEM((SEG, D), low),
        pltpu.VMEM((SEG, FF), low),
        pltpu.VMEM((3, D, SEG), low),
        pltpu.VMEM((FF, SEG), low),
        pltpu.VMEM((MICRO, SEG, D), low),
        pltpu.VMEM((SEG, D), wide),
        pltpu.VMEM((SEG, D), wide),
        pltpu.VMEM((MICRO, SEG, D), low),
        pltpu.VMEM((SEG, D), low),
        pltpu.VMEM((MICRO, SEG, D), low),
        pltpu.SemaphoreType.DMA((4, 4)),
        pltpu.SemaphoreType.DMA((2, MICRO)),
        pltpu.SemaphoreType.DMA((2,)),
        pltpu.SemaphoreType.DMA((4,)),
        pltpu.SemaphoreType.DMA((6, MICRO)),
        pltpu.SemaphoreType.DMA((2, MICRO)),
        pltpu.SemaphoreType.DMA((2, MICRO)),
    ]
    return pl.pallas_call(
        layer_kernel,
        out_shape=outs,
        in_specs=[anywhere] * 4 + [near_by] * 6 + [anywhere] * 4,
        out_specs=(anywhere,) * 10 + (near_by,),
        scratch_shapes=scratch,
        compiler_params=pltpu.CompilerParams(
            collective_id=1, has_side_effects=True, vmem_limit_bytes=60 * 2**20
        ),
        cost_estimate=pl.CostEstimate(flops=27 * 10**9, bytes_accessed=50 * 10**6, transcendentals=0),
        name="relay_layers",
    )(tokens, cotangent, mem_keys, mem_values, index, bias, cosine, sine, gain_a, gain_f, w_qkv, w_o, w_gu, w_d)


def finish_kernel(sq, down, gu_out, o_out, qkv_out, d_out, sq_v, d_v, gu_v, o_v, qkv_v, down_v, sem_in, sem_out):
    parts = (
        (gu_v, gu_out, 0, 11),
        (qkv_v, qkv_out, 13, 6),
        (o_v, o_out, 11, 2),
    )
    loads = [
        pltpu.make_async_copy(
            sq.at[:, pl.ds(base, count)], sq_v.at[:, pl.ds(base, count)], sem_in.at[i]
        )
        for i, (_, _, base, count) in enumerate(parts)
    ]
    load_d = pltpu.make_async_copy(down, d_v, sem_in.at[3])
    for copy in loads:
        copy.start()
    load_d.start()
    stores = []
    for i, (view, out, base, count) in enumerate(parts):
        loads[i].wait()
        for half in range(2):
            for c in range(count):
                at = pl.ds((half * count + c) * BLOCK, BLOCK)
                view[:, at] = sq_v[half, base + c].astype(jnp.float32)
            span = pl.ds(half * count * BLOCK, count * BLOCK)
            stores.append(pltpu.make_async_copy(view.at[:, span], out.at[:, span], sem_out.at[2 * i + half]))
            stores[-1].start()
    load_d.wait()
    for half in range(2):
        for k in range(4):
            down_v[pl.ds(half * 352, 352), pl.ds(k * BLOCK, BLOCK)] = d_v[half, k].astype(jnp.float32)
        span = pl.ds(half * 352, 352)
        stores.append(pltpu.make_async_copy(down_v.at[span], d_out.at[span], sem_out.at[6 + half]))
        stores[-1].start()
    for copy in stores:
        copy.wait()


def finish_gradients(out_sq, out_d):
    anywhere = pl.BlockSpec(memory_space=pl.ANY)
    shapes = ((256, 2 * FF), (256, D), (256, 3 * D), (704, D))
    return pl.pallas_call(
        finish_kernel,
        out_shape=tuple(jax.ShapeDtypeStruct(shape, jnp.float32) for shape in shapes),
        in_specs=[anywhere] * 2,
        out_specs=(anywhere,) * 4,
        scratch_shapes=[pltpu.VMEM(out_sq.shape, jnp.bfloat16), pltpu.VMEM(out_d.shape, jnp.bfloat16)]
        + [pltpu.VMEM(shape, jnp.float32) for shape in shapes]
        + [pltpu.SemaphoreType.DMA((4,)), pltpu.SemaphoreType.DMA((8,))],
        compiler_params=pltpu.CompilerParams(vmem_limit_bytes=40 * 2**20),
        name="finish_gradients",
    )(out_sq, out_d)


def body(
    group_size,
    tokens,
    cotangent,
    mem_keys,
    mem_values,
    mem_index,
    mem_flags,
    norm_attn,
    w_qkv,
    w_out,
    norm_ffn,
    w_gate_up,
    w_down,
):
    live = mem_flags * (lax.axis_index("section") == 1).astype(jnp.int32)
    bias = jnp.broadcast_to(jnp.where(live > 0, 0.0, NEG)[:, None, None], (MICRO, 1, TOPM))
    (act, igrad, na_t, nf_t, o_t, z_t, dgu, dm, f_cols, e_cols, gains) = run_layers(
        tokens,
        cotangent,
        mem_keys,
        mem_values,
        mem_index[:, :, None],
        bias.astype(jnp.float32),
        norm_attn.astype(jnp.float32),
        norm_ffn.astype(jnp.float32),
        w_qkv[0],
        w_out[0],
        w_gate_up[0],
        w_down[0],
    )
    out_sq, out_d, out_gains = reduce_gradients(
        group_size, nf_t, na_t, o_t, z_t.reshape(4, 2, 352, -1), dgu, dm, f_cols, e_cols, gains
    )
    grad_gu, grad_o, grad_qkv, grad_d = finish_gradients(out_sq, out_d)
    start = lax.axis_index("dp") * BLOCK
    gain_rows = lax.dynamic_slice(out_gains, (0, start), (2, BLOCK))
    return (
        act[None],
        igrad[None],
        gain_rows[0:1],
        grad_qkv[None],
        grad_o[None],
        gain_rows[1:2],
        grad_gu[None],
        grad_d[None],
    )


def solution(mesh):
    placed = (
        P(("dp", "group"), None),
        P(("dp", "group"), None),
        P(("dp", "group"), None, None),
        P(("dp", "group"), None, None),
        P(("dp", "group"), None),
        P(("dp", "group")),
        P("section", None),
        P("section", None, None),
        P("section", None, None),
        P("section", None),
        P("section", None, None),
        P("section", None, None),
    )
    return jax.shard_map(
        functools.partial(body, mesh.shape["group"]),
        mesh=mesh,
        in_specs=placed,
        out_specs=(
            P("section", ("dp", "group"), None),
            P("section", ("dp", "group"), None),
            P("section", "dp"),
            P("section", "dp", None),
            P("section", "dp", None),
            P("section", "dp"),
            P("section", "dp", None),
            P("section", "dp", None),
        ),
        check_vma=False,
    )
```

```python
import functools

import jax
import jax.numpy as jnp
import numpy as np
from jax import lax
from jax.experimental import pallas as pl
from jax.experimental.pallas import tpu as pltpu
from jax.sharding import PartitionSpec as P

D = 1024
HEADS = 8
HEAD_DIM = 128
FF = 2816
SEG = 256
TOPM = 128
MICRO = 2
EPS = 1e-05
NEG = -1e30
MESH = pl.DeviceIdType.MESH
BLOCK = 256
LAG = 2


def flip(value, mask):
    return value + mask * (1 - 2 * ((value // mask) % 2))


def summed(left, right):
    return (left.astype(jnp.float32) + right.astype(jnp.float32)).astype(jnp.bfloat16)


def reduce_kernel(extra, *refs):
    n_extra = len(extra)
    (nf_t, na_t, o_t, z_t, dgu, dm, f_cols, e_cols, nf_p, na_p, o_p, z_p, dgu_p, e_p, gains) = refs[:15]
    (out_sq, out_d, out_gains) = refs[15:18]
    refs = refs[18:]
    (a_own, a_in, z_own, z_in, b_own, b_in, e_own, e_in) = refs[:8]
    (g_sq, q0, q1, q2, g_d, d0, d1, d2, gain_out, gain_in) = refs[8:18]
    refs = refs[18:]
    x_sq, x_d = refs[:2]
    (sem_load, sem_bload, sem_bsend, sem_brecv) = refs[2:6]
    (sem_send, sem_recv, sem_copy, gain_send, gain_recv) = refs[6:11]

    section, dpi, group = (lax.axis_index(name) for name in ("section", "dp", "group"))
    mask1 = 1 + section
    mask2 = 2 - section
    half = (group // mask1) % 2
    low2 = (group // mask2) % 2
    bit0 = dpi % 2
    bit1 = (dpi // 2) % 2
    first = (section, dpi, flip(group, mask1))
    second = (section, dpi, flip(group, mask2))
    near = (section, flip(dpi, 1), group)
    far = (section, flip(dpi, 2), group)
    others = [(section, dpi, flip(group, mask)) for mask in extra]
    partners = [first, second, near, far] + others

    barrier = pltpu.get_barrier_semaphore()
    for partner in partners:
        pl.semaphore_signal(barrier, inc=1, device_id=partner, device_id_type=MESH)
    pl.semaphore_wait(barrier, len(partners))

    def remote(src, dst, send, recv, device):
        return pltpu.make_async_remote_copy(
            src_ref=src, dst_ref=dst, send_sem=send, recv_sem=recv, device_id=device, device_id_type=MESH
        )

    def load_a(slot):
        return (
            pltpu.make_async_copy((nf_t, o_t, na_t)[slot], a_own.at[slot], sem_load.at[0, slot]),
            pltpu.make_async_copy((nf_p, o_p, na_p)[slot], a_in.at[slot], sem_load.at[1, slot]),
        )

    def load_z():
        return (
            pltpu.make_async_copy(z_t.at[pl.ds(0, 4), half], z_own, sem_load.at[0, 3]),
            pltpu.make_async_copy(z_p, z_in, sem_load.at[1, 3]),
        )

    def load_gu(i):
        return (
            pltpu.make_async_copy(dgu.at[half * 11 + i], b_own.at[i], sem_bload.at[0, i]),
            pltpu.make_async_copy(dgu_p.at[i], b_in.at[i], sem_bload.at[1, i]),
        )

    def load_e(k):
        return (
            pltpu.make_async_copy(e_cols.at[k], e_own.at[k], sem_bload.at[0, 19 + k]),
            pltpu.make_async_copy(e_p.at[k], e_in.at[k], sem_bload.at[1, 19 + k]),
        )

    def late(part, i):
        return f_cols.at[part * 2 + i] if i < 2 else dm.at[part * 6 + i - 2]

    def load_late(i):
        return pltpu.make_async_copy(late(half, i), b_own.at[11 + i], sem_bload.at[0, 11 + i])

    def send_late(i):
        return remote(late(1 - half, i), b_in.at[11 + i], sem_bsend.at[i], sem_brecv.at[i], first)

    def start(copies):
        for copy in copies:
            copy.start()

    def finish_copies(copies):
        for copy in copies:
            copy.wait()

    kinds = ((0, 0, 11), (1, 11, 2), (2, 13, 6))
    start(load_z())
    start(load_e(0))
    for i in range(8):
        send_late(i).start()
    start(load_a(0))
    for i in range(11):
        start(load_gu(i))
        if i in (2, 5, 8):
            start(load_e(i // 3 + 1))
    start(load_a(1))
    start(load_a(2))
    for i in range(8):
        load_late(i).start()

    class Square:
        base, rows = 4, 256
        partial, recv0, recv1, recv2, xs, out = g_sq, q0, q1, q2, x_sq, out_sq

    class Down:
        base, rows = 0, 352
        partial, recv0, recv1, recv2, xs, out = g_d, d0, d1, d2, x_d, out_d

    def rows_at(cls, part):
        size = cls.rows // 2
        return pl.ds(pl.multiple_of(part * size, 16), size)

    def hop(cls, c, i, src, dst, device):
        k = cls.base + c
        return remote(src, dst, sem_send.at[i, k], sem_recv.at[i, k], device)

    def hops(cls, c):
        both = pl.ds(0, 2)
        if cls is Down:
            return (
                lambda: hop(cls, c, 0, cls.partial.at[c, both, 1 - bit0], cls.recv0.at[c], near),
                lambda: hop(cls, c, 1, cls.recv0.at[c, 1 - bit1], cls.recv1.at[c], far),
                lambda: hop(cls, c, 2, cls.recv1.at[c, rows_at(cls, 1 - low2)], cls.recv2.at[c], second),
            )
        return (
            lambda: hop(cls, c, 0, cls.partial.at[c, both, both, rows_at(cls, 1 - low2)], cls.recv0.at[c], second),
            lambda: hop(cls, c, 1, cls.recv0.at[c, both, 1 - bit0], cls.recv1.at[c], near),
            lambda: hop(cls, c, 2, cls.recv1.at[c, 1 - bit1], cls.recv2.at[c], far),
        )

    def combine(cls, c, i):
        if cls is Down:
            if i == 0:
                for j in range(2):
                    cls.recv0[c, j] = summed(cls.partial[c, j, bit0], cls.recv0[c, j])
            elif i == 1:
                cls.recv1[c] = summed(cls.recv0[c, bit1], cls.recv1[c])
            else:
                cls.recv2[c] = summed(cls.recv1[c, rows_at(cls, low2)], cls.recv2[c])
        elif i == 0:
            for j in range(4):
                cls.recv0[c, j // 2, j % 2] = summed(
                    cls.partial[c, j // 2, j % 2, rows_at(cls, low2)], cls.recv0[c, j // 2, j % 2]
                )
        elif i == 1:
            for j in range(2):
                cls.recv1[c, j] = summed(cls.recv0[c, j, bit0], cls.recv1[c, j])
        else:
            cls.recv2[c] = summed(cls.recv1[c, bit1], cls.recv2[c])

    def to_extra(cls, c, i):
        k = cls.base + c
        src = cls.recv2.at[c] if i == 0 else cls.xs.at[i - 1, c]
        return remote(src, cls.xs.at[i, c], sem_send.at[6 + i, k], sem_recv.at[6 + i, k], others[i])

    def final(cls, c):
        return cls.recv2.at[c] if n_extra == 0 else cls.xs.at[n_extra - 1, c]

    def share_second(cls, c):
        k = cls.base + c
        return remote(final(cls, c), cls.out.at[half, c, rows_at(cls, low2)], sem_send.at[3, k], sem_recv.at[3, k], second)

    def share_first(cls, c):
        k = cls.base + c
        return remote(final(cls, c), cls.out.at[half, c, rows_at(cls, low2)], sem_send.at[4, k], sem_recv.at[4, k], first)

    def pass_on(cls, c):
        k = cls.base + c
        block = cls.out.at[half, c, rows_at(cls, 1 - low2)]
        return remote(block, block, sem_send.at[5, k], sem_recv.at[5, k], first)

    def keep(cls, c):
        return pltpu.make_async_copy(final(cls, c), cls.out.at[half, c, rows_at(cls, low2)], sem_copy.at[cls.base + c])

    def multiply(left, right, left2, right2):
        total = jnp.dot(left, right, preferred_element_type=jnp.float32)
        total += jnp.dot(left2, right2, preferred_element_type=jnp.float32)
        return total.astype(jnp.bfloat16)

    def partial_square(c):
        for kind, base, count in kinds:

            @pl.when(c == base)
            def _():
                finish_copies(load_a(kind))

        @pl.when(c < 11)
        def _():
            finish_copies(load_gu(c))

        for i in range(8):

            @pl.when(c == 11 + i)
            def _():
                load_late(i).wait()
                send_late(i).wait_recv()

        for kind, base, count in kinds:

            @pl.when((c >= base) & (c < base + count))
            def _():
                for j in range(4):
                    rows = pl.ds(j * 256, 256)
                    g_sq[c, j // 2, j % 2] = multiply(
                        a_own[kind, rows, :], b_own[c], a_in[kind, rows, :], b_in[c]
                    )

        hops(Square, c)[0]().start()

    def partial_down(c):
        @pl.when(c == 0)
        def _():
            finish_copies(load_z())

        finish_copies(load_e(c))
        for j in range(4):
            g_d[c, j // 2, j % 2] = multiply(z_own[j], e_own[c], z_in[j], e_in[c])
        hops(Down, c)[0]().start()

    def share(cls, c):
        share_second(cls, c).start()
        share_first(cls, c).start()
        keep(cls, c).start()

    def stage_hop(i, cls, c):
        hops(cls, c)[i]().wait_recv()
        combine(cls, c, i)
        if i < 2:
            hops(cls, c)[i + 1]().start()
        elif n_extra:
            to_extra(cls, c, 0).start()
        else:
            share(cls, c)

    def stage_extra(cls, c, i):
        to_extra(cls, c, i).wait()
        mine = cls.recv2[c] if i == 0 else cls.xs[i - 1, c]
        cls.xs[i, c] = summed(mine, cls.xs[i, c])
        if i + 1 < n_extra:
            to_extra(cls, c, i + 1).start()
        else:
            share(cls, c)

    def stage_pass(cls, c):
        share_second(cls, c).wait_recv()
        pass_on(cls, c).start()

    def partial(cls, c):
        (partial_square if cls is Square else partial_down)(c)

    stages = [partial] + [functools.partial(stage_hop, i) for i in range(3)]
    stages += [functools.partial(lambda i, cls, c: stage_extra(cls, c, i), i) for i in range(n_extra)]
    stages += [stage_pass]

    def gain_exchange(i):
        return remote(gain_out.at[i], gain_in.at[i], gain_send.at[i], gain_recv.at[i], partners[i])

    steps = 23 + LAG * (len(stages) - 1)

    @pl.loop(0, steps)
    def _(t):
        for i, stage in enumerate(stages):
            c = t - LAG * i
            turn = c // 5

            @pl.when((c >= 0) & (c < 20))
            def _():
                @pl.when(c % 5 == 0)
                def _():
                    stage(Down, turn)

                @pl.when(c % 5 != 0)
                def _():
                    stage(Square, c - 1 - turn)

            @pl.when((c >= 20) & (c < 23))
            def _():
                stage(Square, c - 4)

        for i in range(len(partners)):

            @pl.when(t == 3 * i + 2)
            def _():
                if i == 0:
                    gain_out[0] = gains[...]
                else:
                    gain_exchange(i - 1).wait()
                    gain_out[i] = gain_out[i - 1] + gain_in[i - 1]
                gain_exchange(i).start()

    last = len(partners) - 1
    gain_exchange(last).wait()
    out_gains[...] = gain_out[last] + gain_in[last]

    for i in range(8):
        send_late(i).wait_send()

    def finish(cls, c):
        for make in hops(cls, c):
            make().wait_send()
        share_second(cls, c).wait_send()
        share_first(cls, c).wait()
        pass_on(cls, c).wait()
        keep(cls, c).wait()

    @pl.loop(0, 4)
    def _(c):
        finish(Down, c)

    @pl.loop(0, 19)
    def _(c):
        finish(Square, c)


def reduce_gradients(group_size, activations, gains):
    extra = []
    mask = 4
    while mask < group_size:
        extra.append(mask)
        mask *= 2
    n_extra = len(extra)
    low = jnp.bfloat16
    tokens = activations[0].shape[1]
    scratch = [
        pltpu.VMEM((3, D, tokens), low),
        pltpu.VMEM((3, D, tokens), low),
        pltpu.VMEM((4, 352, tokens), low),
        pltpu.VMEM((4, 352, tokens), low),
        pltpu.VMEM((19, tokens, BLOCK), low),
        pltpu.VMEM((19, tokens, BLOCK), low),
        pltpu.VMEM((4, tokens, BLOCK), low),
        pltpu.VMEM((4, tokens, BLOCK), low),
        pltpu.VMEM((19, 2, 2, 256, BLOCK), low),
        pltpu.VMEM((19, 2, 2, 128, BLOCK), low),
        pltpu.VMEM((19, 2, 128, BLOCK), low),
        pltpu.VMEM((19, 128, BLOCK), low),
        pltpu.VMEM((4, 2, 2, 352, BLOCK), low),
        pltpu.VMEM((4, 2, 352, BLOCK), low),
        pltpu.VMEM((4, 352, BLOCK), low),
        pltpu.VMEM((4, 176, BLOCK), low),
        pltpu.VMEM((4 + n_extra, 8, D), jnp.float32),
        pltpu.VMEM((4 + n_extra, 8, D), jnp.float32),
        pltpu.VMEM((max(n_extra, 1), 19 if n_extra else 1, 128, BLOCK), low),
        pltpu.VMEM((max(n_extra, 1), 4 if n_extra else 1, 176, BLOCK), low),
        pltpu.SemaphoreType.DMA((2, 4)),
        pltpu.SemaphoreType.DMA((2, 23)),
        pltpu.SemaphoreType.DMA((8,)),
        pltpu.SemaphoreType.DMA((8,)),
        pltpu.SemaphoreType.DMA((6 + n_extra, 23)),
        pltpu.SemaphoreType.DMA((6 + n_extra, 23)),
        pltpu.SemaphoreType.DMA((23,)),
        pltpu.SemaphoreType.DMA((4 + n_extra,)),
        pltpu.SemaphoreType.DMA((4 + n_extra,)),
    ]
    anywhere = pl.BlockSpec(memory_space=pl.ANY)
    near_by = pl.BlockSpec(memory_space=pltpu.VMEM)
    return pl.pallas_call(
        functools.partial(reduce_kernel, tuple(extra)),
        out_shape=(
            jax.ShapeDtypeStruct((2, 19, 256, BLOCK), low),
            jax.ShapeDtypeStruct((2, 4, 352, BLOCK), low),
            jax.ShapeDtypeStruct((8, D), jnp.float32),
        ),
        in_specs=[anywhere] * 14 + [near_by],
        out_specs=(anywhere, anywhere, near_by),
        scratch_shapes=scratch,
        compiler_params=pltpu.CompilerParams(
            collective_id=0, has_side_effects=True, vmem_limit_bytes=58 * 2**20
        ),
        cost_estimate=pl.CostEstimate(flops=13 * 10**9, bytes_accessed=30 * 10**6, transcendentals=0),
        name="reduce_gradients",
    )(*activations, gains)


def to_f32(value):
    return value.astype(jnp.float32)


def to_low(value):
    return value.astype(jnp.bfloat16)


def by_rows(left, right):
    return lax.dot_general(left, right, (((1,), (1,)), ((), ())), preferred_element_type=jnp.float32)


def by_tokens(left, right):
    return lax.dot_general(left, right, (((0,), (0,)), ((), ())), preferred_element_type=jnp.float32)


def times(left, right):
    return jnp.dot(left, right, preferred_element_type=jnp.float32)


def cols(index, size=BLOCK, base=0):
    return pl.ds(pl.multiple_of(base + index * size, 128), size)


def inverse_rms(values):
    return lax.rsqrt(jnp.mean(values * values, axis=-1, keepdims=True) + EPS)


def layer_kernel(*refs):
    (tokens, cotangent, mem_k, mem_v, index, flags, cosine, sine, gain_a, gain_f) = refs[:10]
    (w_qkv_hbm, w_o_hbm, w_gu_hbm, w_d_hbm) = refs[10:14]
    (act, igrad, na_t, nf_t, o_t, z_t, dgu, dm, f_cols, e_cols) = refs[14:24]
    (na_p, nf_p, o_p, z_p, dgu_p, e_p, gains) = refs[24:31]
    refs = refs[31:]
    (w_qkv, w_o, w_gu, w_d, xs, qkv, probs, resid, factors, grads, picked_k, picked_v) = refs[:12]
    (normed, attended, hidden, turned, hidden_t, y_low, wide, dh, f_low, d_att, gx) = refs[12:23]
    (sem_w, sem_in, sem_mem, sem_t, sem_out, sem_send, sem_recv, sem_xsend, sem_xrecv) = refs[23:32]

    section, dpi, group = (lax.axis_index(name) for name in ("section", "dp", "group"))
    mask1 = 1 + section
    half = (group // mask1) % 2
    twin = (1 - section, dpi, group)
    first = (section, dpi, flip(group, mask1))
    is_lower = section == 0
    is_upper = section == 1
    scale = HEAD_DIM ** (-0.5)

    weights = []
    for i, (src, dst, pieces) in enumerate(
        ((w_qkv_hbm, w_qkv, 4), (w_o_hbm, w_o, 1), (w_gu_hbm, w_gu, 4), (w_d_hbm, w_d, 2))
    ):
        size = src.shape[0] // pieces
        weights.append(
            [
                pltpu.make_async_copy(src.at[pl.ds(p * size, size)], dst.at[pl.ds(p * size, size)], sem_w.at[i, p])
                for p in range(pieces)
            ]
        )

    def rows(m):
        return pl.ds(m * SEG, SEG)

    def load_tokens(m):
        return pltpu.make_async_copy(tokens.at[rows(m)], xs.at[m], sem_in.at[0, m])

    def load_cotangent(m):
        return pltpu.make_async_copy(cotangent.at[rows(m)], grads.at[m], sem_in.at[1, m])

    def send_up(m):
        return pltpu.make_async_remote_copy(
            src_ref=y_low.at[m], dst_ref=xs.at[m], send_sem=sem_send.at[0, m], recv_sem=sem_recv.at[0, m],
            device_id=twin, device_id_type=MESH,
        )

    def send_down(m):
        return pltpu.make_async_remote_copy(
            src_ref=gx.at[m], dst_ref=grads.at[m], send_sem=sem_send.at[1, m], recv_sem=sem_recv.at[1, m],
            device_id=twin, device_id_type=MESH,
        )

    @pl.when(is_lower)
    def _():
        load_tokens(0).start()

    for copy in weights[0]:
        copy.start()

    @pl.when(is_lower)
    def _():
        load_tokens(1).start()

    memory_in = [
        pltpu.make_async_copy(src.at[m], factors.at[m, :, cols(i, D)], sem_mem.at[i, m])
        for m in range(MICRO)
        for i, src in enumerate((mem_k, mem_v))
    ]

    @pl.when(is_upper)
    def _():
        for copy in memory_in:
            copy.start()
        for m in range(MICRO):
            load_cotangent(m).start()

    for group_copies in weights[1:]:
        for copy in group_copies:
            copy.start()

    barrier = pltpu.get_barrier_semaphore()
    pl.semaphore_signal(barrier, inc=1, device_id=twin, device_id_type=MESH)
    pl.semaphore_signal(barrier, inc=1, device_id=first, device_id_type=MESH)
    pl.semaphore_wait(barrier, 2)

    @pl.when(is_lower)
    def _():
        picked_k[...] = jnp.zeros_like(picked_k)
        picked_v[...] = jnp.zeros_like(picked_v)

    @pl.when(is_upper)
    def _():
        for copy in memory_in:
            copy.wait()
        places = lax.broadcasted_iota(jnp.int32, (SEG, TOPM), 0)
        for m in range(MICRO):
            chosen = to_low(to_f32(index[m : m + 1, :] == places).T)
            for n in range(4):
                picked_k[m, :, cols(n)] = to_low(times(chosen, factors[m, :, cols(n)]))
                picked_v[m, :, cols(n)] = to_low(times(chosen, factors[m, :, cols(n, BLOCK, D)]))

    eye = to_low(
        to_f32(
            lax.broadcasted_iota(jnp.int32, (BLOCK, BLOCK), 0) == lax.broadcasted_iota(jnp.int32, (BLOCK, BLOCK), 1)
        )
    )
    sent = []

    def exchange(src, dst, at):
        copy = pltpu.make_async_remote_copy(
            src_ref=src, dst_ref=dst, send_sem=sem_xsend.at[at], recv_sem=sem_xrecv.at[at],
            device_id=first, device_id_type=MESH,
        )
        copy.start()
        sent.append(copy)

    def local(src, dst, sem):
        copy = pltpu.make_async_copy(src, dst, sem)
        copy.start()
        sent.append(copy)

    def turn(src, width, view, out, kind, m):
        def step(j, _):
            view[pl.ds(pl.multiple_of(j * BLOCK, BLOCK), BLOCK), :] = to_low(by_rows(eye, src[:, cols(j)]))
            return 0

        lax.fori_loop(0, width // BLOCK, step, 0, unroll=True)
        local(view, out.at[:, cols(m)], sem_t.at[kind, m])

    def turn_square(src, kind, out, partner_out, m):
        view = turned.at[m, kind]
        turn(src, D, view, out, kind, m)
        exchange(view, partner_out.at[:, cols(m)], kind * MICRO + m)

    def forward(m):
        @pl.when(is_lower)
        def _():
            load_tokens(m).wait()

        @pl.when(is_upper)
        def _():
            send_up(m).wait_recv()

        x = to_f32(xs[m])
        normed[...] = to_low(x * inverse_rms(x) * to_f32(gain_a[...]))
        if m == 0:
            for copy in weights[0]:
                copy.wait()

        def rotated(j, _):
            block = times(normed[...], w_qkv[:, cols(j)])
            for p in range(2):
                part = block[:, p * HEAD_DIM : (p + 1) * HEAD_DIM]
                part = part * cosine[...] + pltpu.roll(part, HEAD_DIM // 2, 1) * sine[...]
                qkv[m, :, cols(2 * j + p, HEAD_DIM)] = to_low(part)
            return 0

        lax.fori_loop(0, 8, rotated, 0, unroll=4)

        def plain(j, _):
            qkv[m, :, cols(j, BLOCK, 2 * D)] = to_low(times(normed[...], w_qkv[:, cols(j, BLOCK, 2 * D)]))
            return 0

        lax.fori_loop(0, 4, plain, 0, unroll=True)
        turn_square(normed, 0, na_t, na_p, m)
        bias = (1 - flags[m] * section).astype(jnp.float32) * NEG
        causal = lax.broadcasted_iota(jnp.int32, (SEG, SEG), 0) >= lax.broadcasted_iota(jnp.int32, (SEG, SEG), 1)

        def head(h, _):
            query = qkv[m, :, cols(h, HEAD_DIM)]
            local = by_rows(query, qkv[m, :, cols(h, HEAD_DIM, D)]) * scale
            local = jnp.where(causal, local, NEG)
            remote = by_rows(query, picked_k[m, :, cols(h, HEAD_DIM)]) * scale + bias
            peak = jnp.maximum(
                jnp.max(local, axis=-1, keepdims=True), jnp.max(remote, axis=-1, keepdims=True)
            )
            local = jnp.exp(local - peak)
            remote = jnp.exp(remote - peak)
            share = 1.0 / (jnp.sum(local, axis=-1, keepdims=True) + jnp.sum(remote, axis=-1, keepdims=True))
            local = to_low(local * share)
            remote = to_low(remote * share)
            probs[m, h, :, :SEG] = local
            probs[m, h, :, SEG:] = remote
            result = times(local, qkv[m, :, cols(h, HEAD_DIM, 2 * D)])
            result += times(remote, picked_v[m, :, cols(h, HEAD_DIM)])
            attended[:, cols(h, HEAD_DIM)] = to_low(result)
            return 0

        lax.fori_loop(0, HEADS, head, 0, unroll=4)
        if m == 0:
            weights[1][0].wait()

        def project(n, _):
            resid[m, :, cols(n)] = to_f32(xs[m, :, cols(n)]) + times(attended[...], w_o[:, cols(n)])
            return 0

        lax.fori_loop(0, 4, project, 0, unroll=True)
        turn_square(attended, 1, o_t, o_p, m)
        h = resid[m]
        normed[...] = to_low(h * inverse_rms(h) * to_f32(gain_f[...]))
        if m == 0:
            for copy in weights[2]:
                copy.wait()

        def gate(j, _):
            a = times(normed[...], w_gu[:, cols(j)])
            u = times(normed[...], w_gu[:, cols(j, BLOCK, FF)])
            sg = jax.nn.sigmoid(a)
            silu = a * sg
            hidden[:, cols(j)] = to_low(silu * u)
            factors[m, :, cols(j)] = to_low(u * sg * (1.0 + a * (1.0 - sg)))
            factors[m, :, cols(j, BLOCK, FF)] = to_low(silu)
            return 0

        lax.fori_loop(0, FF // BLOCK, gate, 0, unroll=4)
        if m == 0:
            for copy in weights[3]:
                copy.wait()

        def down(n, _):
            y_low[m, :, cols(n)] = to_low(resid[m, :, cols(n)] + times(hidden[...], w_d[:, cols(n)]))
            return 0

        lax.fori_loop(0, 4, down, 0, unroll=2)

        @pl.when(is_lower)
        def _():
            send_up(m).start()

        write_out(y_low.at[m], act.at[rows(m)], 0, m).start()
        turn_square(normed, 2, nf_t, nf_p, m)
        turn(hidden, FF, hidden_t.at[m], z_t, 3, m)
        for j in range(4):
            at = pl.multiple_of(704 * j + 352 * (1 - half), 16)
            exchange(
                hidden_t.at[m, pl.ds(at, 352)], z_p.at[j, :, cols(m)], 3 * MICRO + 4 * m + j
            )

    def write_out(src, dst, kind, m):
        return pltpu.make_async_copy(src, dst, sem_out.at[kind, m])

    def block_out(src, dst, kind, m, i):
        return write_out(src.at[m, :, cols(i)], dst.at[i, rows(m)], kind, m)

    block_sets = ((grads, e_cols, 2, 4), (factors, dgu, 3, 22), (f_low, f_cols, 4, 4), (qkv, dm, 5, 12))

    def start_blocks(which, m):
        src, dst, kind, count = block_sets[which]
        for i in range(count):
            block_out(src, dst, kind, m, i).start()

    def wait_blocks(which, m):
        src, dst, kind, count = block_sets[which]
        whole = dst.at[:, rows(m)]
        pltpu.make_async_copy(whole, whole, sem_out.at[kind, m]).wait()

    def norm_back(d_normed, values, gain, incoming):
        inverse = inverse_rms(values)
        scaled = d_normed * to_f32(gain)
        column = jnp.sum(d_normed * (values * inverse), axis=0, keepdims=True)
        centre = jnp.mean(scaled * values, axis=-1, keepdims=True)
        return incoming + inverse * scaled - values * (inverse * inverse * inverse * centre), column

    def backward(m):
        @pl.when(is_upper)
        def _():
            load_cotangent(m).wait()

        @pl.when(is_lower)
        def _():
            send_down(m).wait_recv()

        start_blocks(0, m)
        for i in range(4):
            exchange(grads.at[m, :, cols(i)], e_p.at[i, rows(m)], 14 + m * 15 + i)

        def gate_back(j, _):
            dz = by_rows(grads[m], w_d[pl.ds(pl.multiple_of(j * BLOCK, BLOCK), BLOCK), :])
            factors[m, :, cols(j)] = to_low(dz * to_f32(factors[m, :, cols(j)]))
            factors[m, :, cols(j, BLOCK, FF)] = to_low(dz * to_f32(factors[m, :, cols(j, BLOCK, FF)]))
            return 0

        lax.fori_loop(0, FF // BLOCK, gate_back, 0, unroll=4)
        start_blocks(1, m)
        for i in range(11):
            exchange(
                factors.at[m, :, cols((1 - half) * 11 + i)], dgu_p.at[i, rows(m)], 18 + m * 15 + i
            )


        def gate_up_back(n, _):
            wide[:, cols(n)] = by_rows(factors[m], w_gu[pl.ds(pl.multiple_of(n * BLOCK, BLOCK), BLOCK), :])
            return 0

        lax.fori_loop(0, 4, gate_up_back, 0)
        result, column = norm_back(wide[...], resid[m], gain_f[...], to_f32(grads[m]))
        dh[...] = result
        f_low[m] = to_low(result)
        gains[1:2, :] = column if m == 0 else gains[1:2, :] + column
        start_blocks(2, m)

        def out_back(n, _):
            d_att[:, cols(n)] = to_low(by_rows(f_low[m], w_o[pl.ds(pl.multiple_of(n * BLOCK, BLOCK), BLOCK), :]))
            return 0

        lax.fori_loop(0, 4, out_back, 0, unroll=True)

        def rotate_back(part):
            return part * cosine[...] - pltpu.roll(part, HEAD_DIM // 2, 1) * sine[...]

        def head_back(h, _):
            at_q, at_k, at_v = (cols(h, HEAD_DIM, base) for base in (0, D, 2 * D))
            query, key, value = qkv[m, :, at_q], qkv[m, :, at_k], qkv[m, :, at_v]
            d_out = d_att[:, cols(h, HEAD_DIM)]
            p_local = probs[m, h, :, :SEG]
            p_remote = probs[m, h, :, SEG:]
            d_local = by_rows(d_out, value)
            d_remote = by_rows(d_out, picked_v[m, :, cols(h, HEAD_DIM)])
            wide_local, wide_remote = to_f32(p_local), to_f32(p_remote)
            centre = jnp.sum(wide_local * d_local, axis=-1, keepdims=True) + jnp.sum(
                wide_remote * d_remote, axis=-1, keepdims=True
            )
            d_local = to_low(wide_local * (d_local - centre))
            d_remote = to_low(wide_remote * (d_remote - centre))
            d_query = (times(d_local, key) + times(d_remote, picked_k[m, :, cols(h, HEAD_DIM)])) * scale
            d_key = by_tokens(d_local, query) * scale
            qkv[m, :, at_v] = to_low(by_tokens(p_local, d_out))
            qkv[m, :, at_q] = to_low(rotate_back(d_query))
            qkv[m, :, at_k] = to_low(rotate_back(d_key))
            return 0

        lax.fori_loop(0, HEADS, head_back, 0, unroll=2)
        start_blocks(3, m)

        def qkv_back(n, _):
            wide[:, cols(n)] = by_rows(qkv[m], w_qkv[pl.ds(pl.multiple_of(n * BLOCK, BLOCK), BLOCK), :])
            return 0

        lax.fori_loop(0, 4, qkv_back, 0)
        result, column = norm_back(wide[...], to_f32(xs[m]), gain_a[...], dh[...])
        gx[m] = to_low(result)
        gains[0:1, :] = column if m == 0 else gains[0:1, :] + column

        @pl.when(is_upper)
        def _():
            send_down(m).start()

        write_out(gx.at[m], igrad.at[rows(m)], 1, m).start()

    gains[...] = jnp.zeros_like(gains)
    for m in range(MICRO):
        forward(m)
    for m in range(MICRO):
        backward(m)

    for m in range(MICRO):
        write_out(y_low.at[m], act.at[rows(m)], 0, m).wait()
        write_out(gx.at[m], igrad.at[rows(m)], 1, m).wait()
        for which in range(4):
            wait_blocks(which, m)
    for copy in sent:
        copy.wait()

    @pl.when(is_lower)
    def _():
        for m in range(MICRO):
            send_up(m).wait_send()

    @pl.when(is_upper)
    def _():
        for m in range(MICRO):
            send_down(m).wait_send()


def rotary_constants():
    half = HEAD_DIM // 2
    freqs = np.exp(-np.log(10000.0) * np.arange(half) * 2.0 / HEAD_DIM)
    angles = np.arange(SEG)[:, None] * freqs[None, :]
    cosine = np.concatenate([np.cos(angles), np.cos(angles)], axis=1)
    sine = np.concatenate([-np.sin(angles), np.sin(angles)], axis=1)
    return cosine.astype(np.float32), sine.astype(np.float32)


def run_layers(tokens, cotangent, mem_keys, mem_values, index, flags, gain_a, gain_f, w_qkv, w_o, w_gu, w_d):
    cosine, sine = rotary_constants()
    count = tokens.shape[0]
    low, wide = jnp.bfloat16, jnp.float32
    anywhere = pl.BlockSpec(memory_space=pl.ANY)
    near_by = pl.BlockSpec(memory_space=pltpu.VMEM)
    shape = jax.ShapeDtypeStruct
    outs = (
        shape((count, D), low),
        shape((count, D), low),
        shape((D, count), low),
        shape((D, count), low),
        shape((D, count), low),
        shape((FF, count), low),
        shape((22, count, BLOCK), low),
        shape((12, count, BLOCK), low),
        shape((4, count, BLOCK), low),
        shape((4, count, BLOCK), low),
        shape((D, count), low),
        shape((D, count), low),
        shape((D, count), low),
        shape((4, 352, count), low),
        shape((11, count, BLOCK), low),
        shape((4, count, BLOCK), low),
        shape((8, D), wide),
    )
    scratch = [
        pltpu.VMEM((D, 3 * D), low),
        pltpu.VMEM((D, D), low),
        pltpu.VMEM((D, 2 * FF), low),
        pltpu.VMEM((FF, D), low),
        pltpu.VMEM((MICRO, SEG, D), low),
        pltpu.VMEM((MICRO, SEG, 3 * D), low),
        pltpu.VMEM((MICRO, HEADS, SEG, SEG + TOPM), low),
        pltpu.VMEM((MICRO, SEG, D), wide),
        pltpu.VMEM((MICRO, SEG, 2 * FF), low),
        pltpu.VMEM((MICRO, SEG, D), low),
        pltpu.VMEM((MICRO, TOPM, D), low),
        pltpu.VMEM((MICRO, TOPM, D), low),
        pltpu.VMEM((SEG, D), low),
        pltpu.VMEM((SEG, D), low),
        pltpu.VMEM((SEG, FF), low),
        pltpu.VMEM((MICRO, 3, D, SEG), low),
        pltpu.VMEM((MICRO, FF, SEG), low),
        pltpu.VMEM((MICRO, SEG, D), low),
        pltpu.VMEM((SEG, D), wide),
        pltpu.VMEM((SEG, D), wide),
        pltpu.VMEM((MICRO, SEG, D), low),
        pltpu.VMEM((SEG, D), low),
        pltpu.VMEM((MICRO, SEG, D), low),
        pltpu.SemaphoreType.DMA((4, 4)),
        pltpu.SemaphoreType.DMA((2, MICRO)),
        pltpu.SemaphoreType.DMA((2, MICRO)),
        pltpu.SemaphoreType.DMA((4, MICRO)),
        pltpu.SemaphoreType.DMA((6, MICRO)),
        pltpu.SemaphoreType.DMA((2, MICRO)),
        pltpu.SemaphoreType.DMA((2, MICRO)),
        pltpu.SemaphoreType.DMA((44,)),
        pltpu.SemaphoreType.DMA((44,)),
    ]
    return pl.pallas_call(
        layer_kernel,
        out_shape=outs,
        in_specs=[anywhere] * 4
        + [near_by, pl.BlockSpec(memory_space=pltpu.SMEM)]
        + [near_by] * 4
        + [anywhere] * 4,
        out_specs=(anywhere,) * 16 + (near_by,),
        scratch_shapes=scratch,
        compiler_params=pltpu.CompilerParams(
            collective_id=1, has_side_effects=True, vmem_limit_bytes=60 * 2**20
        ),
        cost_estimate=pl.CostEstimate(flops=27 * 10**9, bytes_accessed=50 * 10**6, transcendentals=0),
        name="relay_layers",
    )(tokens, cotangent, mem_keys, mem_values, index, flags, cosine, sine, gain_a, gain_f, w_qkv, w_o, w_gu, w_d)


def finish_kernel(*refs):
    (sq, down, gains, act, igrad) = refs[:5]
    (gu_out, o_out, qkv_out, d_out, ga_out, gf_out, act_out, igrad_out) = refs[5:13]
    (sq_v, d_v, gu_v, o_v, qkv_v, down_v, sem_in, sem_out) = refs[13:]
    parts = (
        (gu_v, gu_out, 0, 11),
        (qkv_v, qkv_out, 13, 6),
        (o_v, o_out, 11, 2),
    )
    loads = [
        pltpu.make_async_copy(
            sq.at[:, pl.ds(base, count)], sq_v.at[:, pl.ds(base, count)], sem_in.at[i]
        )
        for i, (_, _, base, count) in enumerate(parts)
    ]
    load_d = pltpu.make_async_copy(down, d_v, sem_in.at[3])
    for copy in loads:
        copy.start()
    load_d.start()
    stores = [
        pltpu.make_async_copy(act, act_out, sem_out.at[8]),
        pltpu.make_async_copy(igrad, igrad_out, sem_out.at[9]),
    ]
    for copy in stores:
        copy.start()
    mine = cols(lax.axis_index("dp"))
    ga_out[...] = gains[0:1, mine]
    gf_out[...] = gains[1:2, mine]
    for i, (view, out, base, count) in enumerate(parts):
        loads[i].wait()
        for half in range(2):
            for c in range(count):
                at = pl.ds((half * count + c) * BLOCK, BLOCK)
                view[:, at] = sq_v[half, base + c].astype(jnp.float32)
            span = pl.ds(half * count * BLOCK, count * BLOCK)
            stores.append(pltpu.make_async_copy(view.at[:, span], out.at[:, span], sem_out.at[2 * i + half]))
            stores[-1].start()
    load_d.wait()
    for half in range(2):
        for k in range(4):
            down_v[pl.ds(half * 352, 352), pl.ds(k * BLOCK, BLOCK)] = d_v[half, k].astype(jnp.float32)
        span = pl.ds(half * 352, 352)
        stores.append(pltpu.make_async_copy(down_v.at[span], d_out.at[span], sem_out.at[6 + half]))
        stores[-1].start()
    for copy in stores:
        copy.wait()


def finish_gradients(out_sq, out_d, out_gains, act, igrad):
    anywhere = pl.BlockSpec(memory_space=pl.ANY)
    near_by = pl.BlockSpec(memory_space=pltpu.VMEM)
    shapes = ((256, 2 * FF), (256, D), (256, 3 * D), (704, D))
    wide = jnp.float32
    return pl.pallas_call(
        finish_kernel,
        out_shape=tuple(jax.ShapeDtypeStruct(shape, wide) for shape in shapes + ((1, BLOCK),) * 2)
        + (jax.ShapeDtypeStruct(act.shape, act.dtype),) * 2,
        in_specs=[anywhere] * 2 + [near_by] + [anywhere] * 2,
        out_specs=(anywhere,) * 4 + (near_by,) * 2 + (anywhere,) * 2,
        scratch_shapes=[pltpu.VMEM(out_sq.shape, jnp.bfloat16), pltpu.VMEM(out_d.shape, jnp.bfloat16)]
        + [pltpu.VMEM(shape, wide) for shape in shapes]
        + [pltpu.SemaphoreType.DMA((4,)), pltpu.SemaphoreType.DMA((10,))],
        compiler_params=pltpu.CompilerParams(vmem_limit_bytes=40 * 2**20),
        name="finish_gradients",
    )(out_sq, out_d, out_gains, act, igrad)


def body(
    group_size,
    tokens,
    cotangent,
    mem_keys,
    mem_values,
    mem_index,
    mem_flags,
    norm_attn,
    w_qkv,
    w_out,
    norm_ffn,
    w_gate_up,
    w_down,
):
    (act, igrad, na_t, nf_t, o_t, z_t, dgu, dm, f_cols, e_cols, na_p, nf_p, o_p, z_p, dgu_p, e_p, gains) = run_layers(
        tokens,
        cotangent,
        mem_keys,
        mem_values,
        mem_index,
        mem_flags,
        norm_attn,
        norm_ffn,
        w_qkv[0],
        w_out[0],
        w_gate_up[0],
        w_down[0],
    )
    halves = z_t.reshape(4, 2, 352, -1)
    reduced = reduce_gradients(
        group_size,
        (nf_t, na_t, o_t, halves, dgu, dm, f_cols, e_cols, nf_p, na_p, o_p, z_p, dgu_p, e_p),
        gains,
    )
    (grad_gu, grad_o, grad_qkv, grad_d, grad_na, grad_nf, act, igrad) = finish_gradients(*reduced, act, igrad)
    return (
        act[None],
        igrad[None],
        grad_na,
        grad_qkv[None],
        grad_o[None],
        grad_nf,
        grad_gu[None],
        grad_d[None],
    )


def solution(mesh):
    placed = (
        P(("dp", "group"), None),
        P(("dp", "group"), None),
        P(("dp", "group"), None, None),
        P(("dp", "group"), None, None),
        P(("dp", "group"), None),
        P(("dp", "group")),
        P("section", None),
        P("section", None, None),
        P("section", None, None),
        P("section", None),
        P("section", None, None),
        P("section", None, None),
    )
    return jax.shard_map(
        functools.partial(body, mesh.shape["group"]),
        mesh=mesh,
        in_specs=placed,
        out_specs=(
            P("section", ("dp", "group"), None),
            P("section", ("dp", "group"), None),
            P("section", "dp"),
            P("section", "dp", None),
            P("section", "dp", None),
            P("section", "dp"),
            P("section", "dp", None),
            P("section", "dp", None),
        ),
        check_vma=False,
    )
```

```python
import functools

import jax
import jax.numpy as jnp
import numpy as np
from jax import lax
from jax.experimental import pallas as pl
from jax.experimental.pallas import tpu as pltpu
from jax.sharding import PartitionSpec as P

D = 1024
HEADS = 8
HEAD_DIM = 128
FF = 2816
SEG = 256
TOPM = 128
MICRO = 2
EPS = 1e-05
NEG = -1e30
MESH = pl.DeviceIdType.MESH
BLOCK = 256
LAG = 2


def flip(value, mask):
    return value + mask * (1 - 2 * ((value // mask) % 2))


def down_span(j, bit):
    return pl.ds(pl.multiple_of(1408 * j + 640 * bit, 128), 768)


def summed(left, right):
    return (left.astype(jnp.float32) + right.astype(jnp.float32)).astype(jnp.bfloat16)


def reduce_kernel(extra, *refs):
    n_extra = len(extra)
    (nf_all, na_all, o_all, z_all, dgu, dm, f_cols, e_cols, nf_p, na_p, o_p, z_p, dgu_p, e_p, gains) = refs[:15]
    (out_sq, out_d, out_gains) = refs[15:18]
    refs = refs[18:]
    (a_own, a_in, z_own, z_in, b_own, b_in, e_own, e_in) = refs[:8]
    (g_sq, q0, q1, q2, g_d, d0, d1, d2, gain_out, gain_in) = refs[8:18]
    refs = refs[18:]
    x_sq, x_d, spread = refs[:3]
    (sem_load, sem_bload, sem_bsend, sem_brecv) = refs[3:7]
    (sem_send, sem_recv, sem_copy, gain_send, gain_recv) = refs[7:12]

    section, dpi, group = (lax.axis_index(name) for name in ("section", "dp", "group"))
    mask1 = 1 + section
    mask2 = 2 - section
    half = (group // mask1) % 2
    low2 = (group // mask2) % 2
    bit0 = dpi % 2
    bit1 = (dpi // 2) % 2
    first = (section, dpi, flip(group, mask1))
    second = (section, dpi, flip(group, mask2))
    near = (section, flip(dpi, 1), group)
    far = (section, flip(dpi, 2), group)
    others = [(section, dpi, flip(group, mask)) for mask in extra]
    partners = [first, second, near, far] + others

    barrier = pltpu.get_barrier_semaphore()
    for partner in partners:
        pl.semaphore_signal(barrier, inc=1, device_id=partner, device_id_type=MESH)
    pl.semaphore_wait(barrier, len(partners))

    def remote(src, dst, send, recv, device):
        return pltpu.make_async_remote_copy(
            src_ref=src, dst_ref=dst, send_sem=send, recv_sem=recv, device_id=device, device_id_type=MESH
        )

    def load_a(slot):
        return (
            pltpu.make_async_copy((nf_all, o_all, na_all)[slot], a_own.at[slot], sem_load.at[0, slot]),
            pltpu.make_async_copy((nf_p, o_p, na_p)[slot], a_in.at[slot], sem_load.at[1, slot]),
        )

    def load_z():
        own = [
            pltpu.make_async_copy(z_all.at[:, down_span(j, bit0)], z_own.at[j], sem_load.at[0, 3 + j])
            for j in range(2)
        ]
        return own + [pltpu.make_async_copy(z_p, z_in, sem_load.at[1, 3])]

    def load_gu(i):
        return (
            pltpu.make_async_copy(dgu.at[half * 11 + i], b_own.at[i], sem_bload.at[0, i]),
            pltpu.make_async_copy(dgu_p.at[i], b_in.at[i, pl.ds(0, SEG)], sem_bload.at[1, i]),
        )

    def send_gu(i):
        later = pl.ds(SEG, SEG)
        return remote(
            dgu.at[(1 - half) * 11 + i, later], b_in.at[i, later], sem_bsend.at[i], sem_brecv.at[i], first
        )

    def load_e(k):
        return (
            pltpu.make_async_copy(e_cols.at[k], e_own.at[k], sem_bload.at[0, 19 + k]),
            pltpu.make_async_copy(e_p.at[k], e_in.at[k], sem_bload.at[1, 19 + k]),
        )

    def late(part, i):
        return f_cols.at[part * 2 + i] if i < 2 else dm.at[part * 6 + i - 2]

    def load_late(i):
        return pltpu.make_async_copy(late(half, i), b_own.at[11 + i], sem_bload.at[0, 11 + i])

    def send_late(i):
        return remote(late(1 - half, i), b_in.at[11 + i], sem_bsend.at[11 + i], sem_brecv.at[11 + i], first)

    def start(copies):
        for copy in copies:
            copy.start()

    def finish_copies(copies):
        for copy in copies:
            copy.wait()

    kinds = ((0, 0, 11), (1, 11, 2), (2, 13, 6))
    start(load_z())
    for i in range(3):
        send_gu(i).start()
    start(load_e(0))
    start(load_a(0))
    for i in range(11):
        start(load_gu(i))
        if i in (2, 5, 8):
            start(load_e(i // 3 + 1))
    start(load_a(1))
    start(load_a(2))
    for i in range(8):
        load_late(i).start()

    def send_more(t):
        @pl.when(t < 8)
        def _():
            send_gu(t + 3).start()

        for i in range(8):

            @pl.when(t == 8 + i)
            def _():
                send_late(i).start()

    class Square:
        base, rows = 4, 256
        partial, recv0, recv1, recv2, xs, out = g_sq, q0, q1, q2, x_sq, out_sq

    class Down:
        base, rows = 0, 352
        partial, recv0, recv1, recv2, xs, out = g_d, d0, d1, d2, x_d, out_d

    def rows_at(cls, part):
        size = cls.rows // 2
        return pl.ds(pl.multiple_of(part * size, 16), size)

    def half_rows(part):
        return pl.ds(pl.multiple_of(part * 352, 16), 352)

    def hop(cls, c, i, src, dst, device):
        k = cls.base + c
        return remote(src, dst, sem_send.at[i, k], sem_recv.at[i, k], device)

    def hops(cls, c):
        both = pl.ds(0, 2)
        if cls is Down:
            return (
                lambda: hop(cls, c, 0, cls.partial.at[c, 1 - bit1], cls.recv0.at[c], far),
                lambda: hop(cls, c, 1, cls.recv0.at[c, half_rows(1 - half)], cls.recv1.at[c], first),
                lambda: hop(cls, c, 2, cls.recv1.at[c, rows_at(cls, 1 - low2)], cls.recv2.at[c], second),
            )
        return (
            lambda: hop(cls, c, 0, cls.partial.at[c, both, both, rows_at(cls, 1 - low2)], cls.recv0.at[c], second),
            lambda: hop(cls, c, 1, cls.recv0.at[c, both, 1 - bit0], cls.recv1.at[c], near),
            lambda: hop(cls, c, 2, cls.recv1.at[c, 1 - bit1], cls.recv2.at[c], far),
        )

    def combine(cls, c, i):
        if cls is Down:
            if i == 0:
                cls.recv0[c] = summed(cls.partial[c, bit1], cls.recv0[c])
            elif i == 1:
                cls.recv1[c] = summed(cls.recv0[c, half_rows(half)], cls.recv1[c])
            else:
                cls.recv2[c] = summed(cls.recv1[c, rows_at(cls, low2)], cls.recv2[c])
        elif i == 0:
            for j in range(4):
                cls.recv0[c, j // 2, j % 2] = summed(
                    cls.partial[c, j // 2, j % 2, rows_at(cls, low2)], cls.recv0[c, j // 2, j % 2]
                )
        elif i == 1:
            for j in range(2):
                cls.recv1[c, j] = summed(cls.recv0[c, j, bit0], cls.recv1[c, j])
        else:
            cls.recv2[c] = summed(cls.recv1[c, bit1], cls.recv2[c])

    def to_extra(cls, c, i):
        k = cls.base + c
        src = cls.recv2.at[c] if i == 0 else cls.xs.at[i - 1, c]
        return remote(src, cls.xs.at[i, c], sem_send.at[6 + i, k], sem_recv.at[6 + i, k], others[i])

    def final(cls, c):
        return cls.recv2.at[c] if n_extra == 0 else cls.xs.at[n_extra - 1, c]

    def share_second(cls, c):
        k = cls.base + c
        return remote(final(cls, c), cls.out.at[half, c, rows_at(cls, low2)], sem_send.at[3, k], sem_recv.at[3, k], second)

    def share_first(cls, c):
        k = cls.base + c
        return remote(final(cls, c), cls.out.at[half, c, rows_at(cls, low2)], sem_send.at[4, k], sem_recv.at[4, k], first)

    def pass_on(cls, c):
        k = cls.base + c
        block = cls.out.at[half, c, rows_at(cls, 1 - low2)]
        return remote(block, block, sem_send.at[5, k], sem_recv.at[5, k], first)

    def keep(cls, c):
        return pltpu.make_async_copy(final(cls, c), cls.out.at[half, c, rows_at(cls, low2)], sem_copy.at[cls.base + c])

    def multiply(left, right, left2, right2):
        return (by_tokens(left, right) + by_tokens(left2, right2)).astype(jnp.bfloat16)

    def partial_square(c):
        for kind, base, count in kinds:

            @pl.when(c == base)
            def _():
                finish_copies(load_a(kind))

        @pl.when(c < 11)
        def _():
            finish_copies(load_gu(c))
            send_gu(c).wait_recv()

        for i in range(8):

            @pl.when(c == 11 + i)
            def _():
                load_late(i).wait()
                send_late(i).wait_recv()

        for kind, base, count in kinds:

            @pl.when((c >= base) & (c < base + count))
            def _():
                for j in range(4):
                    rows = pl.ds(j * 256, 256)
                    g_sq[c, j // 2, j % 2] = multiply(
                        a_own[kind, :, rows], b_own[c], a_in[kind, :, rows], b_in[c]
                    )

        hops(Square, c)[0]().start()

    def partial_down(c):
        @pl.when(c == 0)
        def _():
            finish_copies(load_z())

        finish_copies(load_e(c))
        for j in range(2):
            spread[...] = multiply(z_own[j], e_own[c], z_in[j], e_in[c])
            g_d[c, j] = spread[pl.ds(pl.multiple_of(64 * bit0, 16), 704), :]
        hops(Down, c)[0]().start()

    def share(cls, c):
        share_second(cls, c).start()
        share_first(cls, c).start()
        keep(cls, c).start()

    def stage_hop(i, cls, c):
        hops(cls, c)[i]().wait_recv()
        combine(cls, c, i)
        if i < 2:
            hops(cls, c)[i + 1]().start()
        elif n_extra:
            to_extra(cls, c, 0).start()
        else:
            share(cls, c)

    def stage_extra(cls, c, i):
        to_extra(cls, c, i).wait()
        mine = cls.recv2[c] if i == 0 else cls.xs[i - 1, c]
        cls.xs[i, c] = summed(mine, cls.xs[i, c])
        if i + 1 < n_extra:
            to_extra(cls, c, i + 1).start()
        else:
            share(cls, c)

    def stage_pass(cls, c):
        share_second(cls, c).wait_recv()
        pass_on(cls, c).start()

    def partial(cls, c):
        (partial_square if cls is Square else partial_down)(c)

    stages = [partial] + [functools.partial(stage_hop, i) for i in range(3)]
    stages += [functools.partial(lambda i, cls, c: stage_extra(cls, c, i), i) for i in range(n_extra)]
    stages += [stage_pass]

    def gain_exchange(i):
        return remote(gain_out.at[i], gain_in.at[i], gain_send.at[i], gain_recv.at[i], partners[i])

    steps = 23 + LAG * (len(stages) - 1)

    @pl.loop(0, steps)
    def _(t):
        send_more(t)
        for i, stage in enumerate(stages):
            c = t - LAG * i
            turn = c // 5

            @pl.when((c >= 0) & (c < 20))
            def _():
                @pl.when(c % 5 == 0)
                def _():
                    stage(Down, turn)

                @pl.when(c % 5 != 0)
                def _():
                    stage(Square, c - 1 - turn)

            @pl.when((c >= 20) & (c < 23))
            def _():
                stage(Square, c - 4)

        for i in range(len(partners)):

            @pl.when(t == 3 * i + 2)
            def _():
                if i == 0:
                    gain_out[0] = gains[...]
                else:
                    gain_exchange(i - 1).wait()
                    gain_out[i] = gain_out[i - 1] + gain_in[i - 1]
                gain_exchange(i).start()

    last = len(partners) - 1
    gain_exchange(last).wait()
    out_gains[...] = gain_out[last] + gain_in[last]

    for i in range(8):
        send_late(i).wait_send()
    for i in range(11):
        send_gu(i).wait_send()

    def finish(cls, c):
        for make in hops(cls, c):
            make().wait_send()
        share_second(cls, c).wait_send()
        share_first(cls, c).wait()
        pass_on(cls, c).wait()
        keep(cls, c).wait()

    @pl.loop(0, 4)
    def _(c):
        finish(Down, c)

    @pl.loop(0, 19)
    def _(c):
        finish(Square, c)


def reduce_gradients(group_size, activations, gains):
    extra = []
    mask = 4
    while mask < group_size:
        extra.append(mask)
        mask *= 2
    n_extra = len(extra)
    low = jnp.bfloat16
    tokens = activations[0].shape[0]
    scratch = [
        pltpu.VMEM((3, tokens, D), low),
        pltpu.VMEM((3, tokens, D), low),
        pltpu.VMEM((2, tokens, 768), low),
        pltpu.VMEM((2, tokens, 768), low),
        pltpu.VMEM((19, tokens, BLOCK), low),
        pltpu.VMEM((19, tokens, BLOCK), low),
        pltpu.VMEM((4, tokens, BLOCK), low),
        pltpu.VMEM((4, tokens, BLOCK), low),
        pltpu.VMEM((19, 2, 2, 256, BLOCK), low),
        pltpu.VMEM((19, 2, 2, 128, BLOCK), low),
        pltpu.VMEM((19, 2, 128, BLOCK), low),
        pltpu.VMEM((19, 128, BLOCK), low),
        pltpu.VMEM((4, 2, 704, BLOCK), low),
        pltpu.VMEM((4, 704, BLOCK), low),
        pltpu.VMEM((4, 352, BLOCK), low),
        pltpu.VMEM((4, 176, BLOCK), low),
        pltpu.VMEM((4 + n_extra, 8, D), jnp.float32),
        pltpu.VMEM((4 + n_extra, 8, D), jnp.float32),
        pltpu.VMEM((max(n_extra, 1), 19 if n_extra else 1, 128, BLOCK), low),
        pltpu.VMEM((max(n_extra, 1), 4 if n_extra else 1, 176, BLOCK), low),
        pltpu.VMEM((768, BLOCK), low),
        pltpu.SemaphoreType.DMA((2, 5)),
        pltpu.SemaphoreType.DMA((2, 23)),
        pltpu.SemaphoreType.DMA((19,)),
        pltpu.SemaphoreType.DMA((19,)),
        pltpu.SemaphoreType.DMA((6 + n_extra, 23)),
        pltpu.SemaphoreType.DMA((6 + n_extra, 23)),
        pltpu.SemaphoreType.DMA((23,)),
        pltpu.SemaphoreType.DMA((4 + n_extra,)),
        pltpu.SemaphoreType.DMA((4 + n_extra,)),
    ]
    anywhere = pl.BlockSpec(memory_space=pl.ANY)
    near_by = pl.BlockSpec(memory_space=pltpu.VMEM)
    return pl.pallas_call(
        functools.partial(reduce_kernel, tuple(extra)),
        out_shape=(
            jax.ShapeDtypeStruct((2, 19, 256, BLOCK), low),
            jax.ShapeDtypeStruct((2, 4, 352, BLOCK), low),
            jax.ShapeDtypeStruct((8, D), jnp.float32),
        ),
        in_specs=[anywhere] * 14 + [near_by],
        out_specs=(anywhere, anywhere, near_by),
        scratch_shapes=scratch,
        compiler_params=pltpu.CompilerParams(
            collective_id=0, has_side_effects=True, vmem_limit_bytes=58 * 2**20
        ),
        cost_estimate=pl.CostEstimate(flops=13 * 10**9, bytes_accessed=30 * 10**6, transcendentals=0),
        name="reduce_gradients",
    )(*activations, gains)


def to_f32(value):
    return value.astype(jnp.float32)


def to_low(value):
    return value.astype(jnp.bfloat16)


def by_rows(left, right):
    return lax.dot_general(left, right, (((1,), (1,)), ((), ())), preferred_element_type=jnp.float32)


def by_tokens(left, right):
    return lax.dot_general(left, right, (((0,), (0,)), ((), ())), preferred_element_type=jnp.float32)


def times(left, right):
    return jnp.dot(left, right, preferred_element_type=jnp.float32)


def cols(index, size=BLOCK, base=0):
    if isinstance(index, int):
        return pl.ds(base + index * size, size)
    return pl.ds(pl.multiple_of(base + index * size, 128), size)


def inverse_rms(values):
    return lax.rsqrt(jnp.mean(values * values, axis=-1, keepdims=True) + EPS)


def layer_kernel(*refs):
    (tokens, cotangent, mem_k, mem_v, index, flags, cosine, sine, gain_a, gain_f) = refs[:10]
    (w_qkv_hbm, w_o_hbm, w_gu_hbm, w_d_hbm) = refs[10:14]
    (act, igrad, na_all, nf_all, o_all, z_all, dgu, dm, f_cols, e_cols) = refs[14:24]
    (na_p, nf_p, o_p, z_p, dgu_p, e_p, gains) = refs[24:31]
    refs = refs[31:]
    (w_qkv, w_o, w_gu, w_d, xs, qkv, probs, resid, factors, grads, picked_k, picked_v) = refs[:12]
    (kept, hidden, y_low, wide, dh, f_low, d_att, gx) = refs[12:20]
    (sem_w, sem_in, sem_mem, sem_t, sem_out, sem_send, sem_recv, sem_xsend, sem_xrecv) = refs[20:29]

    section, dpi, group = (lax.axis_index(name) for name in ("section", "dp", "group"))
    mask1 = 1 + section
    half = (group // mask1) % 2
    bit0 = dpi % 2
    twin = (1 - section, dpi, group)
    first = (section, dpi, flip(group, mask1))
    near = (section, flip(dpi, 1), group)
    is_lower = section == 0
    is_upper = section == 1
    scale = HEAD_DIM ** (-0.5)

    weights = []
    for i, (src, dst, pieces) in enumerate(
        ((w_qkv_hbm, w_qkv, 4), (w_o_hbm, w_o, 1), (w_gu_hbm, w_gu, 4), (w_d_hbm, w_d, 2))
    ):
        size = src.shape[0] // pieces
        weights.append(
            [
                pltpu.make_async_copy(src.at[pl.ds(p * size, size)], dst.at[pl.ds(p * size, size)], sem_w.at[i, p])
                for p in range(pieces)
            ]
        )

    def rows(m):
        return pl.ds(m * SEG, SEG)

    def load_tokens(m):
        return pltpu.make_async_copy(tokens.at[rows(m)], xs.at[m], sem_in.at[0, m])

    def load_cotangent(m):
        return pltpu.make_async_copy(cotangent.at[rows(m)], grads.at[m], sem_in.at[1, m])

    def send_up(m):
        return pltpu.make_async_remote_copy(
            src_ref=y_low.at[m], dst_ref=xs.at[m], send_sem=sem_send.at[0, m], recv_sem=sem_recv.at[0, m],
            device_id=twin, device_id_type=MESH,
        )

    def send_down(m):
        return pltpu.make_async_remote_copy(
            src_ref=gx.at[m], dst_ref=grads.at[m], send_sem=sem_send.at[1, m], recv_sem=sem_recv.at[1, m],
            device_id=twin, device_id_type=MESH,
        )

    @pl.when(is_lower)
    def _():
        load_tokens(0).start()

    for copy in weights[0]:
        copy.start()

    @pl.when(is_lower)
    def _():
        load_tokens(1).start()

    memory_in = [
        pltpu.make_async_copy(src.at[m], factors.at[m, :, cols(i, D)], sem_mem.at[i, m])
        for m in range(MICRO)
        for i, src in enumerate((mem_k, mem_v))
    ]

    @pl.when(is_upper)
    def _():
        for copy in memory_in:
            copy.start()
        for m in range(MICRO):
            load_cotangent(m).start()

    for group_copies in weights[1:]:
        for copy in group_copies:
            copy.start()

    barrier = pltpu.get_barrier_semaphore()
    pl.semaphore_signal(barrier, inc=1, device_id=twin, device_id_type=MESH)
    pl.semaphore_signal(barrier, inc=1, device_id=first, device_id_type=MESH)
    pl.semaphore_signal(barrier, inc=1, device_id=near, device_id_type=MESH)
    pl.semaphore_wait(barrier, 3)

    @pl.when(is_lower)
    def _():
        picked_k[...] = jnp.zeros_like(picked_k)
        picked_v[...] = jnp.zeros_like(picked_v)

    @pl.when(is_upper)
    def _():
        for copy in memory_in:
            copy.wait()
        places = lax.broadcasted_iota(jnp.int32, (SEG, TOPM), 0)
        for m in range(MICRO):
            chosen = to_low(to_f32(index[m : m + 1, :] == places).T)
            for n in range(4):
                picked_k[m, :, cols(n)] = to_low(times(chosen, factors[m, :, cols(n)]))
                picked_v[m, :, cols(n)] = to_low(times(chosen, factors[m, :, cols(n, BLOCK, D)]))

    sent = []

    def exchange(src, dst, at, device=first):
        copy = pltpu.make_async_remote_copy(
            src_ref=src, dst_ref=dst, send_sem=sem_xsend.at[at], recv_sem=sem_xrecv.at[at],
            device_id=device, device_id_type=MESH,
        )
        copy.start()
        return copy

    def exchange_grads(src, m, i):
        return exchange(src, e_p.at[i, rows(m)], 14 + m * 4 + i, near)

    @pl.when(is_upper)
    def _():
        for m in range(MICRO):
            for i in range(4):
                exchange_grads(cotangent.at[rows(m), cols(i)], m, i)

    def local(src, dst, sem):
        copy = pltpu.make_async_copy(src, dst, sem)
        copy.start()
        sent.append(copy)

    def share_kept(kind, out, partner_out, m):
        view = kept.at[m, kind]
        local(view, out.at[rows(m)], sem_t.at[kind, m])
        sent.append(exchange(view, partner_out.at[rows(m)], kind * MICRO + m))

    def forward(m):
        @pl.when(is_lower)
        def _():
            load_tokens(m).wait()

        @pl.when(is_upper)
        def _():
            send_up(m).wait_recv()

        x = to_f32(xs[m])
        normed = kept.at[m, 0]
        normed[...] = to_low(x * inverse_rms(x) * to_f32(gain_a[...]))
        if m == 0:
            for copy in weights[0]:
                copy.wait()

        def rotated(j):
            block = times(normed[...], w_qkv[:, cols(j)])
            for p in range(2):
                part = block[:, p * HEAD_DIM : (p + 1) * HEAD_DIM]
                part = part * cosine[...] + pltpu.roll(part, HEAD_DIM // 2, 1) * sine[...]
                qkv[m, :, cols(2 * j + p, HEAD_DIM)] = to_low(part)

        for i in range(8):
            rotated(i)

        def plain(j):
            qkv[m, :, cols(j, BLOCK, 2 * D)] = to_low(times(normed[...], w_qkv[:, cols(j, BLOCK, 2 * D)]))

        for i in range(4):
            plain(i)
        share_kept(0, na_all, na_p, m)
        attended = kept.at[m, 1]
        bias = (1 - flags[m] * section).astype(jnp.float32) * NEG
        causal = lax.broadcasted_iota(jnp.int32, (SEG, SEG), 0) >= lax.broadcasted_iota(jnp.int32, (SEG, SEG), 1)

        def head(h):
            query = qkv[m, :, cols(h, HEAD_DIM)]
            local = by_rows(query, qkv[m, :, cols(h, HEAD_DIM, D)]) * scale
            local = jnp.where(causal, local, NEG)
            remote = by_rows(query, picked_k[m, :, cols(h, HEAD_DIM)]) * scale + bias
            peak = jnp.maximum(
                jnp.max(local, axis=-1, keepdims=True), jnp.max(remote, axis=-1, keepdims=True)
            )
            local = jnp.exp(local - peak)
            remote = jnp.exp(remote - peak)
            share = 1.0 / (jnp.sum(local, axis=-1, keepdims=True) + jnp.sum(remote, axis=-1, keepdims=True))
            local = to_low(local * share)
            remote = to_low(remote * share)
            probs[m, h, :, :SEG] = local
            probs[m, h, :, SEG:] = remote
            result = times(local, qkv[m, :, cols(h, HEAD_DIM, 2 * D)])
            result += times(remote, picked_v[m, :, cols(h, HEAD_DIM)])
            attended[:, cols(h, HEAD_DIM)] = to_low(result)

        for i in range(HEADS):
            head(i)
        if m == 0:
            weights[1][0].wait()

        def project(n):
            resid[m, :, cols(n)] = to_f32(xs[m, :, cols(n)]) + times(attended[...], w_o[:, cols(n)])

        for i in range(4):
            project(i)
        share_kept(1, o_all, o_p, m)
        normed_ffn = kept.at[m, 2]
        h = resid[m]
        normed_ffn[...] = to_low(h * inverse_rms(h) * to_f32(gain_f[...]))
        if m == 0:
            for copy in weights[2]:
                copy.wait()

        def gate(j):
            a = times(normed_ffn[...], w_gu[:, cols(j)])
            u = times(normed_ffn[...], w_gu[:, cols(j, BLOCK, FF)])
            sg = jax.nn.sigmoid(a)
            silu = a * sg
            hidden[m, :, cols(j)] = to_low(silu * u)
            factors[m, :, cols(j)] = to_low(u * sg * (1.0 + a * (1.0 - sg)))
            factors[m, :, cols(j, BLOCK, FF)] = to_low(silu)

        for i in range(FF // BLOCK):
            gate(i)
        if m == 0:
            for copy in weights[3]:
                copy.wait()

        def down(n):
            y_low[m, :, cols(n)] = to_low(resid[m, :, cols(n)] + times(hidden[m], w_d[:, cols(n)]))

        for i in range(4):
            down(i)

        @pl.when(is_lower)
        def _():
            send_up(m).start()

        write_out(y_low.at[m], act.at[rows(m)], 0, m).start()
        share_kept(2, nf_all, nf_p, m)
        local(hidden.at[m], z_all.at[rows(m)], sem_t.at[3, m])
        for j in range(2):
            span = hidden.at[m, :, down_span(j, 1 - bit0)]
            sent.append(exchange(span, z_p.at[j, rows(m)], 3 * MICRO + 2 * m + j, near))

    def write_out(src, dst, kind, m):
        return pltpu.make_async_copy(src, dst, sem_out.at[kind, m])

    def block_out(src, dst, kind, m, i):
        return write_out(src.at[m, :, cols(i)], dst.at[i, rows(m)], kind, m)

    block_sets = ((grads, e_cols, 2, 4), (factors, dgu, 3, 22), (f_low, f_cols, 4, 4), (qkv, dm, 5, 12))

    def start_blocks(which, m):
        src, dst, kind, count = block_sets[which]
        for i in range(count):
            block_out(src, dst, kind, m, i).start()

    def wait_blocks(which, m):
        src, dst, kind, count = block_sets[which]
        whole = dst.at[:, rows(m)]
        pltpu.make_async_copy(whole, whole, sem_out.at[kind, m]).wait()

    def norm_back(d_normed, values, gain, incoming):
        inverse = inverse_rms(values)
        scaled = d_normed * to_f32(gain)
        column = jnp.sum(d_normed * (values * inverse), axis=0, keepdims=True)
        centre = jnp.mean(scaled * values, axis=-1, keepdims=True)
        return incoming + inverse * scaled - values * (inverse * inverse * inverse * centre), column

    def backward(m):
        @pl.when(is_upper)
        def _():
            load_cotangent(m).wait()

        @pl.when(is_lower)
        def _():
            send_down(m).wait_recv()

        start_blocks(0, m)

        @pl.when(is_lower)
        def _():
            for i in range(4):
                exchange_grads(grads.at[m, :, cols(i)], m, i)

        def gate_back(j):
            dz = by_rows(grads[m], w_d[cols(j), :])
            factors[m, :, cols(j)] = to_low(dz * to_f32(factors[m, :, cols(j)]))
            factors[m, :, cols(j, BLOCK, FF)] = to_low(dz * to_f32(factors[m, :, cols(j, BLOCK, FF)]))

        for i in range(FF // BLOCK):
            gate_back(i)
        start_blocks(1, m)
        if m == 0:
            for i in range(11):
                block = factors.at[m, :, cols((1 - half) * 11 + i)]
                sent.append(exchange(block, dgu_p.at[i], 22 + i))

        def gate_up_back(n):
            wide[:, cols(n)] = by_rows(factors[m], w_gu[cols(n), :])

        for i in range(4):
            gate_up_back(i)
        result, column = norm_back(wide[...], resid[m], gain_f[...], to_f32(grads[m]))
        dh[...] = result
        f_low[m] = to_low(result)
        gains[1:2, :] = column if m == 0 else gains[1:2, :] + column
        start_blocks(2, m)

        def out_back(n):
            d_att[:, cols(n)] = to_low(by_rows(f_low[m], w_o[cols(n), :]))

        for i in range(4):
            out_back(i)

        def rotate_back(part):
            return part * cosine[...] - pltpu.roll(part, HEAD_DIM // 2, 1) * sine[...]

        def head_back(h):
            at_q, at_k, at_v = (cols(h, HEAD_DIM, base) for base in (0, D, 2 * D))
            query, key, value = qkv[m, :, at_q], qkv[m, :, at_k], qkv[m, :, at_v]
            d_out = d_att[:, cols(h, HEAD_DIM)]
            p_local = probs[m, h, :, :SEG]
            p_remote = probs[m, h, :, SEG:]
            d_local = by_rows(d_out, value)
            d_remote = by_rows(d_out, picked_v[m, :, cols(h, HEAD_DIM)])
            wide_local, wide_remote = to_f32(p_local), to_f32(p_remote)
            centre = jnp.sum(wide_local * d_local, axis=-1, keepdims=True) + jnp.sum(
                wide_remote * d_remote, axis=-1, keepdims=True
            )
            d_local = to_low(wide_local * (d_local - centre))
            d_remote = to_low(wide_remote * (d_remote - centre))
            d_query = (times(d_local, key) + times(d_remote, picked_k[m, :, cols(h, HEAD_DIM)])) * scale
            d_key = by_tokens(d_local, query) * scale
            qkv[m, :, at_v] = to_low(by_tokens(p_local, d_out))
            qkv[m, :, at_q] = to_low(rotate_back(d_query))
            qkv[m, :, at_k] = to_low(rotate_back(d_key))

        for i in range(HEADS):
            head_back(i)
        start_blocks(3, m)

        def qkv_back(n):
            wide[:, cols(n)] = by_rows(qkv[m], w_qkv[cols(n), :])

        for i in range(4):
            qkv_back(i)
        result, column = norm_back(wide[...], to_f32(xs[m]), gain_a[...], dh[...])
        gx[m] = to_low(result)
        gains[0:1, :] = column if m == 0 else gains[0:1, :] + column

        @pl.when(is_upper)
        def _():
            send_down(m).start()

        write_out(gx.at[m], igrad.at[rows(m)], 1, m).start()

    gains[...] = jnp.zeros_like(gains)
    for m in range(MICRO):
        forward(m)
    for m in range(MICRO):
        backward(m)

    for m in range(MICRO):
        write_out(y_low.at[m], act.at[rows(m)], 0, m).wait()
        write_out(gx.at[m], igrad.at[rows(m)], 1, m).wait()
        for which in range(4):
            wait_blocks(which, m)
    for copy in sent:
        copy.wait()
    for m in range(MICRO):
        for i in range(4):
            pltpu.make_async_remote_copy(
                src_ref=grads.at[m, :, cols(i)], dst_ref=e_p.at[i, rows(m)],
                send_sem=sem_xsend.at[14 + m * 4 + i], recv_sem=sem_xrecv.at[14 + m * 4 + i],
                device_id=near, device_id_type=MESH,
            ).wait()

    @pl.when(is_lower)
    def _():
        for m in range(MICRO):
            send_up(m).wait_send()

    @pl.when(is_upper)
    def _():
        for m in range(MICRO):
            send_down(m).wait_send()


def rotary_constants():
    half = HEAD_DIM // 2
    freqs = np.exp(-np.log(10000.0) * np.arange(half) * 2.0 / HEAD_DIM)
    angles = np.arange(SEG)[:, None] * freqs[None, :]
    cosine = np.concatenate([np.cos(angles), np.cos(angles)], axis=1)
    sine = np.concatenate([-np.sin(angles), np.sin(angles)], axis=1)
    return cosine.astype(np.float32), sine.astype(np.float32)


def run_layers(tokens, cotangent, mem_keys, mem_values, index, flags, gain_a, gain_f, w_qkv, w_o, w_gu, w_d):
    cosine, sine = rotary_constants()
    count = tokens.shape[0]
    low, wide = jnp.bfloat16, jnp.float32
    anywhere = pl.BlockSpec(memory_space=pl.ANY)
    near_by = pl.BlockSpec(memory_space=pltpu.VMEM)
    shape = jax.ShapeDtypeStruct
    outs = (
        shape((count, D), low),
        shape((count, D), low),
        shape((count, D), low),
        shape((count, D), low),
        shape((count, D), low),
        shape((count, FF), low),
        shape((22, count, BLOCK), low),
        shape((12, count, BLOCK), low),
        shape((4, count, BLOCK), low),
        shape((4, count, BLOCK), low),
        shape((count, D), low),
        shape((count, D), low),
        shape((count, D), low),
        shape((2, count, 768), low),
        shape((11, SEG, BLOCK), low),
        shape((4, count, BLOCK), low),
        shape((8, D), wide),
    )
    scratch = [
        pltpu.VMEM((D, 3 * D), low),
        pltpu.VMEM((D, D), low),
        pltpu.VMEM((D, 2 * FF), low),
        pltpu.VMEM((FF, D), low),
        pltpu.VMEM((MICRO, SEG, D), low),
        pltpu.VMEM((MICRO, SEG, 3 * D), low),
        pltpu.VMEM((MICRO, HEADS, SEG, SEG + TOPM), low),
        pltpu.VMEM((MICRO, SEG, D), wide),
        pltpu.VMEM((MICRO, SEG, 2 * FF), low),
        pltpu.VMEM((MICRO, SEG, D), low),
        pltpu.VMEM((MICRO, TOPM, D), low),
        pltpu.VMEM((MICRO, TOPM, D), low),
        pltpu.VMEM((MICRO, 3, SEG, D), low),
        pltpu.VMEM((MICRO, SEG, FF), low),
        pltpu.VMEM((MICRO, SEG, D), low),
        pltpu.VMEM((SEG, D), wide),
        pltpu.VMEM((SEG, D), wide),
        pltpu.VMEM((MICRO, SEG, D), low),
        pltpu.VMEM((SEG, D), low),
        pltpu.VMEM((MICRO, SEG, D), low),
        pltpu.SemaphoreType.DMA((4, 4)),
        pltpu.SemaphoreType.DMA((2, MICRO)),
        pltpu.SemaphoreType.DMA((2, MICRO)),
        pltpu.SemaphoreType.DMA((4, MICRO)),
        pltpu.SemaphoreType.DMA((6, MICRO)),
        pltpu.SemaphoreType.DMA((2, MICRO)),
        pltpu.SemaphoreType.DMA((2, MICRO)),
        pltpu.SemaphoreType.DMA((33,)),
        pltpu.SemaphoreType.DMA((33,)),
    ]
    return pl.pallas_call(
        layer_kernel,
        out_shape=outs,
        in_specs=[anywhere] * 4
        + [near_by, pl.BlockSpec(memory_space=pltpu.SMEM)]
        + [near_by] * 4
        + [anywhere] * 4,
        out_specs=(anywhere,) * 16 + (near_by,),
        scratch_shapes=scratch,
        compiler_params=pltpu.CompilerParams(
            collective_id=1, has_side_effects=True, vmem_limit_bytes=60 * 2**20
        ),
        cost_estimate=pl.CostEstimate(flops=27 * 10**9, bytes_accessed=50 * 10**6, transcendentals=0),
        name="relay_layers",
    )(tokens, cotangent, mem_keys, mem_values, index, flags, cosine, sine, gain_a, gain_f, w_qkv, w_o, w_gu, w_d)


def finish_kernel(*refs):
    (sq, down, gains, act, igrad) = refs[:5]
    (gu_out, o_out, qkv_out, d_out, ga_out, gf_out, act_out, igrad_out) = refs[5:13]
    (sq_v, d_v, gu_v, o_v, qkv_v, down_v, pass_v, sem_in, sem_out) = refs[13:]
    parts = (
        (gu_v, gu_out, 0, 11),
        (qkv_v, qkv_out, 13, 6),
        (o_v, o_out, 11, 2),
    )
    loads = [
        pltpu.make_async_copy(
            sq.at[:, pl.ds(base, count)], sq_v.at[:, pl.ds(base, count)], sem_in.at[i]
        )
        for i, (_, _, base, count) in enumerate(parts)
    ]
    load_d = pltpu.make_async_copy(down, d_v, sem_in.at[3])
    passed = [
        (pltpu.make_async_copy(src, pass_v.at[i], sem_in.at[4 + i]), pltpu.make_async_copy(pass_v.at[i], dst, sem_out.at[8 + i]))
        for i, (src, dst) in enumerate(((act, act_out), (igrad, igrad_out)))
    ]
    for load, _ in passed:
        load.start()
    for copy in loads:
        copy.start()
    load_d.start()
    stores = []
    mine = cols(lax.axis_index("dp"))
    ga_out[...] = gains[0:1, mine]
    gf_out[...] = gains[1:2, mine]
    for i, (view, out, base, count) in enumerate(parts):
        loads[i].wait()
        for half in range(2):
            for c in range(count):
                at = pl.ds((half * count + c) * BLOCK, BLOCK)
                view[:, at] = sq_v[half, base + c].astype(jnp.float32)
            span = pl.ds(half * count * BLOCK, count * BLOCK)
            stores.append(pltpu.make_async_copy(view.at[:, span], out.at[:, span], sem_out.at[2 * i + half]))
            stores[-1].start()
    for load, store in passed:
        load.wait()
        store.start()
        stores.append(store)
    load_d.wait()
    for half in range(2):
        for k in range(4):
            down_v[pl.ds(half * 352, 352), pl.ds(k * BLOCK, BLOCK)] = d_v[half, k].astype(jnp.float32)
        span = pl.ds(half * 352, 352)
        stores.append(pltpu.make_async_copy(down_v.at[span], d_out.at[span], sem_out.at[6 + half]))
        stores[-1].start()
    for copy in stores:
        copy.wait()


def finish_gradients(out_sq, out_d, out_gains, act, igrad):
    anywhere = pl.BlockSpec(memory_space=pl.ANY)
    near_by = pl.BlockSpec(memory_space=pltpu.VMEM)
    shapes = ((256, 2 * FF), (256, D), (256, 3 * D), (704, D))
    wide = jnp.float32
    return pl.pallas_call(
        finish_kernel,
        out_shape=tuple(jax.ShapeDtypeStruct(shape, wide) for shape in shapes + ((1, BLOCK),) * 2)
        + (jax.ShapeDtypeStruct(act.shape, act.dtype),) * 2,
        in_specs=[anywhere] * 2 + [near_by] + [anywhere] * 2,
        out_specs=(anywhere,) * 4 + (near_by,) * 2 + (anywhere,) * 2,
        scratch_shapes=[pltpu.VMEM(out_sq.shape, jnp.bfloat16), pltpu.VMEM(out_d.shape, jnp.bfloat16)]
        + [pltpu.VMEM(shape, wide) for shape in shapes]
        + [pltpu.VMEM((2,) + act.shape, act.dtype)]
        + [pltpu.SemaphoreType.DMA((6,)), pltpu.SemaphoreType.DMA((10,))],
        compiler_params=pltpu.CompilerParams(vmem_limit_bytes=60 * 2**20),
        name="finish_gradients",
    )(out_sq, out_d, out_gains, act, igrad)


def body(
    group_size,
    tokens,
    cotangent,
    mem_keys,
    mem_values,
    mem_index,
    mem_flags,
    norm_attn,
    w_qkv,
    w_out,
    norm_ffn,
    w_gate_up,
    w_down,
):
    (act, igrad, na_all, nf_all, o_all, z_all, dgu, dm, f_cols, e_cols, na_p, nf_p, o_p, z_p, dgu_p, e_p, gains) = run_layers(
        tokens,
        cotangent,
        mem_keys,
        mem_values,
        mem_index,
        mem_flags,
        norm_attn,
        norm_ffn,
        w_qkv[0],
        w_out[0],
        w_gate_up[0],
        w_down[0],
    )
    reduced = reduce_gradients(
        group_size,
        (nf_all, na_all, o_all, z_all, dgu, dm, f_cols, e_cols, nf_p, na_p, o_p, z_p, dgu_p, e_p),
        gains,
    )
    (grad_gu, grad_o, grad_qkv, grad_d, grad_na, grad_nf, act, igrad) = finish_gradients(*reduced, act, igrad)
    return (
        act[None],
        igrad[None],
        grad_na,
        grad_qkv[None],
        grad_o[None],
        grad_nf,
        grad_gu[None],
        grad_d[None],
    )


def solution(mesh):
    placed = (
        P(("dp", "group"), None),
        P(("dp", "group"), None),
        P(("dp", "group"), None, None),
        P(("dp", "group"), None, None),
        P(("dp", "group"), None),
        P(("dp", "group")),
        P("section", None),
        P("section", None, None),
        P("section", None, None),
        P("section", None),
        P("section", None, None),
        P("section", None, None),
    )
    return jax.shard_map(
        functools.partial(body, mesh.shape["group"]),
        mesh=mesh,
        in_specs=placed,
        out_specs=(
            P("section", ("dp", "group"), None),
            P("section", ("dp", "group"), None),
            P("section", "dp"),
            P("section", "dp", None),
            P("section", "dp", None),
            P("section", "dp"),
            P("section", "dp", None),
            P("section", "dp", None),
        ),
        check_vma=False,
    )
```

```python
import functools

import jax
import jax.numpy as jnp
import numpy as np
from jax import lax
from jax.experimental import pallas as pl
from jax.experimental.pallas import tpu as pltpu
from jax.sharding import PartitionSpec as P

D = 1024
HEADS = 8
HEAD_DIM = 128
FF = 2816
SEG = 256
TOPM = 128
MICRO = 2
EPS = 1e-05
NEG = -1e30
MESH = pl.DeviceIdType.MESH
BLOCK = 256
LAGS = (0, 3, 6, 9, 13)


def flip(value, mask):
    return value + mask * (1 - 2 * ((value // mask) % 2))


def down_span(j, bit):
    return pl.ds(pl.multiple_of(1408 * j + 640 * bit, 128), 768)


def summed(left, right):
    return (left.astype(jnp.float32) + right.astype(jnp.float32)).astype(jnp.bfloat16)


def reduce_kernel(extra, *refs):
    n_extra = len(extra)
    (nf_all, na_all, o_all, z_all, dgu, dm, f_cols, e_cols, nf_p, na_p, o_p, z_p, dgu_p, e_p, gains) = refs[:15]
    (out_sq, out_d, out_gains) = refs[15:18]
    refs = refs[18:]
    (a_own, a_in, z_own, z_in, b_own, b_in, e_own, e_in) = refs[:8]
    (g_sq, q0, q1, q2, g_d, d0, d1, d2, gain_out, gain_in) = refs[8:18]
    refs = refs[18:]
    n0, n1 = refs[:2]
    refs = refs[2:]
    x_sq, x_d, spread = refs[:3]
    (sem_load, sem_bload, sem_bsend, sem_brecv) = refs[3:7]
    (sem_send, sem_recv, sem_copy, gain_send, gain_recv) = refs[7:12]

    section, dpi, group = (lax.axis_index(name) for name in ("section", "dp", "group"))
    mask1 = 1 + section
    mask2 = 2 - section
    half = (group // mask1) % 2
    low2 = (group // mask2) % 2
    bit0 = dpi % 2
    bit1 = (dpi // 2) % 2
    first = (section, dpi, flip(group, mask1))
    second = (section, dpi, flip(group, mask2))
    near = (section, flip(dpi, 1), group)
    far = (section, flip(dpi, 2), group)
    others = [(section, dpi, flip(group, mask)) for mask in extra]
    partners = [first, second, near, far] + others

    barrier = pltpu.get_barrier_semaphore()
    for partner in partners:
        pl.semaphore_signal(barrier, inc=1, device_id=partner, device_id_type=MESH)
    pl.semaphore_wait(barrier, len(partners))

    def remote(src, dst, send, recv, device):
        return pltpu.make_async_remote_copy(
            src_ref=src, dst_ref=dst, send_sem=send, recv_sem=recv, device_id=device, device_id_type=MESH
        )

    def load_a(slot):
        return (
            pltpu.make_async_copy((nf_all, o_all, na_all)[slot], a_own.at[slot], sem_load.at[0, slot]),
            pltpu.make_async_copy((nf_p, o_p, na_p)[slot], a_in.at[slot], sem_load.at[1, slot]),
        )

    def load_z():
        own = [
            pltpu.make_async_copy(z_all.at[:, down_span(j, bit0)], z_own.at[j], sem_load.at[0, 3 + j])
            for j in range(2)
        ]
        return own + [pltpu.make_async_copy(z_p, z_in, sem_load.at[1, 3])]

    def load_gu(i):
        return (
            pltpu.make_async_copy(dgu.at[half * 11 + i], b_own.at[i], sem_bload.at[0, i]),
            pltpu.make_async_copy(dgu_p.at[i], b_in.at[i, pl.ds(0, SEG)], sem_bload.at[1, i]),
        )

    def send_gu(i):
        later = pl.ds(SEG, SEG)
        return remote(
            dgu.at[(1 - half) * 11 + i, later], b_in.at[i, later], sem_bsend.at[i], sem_brecv.at[i], first
        )

    def load_e(k):
        return (
            pltpu.make_async_copy(e_cols.at[k], e_own.at[k], sem_bload.at[0, 19 + k]),
            pltpu.make_async_copy(e_p.at[k], e_in.at[k], sem_bload.at[1, 19 + k]),
        )

    def late(part, i):
        return f_cols.at[part * 2 + i] if i < 2 else dm.at[part * 6 + i - 2]

    def load_late(i):
        return pltpu.make_async_copy(late(half, i), b_own.at[11 + i], sem_bload.at[0, 11 + i])

    def send_late(i):
        return remote(late(1 - half, i), b_in.at[11 + i], sem_bsend.at[11 + i], sem_brecv.at[11 + i], first)

    def start(copies):
        for copy in copies:
            copy.start()

    def finish_copies(copies):
        for copy in copies:
            copy.wait()

    kinds = ((0, 0, 11), (1, 11, 2), (2, 13, 6))
    start(load_z())
    for i in range(3):
        send_gu(i).start()
    start(load_e(0))
    start(load_a(0))
    for i in range(11):
        start(load_gu(i))
        if i in (2, 5, 8):
            start(load_e(i // 3 + 1))
    start(load_a(1))
    start(load_a(2))
    for i in range(8):
        load_late(i).start()

    def send_more(t):
        @pl.when(t < 8)
        def _():
            send_gu(t + 3).start()

        for i in range(8):

            @pl.when(t == 8 + i)
            def _():
                send_late(i).start()

    class Square:
        base, rows = 4, 256
        partial, recv0, recv1, recv2, xs, out = g_sq, q0, q1, q2, x_sq, out_sq

    class Early:
        base, rows = 4, 256
        partial, recv0, recv1, recv2, xs, out = g_sq, n0, n1, q2, x_sq, out_sq

    class Down:
        base, rows = 0, 352
        partial, recv0, recv1, recv2, xs, out = g_d, d0, d1, d2, x_d, out_d

    def rows_at(cls, part):
        size = cls.rows // 2
        return pl.ds(pl.multiple_of(part * size, 16), size)

    def half_rows(part):
        return pl.ds(pl.multiple_of(part * 352, 16), 352)

    def hop(cls, c, i, src, dst, device):
        k = cls.base + c
        return remote(src, dst, sem_send.at[i, k], sem_recv.at[i, k], device)

    def hops(cls, c):
        both = pl.ds(0, 2)
        if cls is Down:
            return (
                lambda: hop(cls, c, 0, cls.partial.at[c, 1 - bit1], cls.recv0.at[c], far),
                lambda: hop(cls, c, 1, cls.recv0.at[c, half_rows(1 - half)], cls.recv1.at[c], first),
                lambda: hop(cls, c, 2, cls.recv1.at[c, rows_at(cls, 1 - low2)], cls.recv2.at[c], second),
            )
        if cls is Early:
            slot = c // 3
            return (
                lambda: hop(cls, c, 0, cls.partial.at[c, both, 1 - bit0], cls.recv0.at[slot], near),
                lambda: hop(cls, c, 1, cls.recv0.at[slot, 1 - bit1], cls.recv1.at[slot], far),
                lambda: hop(cls, c, 2, cls.recv1.at[slot, rows_at(cls, 1 - low2)], cls.recv2.at[c], second),
            )
        return (
            lambda: hop(cls, c, 0, cls.partial.at[c, both, both, rows_at(cls, 1 - low2)], cls.recv0.at[c], second),
            lambda: hop(cls, c, 1, cls.recv0.at[c, both, 1 - bit0], cls.recv1.at[c], near),
            lambda: hop(cls, c, 2, cls.recv1.at[c, 1 - bit1], cls.recv2.at[c], far),
        )

    def combine(cls, c, i):
        if cls is Down:
            if i == 0:
                cls.recv0[c] = summed(cls.partial[c, bit1], cls.recv0[c])
            elif i == 1:
                cls.recv1[c] = summed(cls.recv0[c, half_rows(half)], cls.recv1[c])
            else:
                cls.recv2[c] = summed(cls.recv1[c, rows_at(cls, low2)], cls.recv2[c])
        elif cls is Early:
            slot = c // 3
            if i == 0:
                for j in range(2):
                    cls.recv0[slot, j] = summed(cls.partial[c, j, bit0], cls.recv0[slot, j])
            elif i == 1:
                cls.recv1[slot] = summed(cls.recv0[slot, bit1], cls.recv1[slot])
            else:
                cls.recv2[c] = summed(cls.recv1[slot, rows_at(cls, low2)], cls.recv2[c])
        elif i == 0:
            for j in range(4):
                cls.recv0[c, j // 2, j % 2] = summed(
                    cls.partial[c, j // 2, j % 2, rows_at(cls, low2)], cls.recv0[c, j // 2, j % 2]
                )
        elif i == 1:
            for j in range(2):
                cls.recv1[c, j] = summed(cls.recv0[c, j, bit0], cls.recv1[c, j])
        else:
            cls.recv2[c] = summed(cls.recv1[c, bit1], cls.recv2[c])

    def to_extra(cls, c, i):
        k = cls.base + c
        src = cls.recv2.at[c] if i == 0 else cls.xs.at[i - 1, c]
        return remote(src, cls.xs.at[i, c], sem_send.at[6 + i, k], sem_recv.at[6 + i, k], others[i])

    def final(cls, c):
        return cls.recv2.at[c] if n_extra == 0 else cls.xs.at[n_extra - 1, c]

    def share_second(cls, c):
        k = cls.base + c
        return remote(final(cls, c), cls.out.at[half, c, rows_at(cls, low2)], sem_send.at[3, k], sem_recv.at[3, k], second)

    def share_first(cls, c):
        k = cls.base + c
        return remote(final(cls, c), cls.out.at[half, c, rows_at(cls, low2)], sem_send.at[4, k], sem_recv.at[4, k], first)

    def pass_on(cls, c):
        k = cls.base + c
        block = cls.out.at[half, c, rows_at(cls, 1 - low2)]
        return remote(block, block, sem_send.at[5, k], sem_recv.at[5, k], first)

    def keep(cls, c):
        return pltpu.make_async_copy(final(cls, c), cls.out.at[half, c, rows_at(cls, low2)], sem_copy.at[cls.base + c])

    def multiply(left, right, left2, right2):
        return (by_tokens(left, right) + by_tokens(left2, right2)).astype(jnp.bfloat16)

    def partial_square(c):
        for kind, base, count in kinds:

            @pl.when(c == base)
            def _():
                finish_copies(load_a(kind))

        @pl.when(c < 11)
        def _():
            finish_copies(load_gu(c))
            send_gu(c).wait_recv()

        for i in range(8):

            @pl.when(c == 11 + i)
            def _():
                load_late(i).wait()
                send_late(i).wait_recv()

        for kind, base, count in kinds:

            @pl.when((c >= base) & (c < base + count))
            def _():
                for j in range(4):
                    rows = pl.ds(j * 256, 256)
                    g_sq[c, j // 2, j % 2] = multiply(
                        a_own[kind, :, rows], b_own[c], a_in[kind, :, rows], b_in[c]
                    )

        @pl.when(c % 3 == 2)
        def _():
            hops(Early, c)[0]().start()

        @pl.when(c % 3 != 2)
        def _():
            hops(Square, c)[0]().start()

    def partial_down(c):
        @pl.when(c == 0)
        def _():
            finish_copies(load_z())

        finish_copies(load_e(c))
        for j in range(2):
            spread[...] = multiply(z_own[j], e_own[c], z_in[j], e_in[c])
            g_d[c, j] = spread[pl.ds(pl.multiple_of(64 * bit0, 16), 704), :]
        hops(Down, c)[0]().start()

    def share(cls, c):
        share_second(cls, c).start()
        share_first(cls, c).start()
        keep(cls, c).start()

    def stage_hop(i, cls, c):
        hops(cls, c)[i]().wait_recv()
        combine(cls, c, i)
        if i < 2:
            hops(cls, c)[i + 1]().start()
        elif n_extra:
            to_extra(cls, c, 0).start()
        else:
            share(cls, c)

    def stage_extra(cls, c, i):
        to_extra(cls, c, i).wait()
        mine = cls.recv2[c] if i == 0 else cls.xs[i - 1, c]
        cls.xs[i, c] = summed(mine, cls.xs[i, c])
        if i + 1 < n_extra:
            to_extra(cls, c, i + 1).start()
        else:
            share(cls, c)

    def stage_pass(cls, c):
        share_second(cls, c).wait_recv()
        pass_on(cls, c).start()

    def partial(cls, c):
        if cls is Down:
            partial_down(c)
        else:
            partial_square(c)

    def by_order(stage, c):
        if stage is partial:
            stage(Square, c)
            return

        @pl.when(c % 3 == 2)
        def _():
            stage(Early, c)

        @pl.when(c % 3 != 2)
        def _():
            stage(Square, c)

    stages = [partial] + [functools.partial(stage_hop, i) for i in range(3)]
    stages += [functools.partial(lambda i, cls, c: stage_extra(cls, c, i), i) for i in range(n_extra)]

    stages += [stage_pass]

    def gain_exchange(i):
        return remote(gain_out.at[i], gain_in.at[i], gain_send.at[i], gain_recv.at[i], partners[i])

    lags = LAGS[:4] + tuple(LAGS[3] + 2 * (i + 1) for i in range(n_extra)) + (LAGS[4] + 2 * n_extra,)
    steps = 23 + lags[-1]

    @pl.loop(0, steps)
    def _(t):
        send_more(t)
        for i, stage in enumerate(stages):
            c = t - lags[i]
            turn = c // 5

            @pl.when((c >= 0) & (c < 20))
            def _():
                @pl.when(c % 5 == 0)
                def _():
                    stage(Down, turn)

                @pl.when(c % 5 != 0)
                def _():
                    by_order(stage, c - 1 - turn)

            @pl.when((c >= 20) & (c < 23))
            def _():
                by_order(stage, c - 4)

        for i in range(len(partners)):

            @pl.when(t == 3 * i + 2)
            def _():
                if i == 0:
                    gain_out[0] = gains[...]
                else:
                    gain_exchange(i - 1).wait()
                    gain_out[i] = gain_out[i - 1] + gain_in[i - 1]
                gain_exchange(i).start()

    last = len(partners) - 1
    gain_exchange(last).wait()
    out_gains[...] = gain_out[last] + gain_in[last]

    for i in range(8):
        send_late(i).wait_send()
    for i in range(11):
        send_gu(i).wait_send()

    def finish(cls, c):
        for make in hops(cls, c):
            make().wait_send()
        share_second(cls, c).wait_send()
        share_first(cls, c).wait()
        pass_on(cls, c).wait()
        keep(cls, c).wait()

    @pl.loop(0, 4)
    def _(c):
        finish(Down, c)

    @pl.loop(0, 19)
    def _(c):
        @pl.when(c % 3 == 2)
        def _():
            finish(Early, c)

        @pl.when(c % 3 != 2)
        def _():
            finish(Square, c)


def reduce_gradients(group_size, activations, gains):
    extra = []
    mask = 4
    while mask < group_size:
        extra.append(mask)
        mask *= 2
    n_extra = len(extra)
    low = jnp.bfloat16
    tokens = activations[0].shape[0]
    scratch = [
        pltpu.VMEM((3, tokens, D), low),
        pltpu.VMEM((3, tokens, D), low),
        pltpu.VMEM((2, tokens, 768), low),
        pltpu.VMEM((2, tokens, 768), low),
        pltpu.VMEM((19, tokens, BLOCK), low),
        pltpu.VMEM((19, tokens, BLOCK), low),
        pltpu.VMEM((4, tokens, BLOCK), low),
        pltpu.VMEM((4, tokens, BLOCK), low),
        pltpu.VMEM((19, 2, 2, 256, BLOCK), low),
        pltpu.VMEM((19, 2, 2, 128, BLOCK), low),
        pltpu.VMEM((19, 2, 128, BLOCK), low),
        pltpu.VMEM((19, 128, BLOCK), low),
        pltpu.VMEM((4, 2, 704, BLOCK), low),
        pltpu.VMEM((4, 704, BLOCK), low),
        pltpu.VMEM((4, 352, BLOCK), low),
        pltpu.VMEM((4, 176, BLOCK), low),
        pltpu.VMEM((4 + n_extra, 8, D), jnp.float32),
        pltpu.VMEM((4 + n_extra, 8, D), jnp.float32),
        pltpu.VMEM((6, 2, 256, BLOCK), low),
        pltpu.VMEM((6, 256, BLOCK), low),
        pltpu.VMEM((max(n_extra, 1), 19 if n_extra else 1, 128, BLOCK), low),
        pltpu.VMEM((max(n_extra, 1), 4 if n_extra else 1, 176, BLOCK), low),
        pltpu.VMEM((768, BLOCK), low),
        pltpu.SemaphoreType.DMA((2, 5)),
        pltpu.SemaphoreType.DMA((2, 23)),
        pltpu.SemaphoreType.DMA((19,)),
        pltpu.SemaphoreType.DMA((19,)),
        pltpu.SemaphoreType.DMA((6 + n_extra, 23)),
        pltpu.SemaphoreType.DMA((6 + n_extra, 23)),
        pltpu.SemaphoreType.DMA((23,)),
        pltpu.SemaphoreType.DMA((4 + n_extra,)),
        pltpu.SemaphoreType.DMA((4 + n_extra,)),
    ]
    anywhere = pl.BlockSpec(memory_space=pl.ANY)
    near_by = pl.BlockSpec(memory_space=pltpu.VMEM)
    return pl.pallas_call(
        functools.partial(reduce_kernel, tuple(extra)),
        out_shape=(
            jax.ShapeDtypeStruct((2, 19, 256, BLOCK), low),
            jax.ShapeDtypeStruct((2, 4, 352, BLOCK), low),
            jax.ShapeDtypeStruct((8, D), jnp.float32),
        ),
        in_specs=[anywhere] * 14 + [near_by],
        out_specs=(anywhere, anywhere, near_by),
        scratch_shapes=scratch,
        compiler_params=pltpu.CompilerParams(
            collective_id=0, has_side_effects=True, vmem_limit_bytes=58 * 2**20
        ),
        cost_estimate=pl.CostEstimate(flops=13 * 10**9, bytes_accessed=30 * 10**6, transcendentals=0),
        name="reduce_gradients",
    )(*activations, gains)


def to_f32(value):
    return value.astype(jnp.float32)


def to_low(value):
    return value.astype(jnp.bfloat16)


def by_rows(left, right):
    return lax.dot_general(left, right, (((1,), (1,)), ((), ())), preferred_element_type=jnp.float32)


def by_tokens(left, right):
    return lax.dot_general(left, right, (((0,), (0,)), ((), ())), preferred_element_type=jnp.float32)


def times(left, right):
    return jnp.dot(left, right, preferred_element_type=jnp.float32)


def cols(index, size=BLOCK, base=0):
    if isinstance(index, int):
        return pl.ds(base + index * size, size)
    return pl.ds(pl.multiple_of(base + index * size, 128), size)


def inverse_rms(values):
    return lax.rsqrt(jnp.mean(values * values, axis=-1, keepdims=True) + EPS)


def layer_kernel(*refs):
    (tokens, cotangent, mem_k, mem_v, index, flags, cosine, sine, gain_a, gain_f) = refs[:10]
    (w_qkv_hbm, w_o_hbm, w_gu_hbm, w_d_hbm) = refs[10:14]
    (act, igrad, na_all, nf_all, o_all, z_all, dgu, dm, f_cols, e_cols) = refs[14:24]
    (na_p, nf_p, o_p, z_p, dgu_p, e_p, gains) = refs[24:31]
    refs = refs[31:]
    (w_qkv, w_o, w_gu, w_d, xs, qkv, probs, resid, factors, grads, picked_k, picked_v) = refs[:12]
    (kept, hidden, y_low, wide, dh, f_low, d_att, gx) = refs[12:20]
    (sem_w, sem_in, sem_mem, sem_t, sem_out, sem_send, sem_recv, sem_xsend, sem_xrecv) = refs[20:29]

    section, dpi, group = (lax.axis_index(name) for name in ("section", "dp", "group"))
    mask1 = 1 + section
    half = (group // mask1) % 2
    bit0 = dpi % 2
    twin = (1 - section, dpi, group)
    first = (section, dpi, flip(group, mask1))
    near = (section, flip(dpi, 1), group)
    is_lower = section == 0
    is_upper = section == 1
    scale = HEAD_DIM ** (-0.5)

    weights = []
    for i, (src, dst, pieces) in enumerate(
        ((w_qkv_hbm, w_qkv, 4), (w_o_hbm, w_o, 1), (w_gu_hbm, w_gu, 4), (w_d_hbm, w_d, 2))
    ):
        size = src.shape[0] // pieces
        weights.append(
            [
                pltpu.make_async_copy(src.at[pl.ds(p * size, size)], dst.at[pl.ds(p * size, size)], sem_w.at[i, p])
                for p in range(pieces)
            ]
        )

    def rows(m):
        return pl.ds(m * SEG, SEG)

    def load_tokens(m):
        return pltpu.make_async_copy(tokens.at[rows(m)], xs.at[m], sem_in.at[0, m])

    def load_cotangent(m):
        return pltpu.make_async_copy(cotangent.at[rows(m)], grads.at[m], sem_in.at[1, m])

    def send_up(m):
        return pltpu.make_async_remote_copy(
            src_ref=y_low.at[m], dst_ref=xs.at[m], send_sem=sem_send.at[0, m], recv_sem=sem_recv.at[0, m],
            device_id=twin, device_id_type=MESH,
        )

    def send_down(m):
        return pltpu.make_async_remote_copy(
            src_ref=gx.at[m], dst_ref=grads.at[m], send_sem=sem_send.at[1, m], recv_sem=sem_recv.at[1, m],
            device_id=twin, device_id_type=MESH,
        )

    @pl.when(is_lower)
    def _():
        load_tokens(0).start()

    for copy in weights[0]:
        copy.start()

    @pl.when(is_lower)
    def _():
        load_tokens(1).start()

    memory_in = [
        pltpu.make_async_copy(src.at[m], factors.at[m, :, cols(i, D)], sem_mem.at[i, m])
        for m in range(MICRO)
        for i, src in enumerate((mem_k, mem_v))
    ]

    @pl.when(is_upper)
    def _():
        for copy in memory_in:
            copy.start()
        for m in range(MICRO):
            load_cotangent(m).start()

    for group_copies in weights[1:]:
        for copy in group_copies:
            copy.start()

    barrier = pltpu.get_barrier_semaphore()
    pl.semaphore_signal(barrier, inc=1, device_id=twin, device_id_type=MESH)
    pl.semaphore_signal(barrier, inc=1, device_id=first, device_id_type=MESH)
    pl.semaphore_signal(barrier, inc=1, device_id=near, device_id_type=MESH)
    pl.semaphore_wait(barrier, 3)

    @pl.when(is_lower)
    def _():
        picked_k[...] = jnp.zeros_like(picked_k)
        picked_v[...] = jnp.zeros_like(picked_v)

    @pl.when(is_upper)
    def _():
        for copy in memory_in:
            copy.wait()
        places = lax.broadcasted_iota(jnp.int32, (SEG, TOPM), 0)
        for m in range(MICRO):
            chosen = to_low(to_f32(index[m : m + 1, :] == places).T)
            for n in range(4):
                picked_k[m, :, cols(n)] = to_low(times(chosen, factors[m, :, cols(n)]))
                picked_v[m, :, cols(n)] = to_low(times(chosen, factors[m, :, cols(n, BLOCK, D)]))

    sent = []

    def exchange(src, dst, at, device=first):
        copy = pltpu.make_async_remote_copy(
            src_ref=src, dst_ref=dst, send_sem=sem_xsend.at[at], recv_sem=sem_xrecv.at[at],
            device_id=device, device_id_type=MESH,
        )
        copy.start()
        return copy

    def exchange_grads(src, m, i):
        return exchange(src, e_p.at[i, rows(m)], 14 + m * 4 + i, near)

    @pl.when(is_upper)
    def _():
        for m in range(MICRO):
            for i in range(4):
                exchange_grads(cotangent.at[rows(m), cols(i)], m, i)

    def local(src, dst, sem):
        copy = pltpu.make_async_copy(src, dst, sem)
        copy.start()
        sent.append(copy)

    def share_kept(kind, out, partner_out, m):
        view = kept.at[m, kind]
        local(view, out.at[rows(m)], sem_t.at[kind, m])
        sent.append(exchange(view, partner_out.at[rows(m)], kind * MICRO + m))

    def forward(m):
        @pl.when(is_lower)
        def _():
            load_tokens(m).wait()

        @pl.when(is_upper)
        def _():
            send_up(m).wait_recv()

        x = to_f32(xs[m])
        normed = kept.at[m, 0]
        normed[...] = to_low(x * inverse_rms(x) * to_f32(gain_a[...]))
        if m == 0:
            for copy in weights[0]:
                copy.wait()

        def rotated(j):
            block = times(normed[...], w_qkv[:, cols(j)])
            for p in range(2):
                part = block[:, p * HEAD_DIM : (p + 1) * HEAD_DIM]
                part = part * cosine[...] + pltpu.roll(part, HEAD_DIM // 2, 1) * sine[...]
                qkv[m, :, cols(2 * j + p, HEAD_DIM)] = to_low(part)

        for i in range(8):
            rotated(i)

        def plain(j):
            qkv[m, :, cols(j, BLOCK, 2 * D)] = to_low(times(normed[...], w_qkv[:, cols(j, BLOCK, 2 * D)]))

        for i in range(4):
            plain(i)
        share_kept(0, na_all, na_p, m)
        attended = kept.at[m, 1]
        steep = scale * 1.4426950408889634
        ones = jnp.ones((SEG, HEAD_DIM), jnp.bfloat16)
        bias = (1 - flags[m] * section).astype(jnp.float32) * NEG
        causal = lax.broadcasted_iota(jnp.int32, (SEG, SEG), 0) >= lax.broadcasted_iota(jnp.int32, (SEG, SEG), 1)

        def head(h):
            query = qkv[m, :, cols(h, HEAD_DIM)]
            local = by_rows(query, qkv[m, :, cols(h, HEAD_DIM, D)])
            local = jnp.where(causal, local, NEG)
            remote = by_rows(query, picked_k[m, :, cols(h, HEAD_DIM)]) + bias
            peak = jnp.maximum(
                jnp.max(local, axis=-1, keepdims=True), jnp.max(remote, axis=-1, keepdims=True)
            )
            local = jnp.exp2((local - peak) * steep)
            remote = jnp.exp2((remote - peak) * steep)
            value = jnp.concatenate([qkv[m, :, cols(h, HEAD_DIM, 2 * D)], ones], axis=1)
            value_m = jnp.concatenate([picked_v[m, :, cols(h, HEAD_DIM)], ones[:TOPM]], axis=1)
            result = times(to_low(local), value) + times(to_low(remote), value_m)
            share = 1.0 / result[:, HEAD_DIM:]
            attended[:, cols(h, HEAD_DIM)] = to_low(result[:, :HEAD_DIM] * share)
            probs[m, h, :, :HEAD_DIM] = to_low(local[:, :HEAD_DIM] * share)
            probs[m, h, :, HEAD_DIM:SEG] = to_low(local[:, HEAD_DIM:] * share)
            probs[m, h, :, SEG:] = to_low(remote * share)

        for i in range(HEADS):
            head(i)
        if m == 0:
            weights[1][0].wait()

        def project(n):
            resid[m, :, cols(n)] = to_f32(xs[m, :, cols(n)]) + times(attended[...], w_o[:, cols(n)])

        for i in range(4):
            project(i)
        share_kept(1, o_all, o_p, m)
        normed_ffn = kept.at[m, 2]
        h = resid[m]
        normed_ffn[...] = to_low(h * inverse_rms(h) * to_f32(gain_f[...]))
        if m == 0:
            for copy in weights[2]:
                copy.wait()

        def gate(j):
            a = times(normed_ffn[...], w_gu[:, cols(j)])
            u = times(normed_ffn[...], w_gu[:, cols(j, BLOCK, FF)])
            sg = jax.nn.sigmoid(a)
            silu = a * sg
            hidden[m, :, cols(j)] = to_low(silu * u)
            factors[m, :, cols(j)] = to_low(u * sg * (1.0 + a * (1.0 - sg)))
            factors[m, :, cols(j, BLOCK, FF)] = to_low(silu)

        for i in range(FF // BLOCK):
            gate(i)
        if m == 0:
            for copy in weights[3]:
                copy.wait()

        def down(n):
            y_low[m, :, cols(n)] = to_low(resid[m, :, cols(n)] + times(hidden[m], w_d[:, cols(n)]))

        for i in range(4):
            down(i)

        @pl.when(is_lower)
        def _():
            send_up(m).start()

        write_out(y_low.at[m], act.at[rows(m)], 0, m).start()
        share_kept(2, nf_all, nf_p, m)
        local(hidden.at[m], z_all.at[rows(m)], sem_t.at[3, m])
        for j in range(2):
            span = hidden.at[m, :, down_span(j, 1 - bit0)]
            sent.append(exchange(span, z_p.at[j, rows(m)], 3 * MICRO + 2 * m + j, near))

    def write_out(src, dst, kind, m):
        return pltpu.make_async_copy(src, dst, sem_out.at[kind, m])

    def block_out(src, dst, kind, m, i):
        return write_out(src.at[m, :, cols(i)], dst.at[i, rows(m)], kind, m)

    block_sets = ((grads, e_cols, 2, 4), (factors, dgu, 3, 22), (f_low, f_cols, 4, 4), (qkv, dm, 5, 12))

    def start_blocks(which, m):
        src, dst, kind, count = block_sets[which]
        for i in range(count):
            block_out(src, dst, kind, m, i).start()

    def wait_blocks(which, m):
        src, dst, kind, count = block_sets[which]
        whole = dst.at[:, rows(m)]
        pltpu.make_async_copy(whole, whole, sem_out.at[kind, m]).wait()

    def norm_back(d_normed, values, gain, incoming):
        inverse = inverse_rms(values)
        scaled = d_normed * to_f32(gain)
        column = jnp.sum(d_normed * (values * inverse), axis=0, keepdims=True)
        centre = jnp.mean(scaled * values, axis=-1, keepdims=True)
        return incoming + inverse * scaled - values * (inverse * inverse * inverse * centre), column

    def backward(m):
        @pl.when(is_upper)
        def _():
            load_cotangent(m).wait()

        @pl.when(is_lower)
        def _():
            send_down(m).wait_recv()

        start_blocks(0, m)

        @pl.when(is_lower)
        def _():
            for i in range(4):
                exchange_grads(grads.at[m, :, cols(i)], m, i)

        def gate_back(j):
            dz = by_rows(grads[m], w_d[cols(j), :])
            factors[m, :, cols(j)] = to_low(dz * to_f32(factors[m, :, cols(j)]))
            factors[m, :, cols(j, BLOCK, FF)] = to_low(dz * to_f32(factors[m, :, cols(j, BLOCK, FF)]))

        for i in range(FF // BLOCK):
            gate_back(i)
        start_blocks(1, m)
        if m == 0:
            for i in range(11):
                block = factors.at[m, :, cols((1 - half) * 11 + i)]
                sent.append(exchange(block, dgu_p.at[i], 22 + i))

        def gate_up_back(n):
            wide[:, cols(n)] = by_rows(factors[m], w_gu[cols(n), :])

        for i in range(4):
            gate_up_back(i)
        result, column = norm_back(wide[...], resid[m], gain_f[...], to_f32(grads[m]))
        dh[...] = result
        f_low[m] = to_low(result)
        gains[1:2, :] = column if m == 0 else gains[1:2, :] + column
        start_blocks(2, m)

        def out_back(n):
            d_att[:, cols(n)] = to_low(by_rows(f_low[m], w_o[cols(n), :]))

        for i in range(4):
            out_back(i)

        def rotate_back(part):
            return part * cosine[...] - pltpu.roll(part, HEAD_DIM // 2, 1) * sine[...]

        def head_back(h):
            at_q, at_k, at_v = (cols(h, HEAD_DIM, base) for base in (0, D, 2 * D))
            query, key, value = qkv[m, :, at_q], qkv[m, :, at_k], qkv[m, :, at_v]
            d_out = d_att[:, cols(h, HEAD_DIM)]
            p_local = probs[m, h, :, :SEG]
            p_remote = probs[m, h, :, SEG:]
            d_local = by_rows(d_out, value)
            d_remote = by_rows(d_out, picked_v[m, :, cols(h, HEAD_DIM)])
            wide_local, wide_remote = to_f32(p_local), to_f32(p_remote)
            centre = jnp.sum(to_f32(d_out) * to_f32(kept[m, 1, :, cols(h, HEAD_DIM)]), axis=-1, keepdims=True)
            d_local = to_low(wide_local * (d_local - centre))
            d_remote = to_low(wide_remote * (d_remote - centre))
            d_query = (times(d_local, key) + times(d_remote, picked_k[m, :, cols(h, HEAD_DIM)])) * scale
            d_key = by_tokens(d_local, query) * scale
            qkv[m, :, at_v] = to_low(by_tokens(p_local, d_out))
            qkv[m, :, at_q] = to_low(rotate_back(d_query))
            qkv[m, :, at_k] = to_low(rotate_back(d_key))

        for i in range(HEADS):
            head_back(i)
        start_blocks(3, m)

        def qkv_back(n):
            wide[:, cols(n)] = by_rows(qkv[m], w_qkv[cols(n), :])

        for i in range(4):
            qkv_back(i)
        result, column = norm_back(wide[...], to_f32(xs[m]), gain_a[...], dh[...])
        gx[m] = to_low(result)
        gains[0:1, :] = column if m == 0 else gains[0:1, :] + column

        @pl.when(is_upper)
        def _():
            send_down(m).start()

        write_out(gx.at[m], igrad.at[rows(m)], 1, m).start()

    gains[...] = jnp.zeros_like(gains)
    for m in range(MICRO):
        forward(m)
    for m in range(MICRO):
        backward(m)

    for m in range(MICRO):
        write_out(y_low.at[m], act.at[rows(m)], 0, m).wait()
        write_out(gx.at[m], igrad.at[rows(m)], 1, m).wait()
        for which in range(4):
            wait_blocks(which, m)
    for copy in sent:
        copy.wait()
    for m in range(MICRO):
        for i in range(4):
            pltpu.make_async_remote_copy(
                src_ref=grads.at[m, :, cols(i)], dst_ref=e_p.at[i, rows(m)],
                send_sem=sem_xsend.at[14 + m * 4 + i], recv_sem=sem_xrecv.at[14 + m * 4 + i],
                device_id=near, device_id_type=MESH,
            ).wait()

    @pl.when(is_lower)
    def _():
        for m in range(MICRO):
            send_up(m).wait_send()

    @pl.when(is_upper)
    def _():
        for m in range(MICRO):
            send_down(m).wait_send()


def rotary_constants():
    half = HEAD_DIM // 2
    freqs = np.exp(-np.log(10000.0) * np.arange(half) * 2.0 / HEAD_DIM)
    angles = np.arange(SEG)[:, None] * freqs[None, :]
    cosine = np.concatenate([np.cos(angles), np.cos(angles)], axis=1)
    sine = np.concatenate([-np.sin(angles), np.sin(angles)], axis=1)
    return cosine.astype(np.float32), sine.astype(np.float32)


def run_layers(tokens, cotangent, mem_keys, mem_values, index, flags, gain_a, gain_f, w_qkv, w_o, w_gu, w_d):
    cosine, sine = rotary_constants()
    count = tokens.shape[0]
    low, wide = jnp.bfloat16, jnp.float32
    anywhere = pl.BlockSpec(memory_space=pl.ANY)
    near_by = pl.BlockSpec(memory_space=pltpu.VMEM)
    shape = jax.ShapeDtypeStruct
    outs = (
        shape((count, D), low),
        shape((count, D), low),
        shape((count, D), low),
        shape((count, D), low),
        shape((count, D), low),
        shape((count, FF), low),
        shape((22, count, BLOCK), low),
        shape((12, count, BLOCK), low),
        shape((4, count, BLOCK), low),
        shape((4, count, BLOCK), low),
        shape((count, D), low),
        shape((count, D), low),
        shape((count, D), low),
        shape((2, count, 768), low),
        shape((11, SEG, BLOCK), low),
        shape((4, count, BLOCK), low),
        shape((8, D), wide),
    )
    scratch = [
        pltpu.VMEM((D, 3 * D), low),
        pltpu.VMEM((D, D), low),
        pltpu.VMEM((D, 2 * FF), low),
        pltpu.VMEM((FF, D), low),
        pltpu.VMEM((MICRO, SEG, D), low),
        pltpu.VMEM((MICRO, SEG, 3 * D), low),
        pltpu.VMEM((MICRO, HEADS, SEG, SEG + TOPM), low),
        pltpu.VMEM((MICRO, SEG, D), wide),
        pltpu.VMEM((MICRO, SEG, 2 * FF), low),
        pltpu.VMEM((MICRO, SEG, D), low),
        pltpu.VMEM((MICRO, TOPM, D), low),
        pltpu.VMEM((MICRO, TOPM, D), low),
        pltpu.VMEM((MICRO, 3, SEG, D), low),
        pltpu.VMEM((MICRO, SEG, FF), low),
        pltpu.VMEM((MICRO, SEG, D), low),
        pltpu.VMEM((SEG, D), wide),
        pltpu.VMEM((SEG, D), wide),
        pltpu.VMEM((MICRO, SEG, D), low),
        pltpu.VMEM((SEG, D), low),
        pltpu.VMEM((MICRO, SEG, D), low),
        pltpu.SemaphoreType.DMA((4, 4)),
        pltpu.SemaphoreType.DMA((2, MICRO)),
        pltpu.SemaphoreType.DMA((2, MICRO)),
        pltpu.SemaphoreType.DMA((4, MICRO)),
        pltpu.SemaphoreType.DMA((6, MICRO)),
        pltpu.SemaphoreType.DMA((2, MICRO)),
        pltpu.SemaphoreType.DMA((2, MICRO)),
        pltpu.SemaphoreType.DMA((33,)),
        pltpu.SemaphoreType.DMA((33,)),
    ]
    return pl.pallas_call(
        layer_kernel,
        out_shape=outs,
        in_specs=[anywhere] * 4
        + [near_by, pl.BlockSpec(memory_space=pltpu.SMEM)]
        + [near_by] * 4
        + [anywhere] * 4,
        out_specs=(anywhere,) * 16 + (near_by,),
        scratch_shapes=scratch,
        compiler_params=pltpu.CompilerParams(
            collective_id=1, has_side_effects=True, vmem_limit_bytes=60 * 2**20
        ),
        cost_estimate=pl.CostEstimate(flops=27 * 10**9, bytes_accessed=50 * 10**6, transcendentals=0),
        name="relay_layers",
    )(tokens, cotangent, mem_keys, mem_values, index, flags, cosine, sine, gain_a, gain_f, w_qkv, w_o, w_gu, w_d)


def finish_kernel(*refs):
    (sq, down, gains, act, igrad) = refs[:5]
    (gu_out, o_out, qkv_out, d_out, ga_out, gf_out, act_out, igrad_out) = refs[5:13]
    (sq_v, d_v, gu_v, o_v, qkv_v, down_v, pass_v, sem_in, sem_out) = refs[13:]
    parts = (
        (gu_v, gu_out, 0, 11),
        (qkv_v, qkv_out, 13, 6),
        (o_v, o_out, 11, 2),
    )
    loads = [
        [
            pltpu.make_async_copy(
                sq.at[half, pl.ds(base, count)], sq_v.at[half, pl.ds(base, count)], sem_in.at[2 * i + half]
            )
            for half in range(2)
        ]
        for i, (_, _, base, count) in enumerate(parts)
    ]
    load_d = pltpu.make_async_copy(down, d_v, sem_in.at[6])
    passed = [
        (pltpu.make_async_copy(src, pass_v.at[i], sem_in.at[7 + i]), pltpu.make_async_copy(pass_v.at[i], dst, sem_out.at[8 + i]))
        for i, (src, dst) in enumerate(((act, act_out), (igrad, igrad_out)))
    ]
    for pair in loads:
        for copy in pair:
            copy.start()
    load_d.start()
    for load, _ in passed:
        load.start()
    stores = []
    mine = cols(lax.axis_index("dp"))
    ga_out[...] = gains[0:1, mine]
    gf_out[...] = gains[1:2, mine]
    for i, (view, out, base, count) in enumerate(parts):
        for half in range(2):
            loads[i][half].wait()
            for c in range(count):
                at = pl.ds((half * count + c) * BLOCK, BLOCK)
                view[:, at] = sq_v[half, base + c].astype(jnp.float32)
            span = pl.ds(half * count * BLOCK, count * BLOCK)
            stores.append(pltpu.make_async_copy(view.at[:, span], out.at[:, span], sem_out.at[2 * i + half]))
            stores[-1].start()
    for load, store in passed:
        load.wait()
        store.start()
        stores.append(store)
    load_d.wait()
    for half in range(2):
        for k in range(4):
            down_v[pl.ds(half * 352, 352), pl.ds(k * BLOCK, BLOCK)] = d_v[half, k].astype(jnp.float32)
        span = pl.ds(half * 352, 352)
        stores.append(pltpu.make_async_copy(down_v.at[span], d_out.at[span], sem_out.at[6 + half]))
        stores[-1].start()
    for copy in stores:
        copy.wait()


def finish_gradients(out_sq, out_d, out_gains, act, igrad):
    anywhere = pl.BlockSpec(memory_space=pl.ANY)
    near_by = pl.BlockSpec(memory_space=pltpu.VMEM)
    shapes = ((256, 2 * FF), (256, D), (256, 3 * D), (704, D))
    wide = jnp.float32
    return pl.pallas_call(
        finish_kernel,
        out_shape=tuple(jax.ShapeDtypeStruct(shape, wide) for shape in shapes + ((1, BLOCK),) * 2)
        + (jax.ShapeDtypeStruct(act.shape, act.dtype),) * 2,
        in_specs=[anywhere] * 2 + [near_by] + [anywhere] * 2,
        out_specs=(anywhere,) * 4 + (near_by,) * 2 + (anywhere,) * 2,
        scratch_shapes=[pltpu.VMEM(out_sq.shape, jnp.bfloat16), pltpu.VMEM(out_d.shape, jnp.bfloat16)]
        + [pltpu.VMEM(shape, wide) for shape in shapes]
        + [pltpu.VMEM((2,) + act.shape, act.dtype)]
        + [pltpu.SemaphoreType.DMA((9,)), pltpu.SemaphoreType.DMA((10,))],
        compiler_params=pltpu.CompilerParams(vmem_limit_bytes=60 * 2**20),
        name="finish_gradients",
    )(out_sq, out_d, out_gains, act, igrad)


def body(
    group_size,
    tokens,
    cotangent,
    mem_keys,
    mem_values,
    mem_index,
    mem_flags,
    norm_attn,
    w_qkv,
    w_out,
    norm_ffn,
    w_gate_up,
    w_down,
):
    (act, igrad, na_all, nf_all, o_all, z_all, dgu, dm, f_cols, e_cols, na_p, nf_p, o_p, z_p, dgu_p, e_p, gains) = run_layers(
        tokens,
        cotangent,
        mem_keys,
        mem_values,
        mem_index,
        mem_flags,
        norm_attn,
        norm_ffn,
        w_qkv[0],
        w_out[0],
        w_gate_up[0],
        w_down[0],
    )
    reduced = reduce_gradients(
        group_size,
        (nf_all, na_all, o_all, z_all, dgu, dm, f_cols, e_cols, nf_p, na_p, o_p, z_p, dgu_p, e_p),
        gains,
    )
    (grad_gu, grad_o, grad_qkv, grad_d, grad_na, grad_nf, act, igrad) = finish_gradients(*reduced, act, igrad)
    return (
        act[None],
        igrad[None],
        grad_na,
        grad_qkv[None],
        grad_o[None],
        grad_nf,
        grad_gu[None],
        grad_d[None],
    )


def solution(mesh):
    placed = (
        P(("dp", "group"), None),
        P(("dp", "group"), None),
        P(("dp", "group"), None, None),
        P(("dp", "group"), None, None),
        P(("dp", "group"), None),
        P(("dp", "group")),
        P("section", None),
        P("section", None, None),
        P("section", None, None),
        P("section", None),
        P("section", None, None),
        P("section", None, None),
    )
    return jax.shard_map(
        functools.partial(body, mesh.shape["group"]),
        mesh=mesh,
        in_specs=placed,
        out_specs=(
            P("section", ("dp", "group"), None),
            P("section", ("dp", "group"), None),
            P("section", "dp"),
            P("section", "dp", None),
            P("section", "dp", None),
            P("section", "dp"),
            P("section", "dp", None),
            P("section", "dp", None),
        ),
        check_vma=False,
    )
```

```python
import functools

import jax
import jax.numpy as jnp
import numpy as np
from jax import lax
from jax.experimental import pallas as pl
from jax.experimental.pallas import tpu as pltpu
from jax.sharding import PartitionSpec as P

D = 1024
HEADS = 8
HEAD_DIM = 128
FF = 2816
SEG = 256
TOPM = 128
MICRO = 2
EPS = 1e-05
NEG = -1e30
MESH = pl.DeviceIdType.MESH
BLOCK = 256
LAGS = (0, 3, 6, 9, 13)


def flip(value, mask):
    return value + mask * (1 - 2 * ((value // mask) % 2))


def down_span(j, bit):
    return pl.ds(pl.multiple_of(1408 * j + 640 * bit, 128), 768)


def summed(left, right):
    return (left.astype(jnp.float32) + right.astype(jnp.float32)).astype(jnp.bfloat16)


def reduce_kernel(extra, *refs):
    n_extra = len(extra)
    (nf_all, na_all, o_all, z_all, dgu, dm, f_cols, e_cols, nf_p, na_p, o_p, z_p, dgu_p, e_p, gains) = refs[:15]
    (out_sq, out_d, out_gains) = refs[15:18]
    refs = refs[18:]
    (a_own, a_in, z_own, z_in, b_own, b_in, e_own, e_in) = refs[:8]
    (g_sq, q0, q1, q2, g_d, d0, d1, d2, gain_out, gain_in) = refs[8:18]
    refs = refs[18:]
    n0, n1 = refs[:2]
    refs = refs[2:]
    x_sq, x_d, spread = refs[:3]
    (sem_load, sem_bload, sem_bsend, sem_brecv) = refs[3:7]
    (sem_send, sem_recv, sem_copy, gain_send, gain_recv) = refs[7:12]

    section, dpi, group = (lax.axis_index(name) for name in ("section", "dp", "group"))
    mask1 = 1 + section
    mask2 = 2 - section
    half = (group // mask1) % 2
    low2 = (group // mask2) % 2
    bit0 = dpi % 2
    bit1 = (dpi // 2) % 2
    first = (section, dpi, flip(group, mask1))
    second = (section, dpi, flip(group, mask2))
    near = (section, flip(dpi, 1), group)
    far = (section, flip(dpi, 2), group)
    others = [(section, dpi, flip(group, mask)) for mask in extra]
    partners = [first, second, near, far] + others

    barrier = pltpu.get_barrier_semaphore()
    for partner in partners:
        pl.semaphore_signal(barrier, inc=1, device_id=partner, device_id_type=MESH)
    pl.semaphore_wait(barrier, len(partners))

    def remote(src, dst, send, recv, device):
        return pltpu.make_async_remote_copy(
            src_ref=src, dst_ref=dst, send_sem=send, recv_sem=recv, device_id=device, device_id_type=MESH
        )

    def load_a(slot):
        return (
            pltpu.make_async_copy((nf_all, o_all, na_all)[slot], a_own.at[slot], sem_load.at[0, slot]),
            pltpu.make_async_copy((nf_p, o_p, na_p)[slot], a_in.at[slot], sem_load.at[1, slot]),
        )

    def load_z():
        own = [
            pltpu.make_async_copy(z_all.at[:, down_span(j, bit0)], z_own.at[j], sem_load.at[0, 3 + j])
            for j in range(2)
        ]
        return own + [pltpu.make_async_copy(z_p, z_in, sem_load.at[1, 3])]

    def load_gu(i):
        return (
            pltpu.make_async_copy(dgu.at[half * 11 + i], b_own.at[i], sem_bload.at[0, i]),
            pltpu.make_async_copy(dgu_p.at[i], b_in.at[i, pl.ds(0, SEG)], sem_bload.at[1, i]),
        )

    def send_gu(i):
        later = pl.ds(SEG, SEG)
        return remote(
            dgu.at[(1 - half) * 11 + i, later], b_in.at[i, later], sem_bsend.at[i], sem_brecv.at[i], first
        )

    def load_e(k):
        return (
            pltpu.make_async_copy(e_cols.at[k], e_own.at[k], sem_bload.at[0, 19 + k]),
            pltpu.make_async_copy(e_p.at[k], e_in.at[k], sem_bload.at[1, 19 + k]),
        )

    def late(part, i):
        return f_cols.at[part * 2 + i] if i < 2 else dm.at[part * 6 + i - 2]

    def load_late(i):
        return pltpu.make_async_copy(late(half, i), b_own.at[11 + i], sem_bload.at[0, 11 + i])

    def send_late(i):
        return remote(late(1 - half, i), b_in.at[11 + i], sem_bsend.at[11 + i], sem_brecv.at[11 + i], first)

    def start(copies):
        for copy in copies:
            copy.start()

    def finish_copies(copies):
        for copy in copies:
            copy.wait()

    kinds = ((0, 0, 11), (1, 11, 2), (2, 13, 6))
    start(load_z())
    for i in range(3):
        send_gu(i).start()
    start(load_e(0))
    start(load_a(0))
    for i in range(11):
        start(load_gu(i))
        if i in (2, 5, 8):
            start(load_e(i // 3 + 1))
    start(load_a(1))
    start(load_a(2))
    for i in range(8):
        load_late(i).start()

    def send_more(t):
        @pl.when(t < 8)
        def _():
            send_gu(t + 3).start()

        for i in range(8):

            @pl.when(t == 8 + i)
            def _():
                send_late(i).start()

    class Square:
        base, rows = 4, 256
        partial, recv0, recv1, recv2, xs, out = g_sq, q0, q1, q2, x_sq, out_sq

    class Early:
        base, rows = 4, 256
        partial, recv0, recv1, recv2, xs, out = g_sq, n0, n1, q2, x_sq, out_sq

    class Down:
        base, rows = 0, 352
        partial, recv0, recv1, recv2, xs, out = g_d, d0, d1, d2, x_d, out_d

    def rows_at(cls, part):
        size = cls.rows // 2
        return pl.ds(pl.multiple_of(part * size, 16), size)

    def half_rows(part):
        return pl.ds(pl.multiple_of(part * 352, 16), 352)

    def hop(cls, c, i, src, dst, device):
        k = cls.base + c
        return remote(src, dst, sem_send.at[i, k], sem_recv.at[i, k], device)

    def hops(cls, c):
        both = pl.ds(0, 2)
        if cls is Down:
            return (
                lambda: hop(cls, c, 0, cls.partial.at[c, 1 - bit1], cls.recv0.at[c], far),
                lambda: hop(cls, c, 1, cls.recv0.at[c, half_rows(1 - half)], cls.recv1.at[c], first),
                lambda: hop(cls, c, 2, cls.recv1.at[c, rows_at(cls, 1 - low2)], cls.recv2.at[c], second),
            )
        if cls is Early:
            slot = c // 4
            return (
                lambda: hop(cls, c, 0, cls.partial.at[c, both, 1 - bit0], cls.recv0.at[slot], near),
                lambda: hop(cls, c, 1, cls.recv0.at[slot, 1 - bit1], cls.recv1.at[slot], far),
                lambda: hop(cls, c, 2, cls.recv1.at[slot, rows_at(cls, 1 - low2)], cls.recv2.at[c], second),
            )
        return (
            lambda: hop(cls, c, 0, cls.partial.at[c, both, both, rows_at(cls, 1 - low2)], cls.recv0.at[c], second),
            lambda: hop(cls, c, 1, cls.recv0.at[c, both, 1 - bit0], cls.recv1.at[c], near),
            lambda: hop(cls, c, 2, cls.recv1.at[c, 1 - bit1], cls.recv2.at[c], far),
        )

    def combine(cls, c, i):
        if cls is Down:
            if i == 0:
                cls.recv0[c] = summed(cls.partial[c, bit1], cls.recv0[c])
            elif i == 1:
                cls.recv1[c] = summed(cls.recv0[c, half_rows(half)], cls.recv1[c])
            else:
                cls.recv2[c] = summed(cls.recv1[c, rows_at(cls, low2)], cls.recv2[c])
        elif cls is Early:
            slot = c // 4
            if i == 0:
                for j in range(2):
                    cls.recv0[slot, j] = summed(cls.partial[c, j, bit0], cls.recv0[slot, j])
            elif i == 1:
                cls.recv1[slot] = summed(cls.recv0[slot, bit1], cls.recv1[slot])
            else:
                cls.recv2[c] = summed(cls.recv1[slot, rows_at(cls, low2)], cls.recv2[c])
        elif i == 0:
            for j in range(4):
                cls.recv0[c, j // 2, j % 2] = summed(
                    cls.partial[c, j // 2, j % 2, rows_at(cls, low2)], cls.recv0[c, j // 2, j % 2]
                )
        elif i == 1:
            for j in range(2):
                cls.recv1[c, j] = summed(cls.recv0[c, j, bit0], cls.recv1[c, j])
        else:
            cls.recv2[c] = summed(cls.recv1[c, bit1], cls.recv2[c])

    def to_extra(cls, c, i):
        k = cls.base + c
        src = cls.recv2.at[c] if i == 0 else cls.xs.at[i - 1, c]
        return remote(src, cls.xs.at[i, c], sem_send.at[6 + i, k], sem_recv.at[6 + i, k], others[i])

    def final(cls, c):
        return cls.recv2.at[c] if n_extra == 0 else cls.xs.at[n_extra - 1, c]

    def share_second(cls, c):
        k = cls.base + c
        return remote(final(cls, c), cls.out.at[half, c, rows_at(cls, low2)], sem_send.at[3, k], sem_recv.at[3, k], second)

    def share_first(cls, c):
        k = cls.base + c
        return remote(final(cls, c), cls.out.at[half, c, rows_at(cls, low2)], sem_send.at[4, k], sem_recv.at[4, k], first)

    def pass_on(cls, c):
        k = cls.base + c
        block = cls.out.at[half, c, rows_at(cls, 1 - low2)]
        return remote(block, block, sem_send.at[5, k], sem_recv.at[5, k], first)

    def keep(cls, c):
        return pltpu.make_async_copy(final(cls, c), cls.out.at[half, c, rows_at(cls, low2)], sem_copy.at[cls.base + c])

    def multiply(left, right, left2, right2):
        return (by_tokens(left, right) + by_tokens(left2, right2)).astype(jnp.bfloat16)

    def partial_square(c):
        for kind, base, count in kinds:

            @pl.when(c == base)
            def _():
                finish_copies(load_a(kind))

        @pl.when(c < 11)
        def _():
            finish_copies(load_gu(c))
            send_gu(c).wait_recv()

        for i in range(8):

            @pl.when(c == 11 + i)
            def _():
                load_late(i).wait()
                send_late(i).wait_recv()

        for kind, base, count in kinds:

            @pl.when((c >= base) & (c < base + count))
            def _():
                for j in range(4):
                    rows = pl.ds(j * 256, 256)
                    g_sq[c, j // 2, j % 2] = multiply(
                        a_own[kind, :, rows], b_own[c], a_in[kind, :, rows], b_in[c]
                    )

        @pl.when(c % 4 == 1)
        def _():
            hops(Early, c)[0]().start()

        @pl.when(c % 4 != 1)
        def _():
            hops(Square, c)[0]().start()

    def partial_down(c):
        @pl.when(c == 0)
        def _():
            finish_copies(load_z())

        finish_copies(load_e(c))
        for j in range(2):
            spread[...] = multiply(z_own[j], e_own[c], z_in[j], e_in[c])
            g_d[c, j] = spread[pl.ds(pl.multiple_of(64 * bit0, 16), 704), :]
        hops(Down, c)[0]().start()

    def share(cls, c):
        share_second(cls, c).start()
        share_first(cls, c).start()
        keep(cls, c).start()

    def stage_hop(i, cls, c):
        hops(cls, c)[i]().wait_recv()
        combine(cls, c, i)
        if i < 2:
            hops(cls, c)[i + 1]().start()
        elif n_extra:
            to_extra(cls, c, 0).start()
        else:
            share(cls, c)

    def stage_extra(cls, c, i):
        to_extra(cls, c, i).wait()
        mine = cls.recv2[c] if i == 0 else cls.xs[i - 1, c]
        cls.xs[i, c] = summed(mine, cls.xs[i, c])
        if i + 1 < n_extra:
            to_extra(cls, c, i + 1).start()
        else:
            share(cls, c)

    def stage_pass(cls, c):
        share_second(cls, c).wait_recv()
        pass_on(cls, c).start()

    def partial(cls, c):
        if cls is Down:
            partial_down(c)
        else:
            partial_square(c)

    def by_order(stage, c):
        if stage is partial:
            stage(Square, c)
            return

        @pl.when(c % 4 == 1)
        def _():
            stage(Early, c)

        @pl.when(c % 4 != 1)
        def _():
            stage(Square, c)

    stages = [partial] + [functools.partial(stage_hop, i) for i in range(3)]
    stages += [functools.partial(lambda i, cls, c: stage_extra(cls, c, i), i) for i in range(n_extra)]

    stages += [stage_pass]

    def gain_exchange(i):
        return remote(gain_out.at[i], gain_in.at[i], gain_send.at[i], gain_recv.at[i], partners[i])

    lags = LAGS[:4] + tuple(LAGS[3] + 2 * (i + 1) for i in range(n_extra)) + (LAGS[4] + 2 * n_extra,)
    steps = 23 + lags[-1]

    @pl.loop(0, steps)
    def _(t):
        send_more(t)
        for i, stage in enumerate(stages):
            c = t - lags[i]
            turn = c // 5

            @pl.when((c >= 0) & (c < 20))
            def _():
                @pl.when(c % 5 == 0)
                def _():
                    stage(Down, turn)

                @pl.when(c % 5 != 0)
                def _():
                    by_order(stage, c - 1 - turn)

            @pl.when((c >= 20) & (c < 23))
            def _():
                by_order(stage, c - 4)

        for i in range(len(partners)):

            @pl.when(t == 3 * i + 2)
            def _():
                if i == 0:
                    gain_out[0] = gains[...]
                else:
                    gain_exchange(i - 1).wait()
                    gain_out[i] = gain_out[i - 1] + gain_in[i - 1]
                gain_exchange(i).start()

    last = len(partners) - 1
    gain_exchange(last).wait()
    out_gains[...] = gain_out[last] + gain_in[last]

    for i in range(8):
        send_late(i).wait_send()
    for i in range(11):
        send_gu(i).wait_send()

    def finish(cls, c):
        for make in hops(cls, c):
            make().wait_send()
        share_second(cls, c).wait_send()
        share_first(cls, c).wait()
        pass_on(cls, c).wait()
        keep(cls, c).wait()

    @pl.loop(0, 4)
    def _(c):
        finish(Down, c)

    @pl.loop(0, 19)
    def _(c):
        @pl.when(c % 4 == 1)
        def _():
            finish(Early, c)

        @pl.when(c % 4 != 1)
        def _():
            finish(Square, c)


def reduce_gradients(group_size, activations, gains):
    extra = []
    mask = 4
    while mask < group_size:
        extra.append(mask)
        mask *= 2
    n_extra = len(extra)
    low = jnp.bfloat16
    tokens = activations[0].shape[0]
    scratch = [
        pltpu.VMEM((3, tokens, D), low),
        pltpu.VMEM((3, tokens, D), low),
        pltpu.VMEM((2, tokens, 768), low),
        pltpu.VMEM((2, tokens, 768), low),
        pltpu.VMEM((19, tokens, BLOCK), low),
        pltpu.VMEM((19, tokens, BLOCK), low),
        pltpu.VMEM((4, tokens, BLOCK), low),
        pltpu.VMEM((4, tokens, BLOCK), low),
        pltpu.VMEM((19, 2, 2, 256, BLOCK), low),
        pltpu.VMEM((19, 2, 2, 128, BLOCK), low),
        pltpu.VMEM((19, 2, 128, BLOCK), low),
        pltpu.VMEM((19, 128, BLOCK), low),
        pltpu.VMEM((4, 2, 704, BLOCK), low),
        pltpu.VMEM((4, 704, BLOCK), low),
        pltpu.VMEM((4, 352, BLOCK), low),
        pltpu.VMEM((4, 176, BLOCK), low),
        pltpu.VMEM((4 + n_extra, 8, D), jnp.float32),
        pltpu.VMEM((4 + n_extra, 8, D), jnp.float32),
        pltpu.VMEM((6, 2, 256, BLOCK), low),
        pltpu.VMEM((6, 256, BLOCK), low),
        pltpu.VMEM((max(n_extra, 1), 19 if n_extra else 1, 128, BLOCK), low),
        pltpu.VMEM((max(n_extra, 1), 4 if n_extra else 1, 176, BLOCK), low),
        pltpu.VMEM((768, BLOCK), low),
        pltpu.SemaphoreType.DMA((2, 5)),
        pltpu.SemaphoreType.DMA((2, 23)),
        pltpu.SemaphoreType.DMA((19,)),
        pltpu.SemaphoreType.DMA((19,)),
        pltpu.SemaphoreType.DMA((6 + n_extra, 23)),
        pltpu.SemaphoreType.DMA((6 + n_extra, 23)),
        pltpu.SemaphoreType.DMA((23,)),
        pltpu.SemaphoreType.DMA((4 + n_extra,)),
        pltpu.SemaphoreType.DMA((4 + n_extra,)),
    ]
    anywhere = pl.BlockSpec(memory_space=pl.ANY)
    near_by = pl.BlockSpec(memory_space=pltpu.VMEM)
    return pl.pallas_call(
        functools.partial(reduce_kernel, tuple(extra)),
        out_shape=(
            jax.ShapeDtypeStruct((2, 19, 256, BLOCK), low),
            jax.ShapeDtypeStruct((2, 4, 352, BLOCK), low),
            jax.ShapeDtypeStruct((8, D), jnp.float32),
        ),
        in_specs=[anywhere] * 14 + [near_by],
        out_specs=(anywhere, anywhere, near_by),
        scratch_shapes=scratch,
        compiler_params=pltpu.CompilerParams(
            collective_id=0, has_side_effects=True, vmem_limit_bytes=58 * 2**20
        ),
        cost_estimate=pl.CostEstimate(flops=13 * 10**9, bytes_accessed=30 * 10**6, transcendentals=0),
        name="reduce_gradients",
    )(*activations, gains)


def to_f32(value):
    return value.astype(jnp.float32)


def to_low(value):
    return value.astype(jnp.bfloat16)


def by_rows(left, right):
    return lax.dot_general(left, right, (((1,), (1,)), ((), ())), preferred_element_type=jnp.float32)


def by_tokens(left, right):
    return lax.dot_general(left, right, (((0,), (0,)), ((), ())), preferred_element_type=jnp.float32)


def times(left, right):
    return jnp.dot(left, right, preferred_element_type=jnp.float32)


def cols(index, size=BLOCK, base=0):
    if isinstance(index, int):
        return pl.ds(base + index * size, size)
    return pl.ds(pl.multiple_of(base + index * size, 128), size)


def inverse_rms(values):
    return lax.rsqrt(jnp.mean(values * values, axis=-1, keepdims=True) + EPS)


def layer_kernel(*refs):
    (tokens, cotangent, mem_k, mem_v, index, flags, cosine, sine, gain_a, gain_f) = refs[:10]
    (w_qkv_hbm, w_o_hbm, w_gu_hbm, w_d_hbm) = refs[10:14]
    (act, igrad, na_all, nf_all, o_all, z_all, dgu, dm, f_cols, e_cols) = refs[14:24]
    (na_p, nf_p, o_p, z_p, dgu_p, e_p, gains) = refs[24:31]
    refs = refs[31:]
    (w_qkv, w_o, w_gu, w_d, xs, qkv, probs, resid, factors, grads, picked_k, picked_v) = refs[:12]
    (kept, hidden, y_low, wide, dh, f_low, d_att, gx) = refs[12:20]
    (sem_w, sem_in, sem_mem, sem_t, sem_out, sem_send, sem_recv, sem_xsend, sem_xrecv) = refs[20:29]

    section, dpi, group = (lax.axis_index(name) for name in ("section", "dp", "group"))
    mask1 = 1 + section
    half = (group // mask1) % 2
    bit0 = dpi % 2
    twin = (1 - section, dpi, group)
    first = (section, dpi, flip(group, mask1))
    near = (section, flip(dpi, 1), group)
    is_lower = section == 0
    is_upper = section == 1
    scale = HEAD_DIM ** (-0.5)

    weights = []
    for i, (src, dst, pieces) in enumerate(
        ((w_qkv_hbm, w_qkv, 4), (w_o_hbm, w_o, 1), (w_gu_hbm, w_gu, 4), (w_d_hbm, w_d, 2))
    ):
        size = src.shape[0] // pieces
        weights.append(
            [
                pltpu.make_async_copy(src.at[pl.ds(p * size, size)], dst.at[pl.ds(p * size, size)], sem_w.at[i, p])
                for p in range(pieces)
            ]
        )

    def rows(m):
        return pl.ds(m * SEG, SEG)

    def load_tokens(m):
        return pltpu.make_async_copy(tokens.at[rows(m)], xs.at[m], sem_in.at[0, m])

    def load_cotangent(m):
        return pltpu.make_async_copy(cotangent.at[rows(m)], grads.at[m], sem_in.at[1, m])

    def send_up(m):
        return pltpu.make_async_remote_copy(
            src_ref=y_low.at[m], dst_ref=xs.at[m], send_sem=sem_send.at[0, m], recv_sem=sem_recv.at[0, m],
            device_id=twin, device_id_type=MESH,
        )

    def send_down(m):
        return pltpu.make_async_remote_copy(
            src_ref=gx.at[m], dst_ref=grads.at[m], send_sem=sem_send.at[1, m], recv_sem=sem_recv.at[1, m],
            device_id=twin, device_id_type=MESH,
        )

    @pl.when(is_lower)
    def _():
        load_tokens(0).start()

    for copy in weights[0]:
        copy.start()

    @pl.when(is_lower)
    def _():
        load_tokens(1).start()

    memory_in = [
        pltpu.make_async_copy(src.at[m], factors.at[m, :, cols(i, D)], sem_mem.at[i, m])
        for m in range(MICRO)
        for i, src in enumerate((mem_k, mem_v))
    ]

    @pl.when(is_upper)
    def _():
        for copy in memory_in:
            copy.start()
        for m in range(MICRO):
            load_cotangent(m).start()

    for group_copies in weights[1:]:
        for copy in group_copies:
            copy.start()

    barrier = pltpu.get_barrier_semaphore()
    pl.semaphore_signal(barrier, inc=1, device_id=twin, device_id_type=MESH)
    pl.semaphore_signal(barrier, inc=1, device_id=first, device_id_type=MESH)
    pl.semaphore_signal(barrier, inc=1, device_id=near, device_id_type=MESH)
    pl.semaphore_wait(barrier, 3)

    @pl.when(is_lower)
    def _():
        picked_k[...] = jnp.zeros_like(picked_k)
        picked_v[...] = jnp.zeros_like(picked_v)

    @pl.when(is_upper)
    def _():
        for copy in memory_in:
            copy.wait()
        places = lax.broadcasted_iota(jnp.int32, (SEG, TOPM), 0)
        for m in range(MICRO):
            chosen = to_low(to_f32(index[m : m + 1, :] == places).T)
            for n in range(4):
                picked_k[m, :, cols(n)] = to_low(times(chosen, factors[m, :, cols(n)]))
                picked_v[m, :, cols(n)] = to_low(times(chosen, factors[m, :, cols(n, BLOCK, D)]))

    sent = []

    def exchange(src, dst, at, device=first):
        copy = pltpu.make_async_remote_copy(
            src_ref=src, dst_ref=dst, send_sem=sem_xsend.at[at], recv_sem=sem_xrecv.at[at],
            device_id=device, device_id_type=MESH,
        )
        copy.start()
        return copy

    def exchange_grads(src, m, i):
        return exchange(src, e_p.at[i, rows(m)], 14 + m * 4 + i, near)

    @pl.when(is_upper)
    def _():
        for m in range(MICRO):
            for i in range(4):
                exchange_grads(cotangent.at[rows(m), cols(i)], m, i)

    def local(src, dst, sem):
        copy = pltpu.make_async_copy(src, dst, sem)
        copy.start()
        sent.append(copy)

    def share_kept(kind, out, partner_out, m):
        view = kept.at[m, kind]
        local(view, out.at[rows(m)], sem_t.at[kind, m])
        sent.append(exchange(view, partner_out.at[rows(m)], kind * MICRO + m))

    def forward(m):
        @pl.when(is_lower)
        def _():
            load_tokens(m).wait()

        @pl.when(is_upper)
        def _():
            send_up(m).wait_recv()

        x = to_f32(xs[m])
        normed = kept.at[m, 0]
        normed[...] = to_low(x * inverse_rms(x) * to_f32(gain_a[...]))
        if m == 0:
            for copy in weights[0]:
                copy.wait()

        def rotated(j):
            block = times(normed[...], w_qkv[:, cols(j)])
            for p in range(2):
                part = block[:, p * HEAD_DIM : (p + 1) * HEAD_DIM]
                part = part * cosine[...] + pltpu.roll(part, HEAD_DIM // 2, 1) * sine[...]
                qkv[m, :, cols(2 * j + p, HEAD_DIM)] = to_low(part)

        for i in range(8):
            rotated(i)

        def plain(j):
            qkv[m, :, cols(j, BLOCK, 2 * D)] = to_low(times(normed[...], w_qkv[:, cols(j, BLOCK, 2 * D)]))

        for i in range(4):
            plain(i)
        share_kept(0, na_all, na_p, m)
        attended = kept.at[m, 1]
        steep = scale * 1.4426950408889634
        ones = jnp.ones((SEG, HEAD_DIM), jnp.bfloat16)
        bias = (1 - flags[m] * section).astype(jnp.float32) * NEG
        causal = lax.broadcasted_iota(jnp.int32, (SEG, SEG), 0) >= lax.broadcasted_iota(jnp.int32, (SEG, SEG), 1)

        def head(h):
            query = qkv[m, :, cols(h, HEAD_DIM)]
            local = by_rows(query, qkv[m, :, cols(h, HEAD_DIM, D)])
            local = jnp.where(causal, local, NEG)
            remote = by_rows(query, picked_k[m, :, cols(h, HEAD_DIM)]) + bias
            peak = jnp.maximum(
                jnp.max(local, axis=-1, keepdims=True), jnp.max(remote, axis=-1, keepdims=True)
            )
            local = jnp.exp2((local - peak) * steep)
            remote = jnp.exp2((remote - peak) * steep)
            value = jnp.concatenate([qkv[m, :, cols(h, HEAD_DIM, 2 * D)], ones], axis=1)
            value_m = jnp.concatenate([picked_v[m, :, cols(h, HEAD_DIM)], ones[:TOPM]], axis=1)
            result = times(to_low(local), value) + times(to_low(remote), value_m)
            share = 1.0 / result[:, HEAD_DIM:]
            attended[:, cols(h, HEAD_DIM)] = to_low(result[:, :HEAD_DIM] * share)
            probs[m, h, :, :HEAD_DIM] = to_low(local[:, :HEAD_DIM] * share)
            probs[m, h, :, HEAD_DIM:SEG] = to_low(local[:, HEAD_DIM:] * share)
            probs[m, h, :, SEG:] = to_low(remote * share)

        for i in range(HEADS):
            head(i)
        if m == 0:
            weights[1][0].wait()

        def project(n):
            resid[m, :, cols(n)] = to_f32(xs[m, :, cols(n)]) + times(attended[...], w_o[:, cols(n)])

        for i in range(4):
            project(i)
        share_kept(1, o_all, o_p, m)
        normed_ffn = kept.at[m, 2]
        h = resid[m]
        normed_ffn[...] = to_low(h * inverse_rms(h) * to_f32(gain_f[...]))
        if m == 0:
            for copy in weights[2]:
                copy.wait()

        def gate(j):
            a = times(normed_ffn[...], w_gu[:, cols(j)])
            u = times(normed_ffn[...], w_gu[:, cols(j, BLOCK, FF)])
            sg = jax.nn.sigmoid(a)
            silu = a * sg
            hidden[m, :, cols(j)] = to_low(silu * u)
            factors[m, :, cols(j)] = to_low(u * sg * (1.0 + a * (1.0 - sg)))
            factors[m, :, cols(j, BLOCK, FF)] = to_low(silu)

        for i in range(FF // BLOCK):
            gate(i)
        if m == 0:
            for copy in weights[3]:
                copy.wait()

        def down(n):
            y_low[m, :, cols(n)] = to_low(resid[m, :, cols(n)] + times(hidden[m], w_d[:, cols(n)]))

        for i in range(4):
            down(i)

        @pl.when(is_lower)
        def _():
            send_up(m).start()

        write_out(y_low.at[m], act.at[rows(m)], 0, m).start()
        share_kept(2, nf_all, nf_p, m)
        local(hidden.at[m], z_all.at[rows(m)], sem_t.at[3, m])
        for j in range(2):
            span = hidden.at[m, :, down_span(j, 1 - bit0)]
            sent.append(exchange(span, z_p.at[j, rows(m)], 3 * MICRO + 2 * m + j, near))

    def write_out(src, dst, kind, m):
        return pltpu.make_async_copy(src, dst, sem_out.at[kind, m])

    def block_out(src, dst, kind, m, i):
        return write_out(src.at[m, :, cols(i)], dst.at[i, rows(m)], kind, m)

    block_sets = ((grads, e_cols, 2, 4), (factors, dgu, 3, 22), (f_low, f_cols, 4, 4), (qkv, dm, 5, 12))

    def start_blocks(which, m):
        src, dst, kind, count = block_sets[which]
        for i in range(count):
            block_out(src, dst, kind, m, i).start()

    def wait_blocks(which, m):
        src, dst, kind, count = block_sets[which]
        whole = dst.at[:, rows(m)]
        pltpu.make_async_copy(whole, whole, sem_out.at[kind, m]).wait()

    def norm_back(d_normed, values, gain, incoming):
        inverse = inverse_rms(values)
        scaled = d_normed * to_f32(gain)
        column = jnp.sum(d_normed * (values * inverse), axis=0, keepdims=True)
        centre = jnp.mean(scaled * values, axis=-1, keepdims=True)
        return incoming + inverse * scaled - values * (inverse * inverse * inverse * centre), column

    def backward(m):
        @pl.when(is_upper)
        def _():
            load_cotangent(m).wait()

        @pl.when(is_lower)
        def _():
            send_down(m).wait_recv()

        start_blocks(0, m)

        @pl.when(is_lower)
        def _():
            for i in range(4):
                exchange_grads(grads.at[m, :, cols(i)], m, i)

        def gate_back(j):
            dz = by_rows(grads[m], w_d[cols(j), :])
            factors[m, :, cols(j)] = to_low(dz * to_f32(factors[m, :, cols(j)]))
            factors[m, :, cols(j, BLOCK, FF)] = to_low(dz * to_f32(factors[m, :, cols(j, BLOCK, FF)]))

        for i in range(FF // BLOCK):
            gate_back(i)
        start_blocks(1, m)
        if m == 0:
            for i in range(11):
                block = factors.at[m, :, cols((1 - half) * 11 + i)]
                sent.append(exchange(block, dgu_p.at[i], 22 + i))

        def gate_up_back(n):
            wide[:, cols(n)] = by_rows(factors[m], w_gu[cols(n), :])

        for i in range(4):
            gate_up_back(i)
        result, column = norm_back(wide[...], resid[m], gain_f[...], to_f32(grads[m]))
        dh[...] = result
        f_low[m] = to_low(result)
        gains[1:2, :] = column if m == 0 else gains[1:2, :] + column
        start_blocks(2, m)

        def out_back(n):
            d_att[:, cols(n)] = to_low(by_rows(f_low[m], w_o[cols(n), :]))

        for i in range(4):
            out_back(i)

        def rotate_back(part):
            return part * cosine[...] - pltpu.roll(part, HEAD_DIM // 2, 1) * sine[...]

        def head_back(h):
            at_q, at_k, at_v = (cols(h, HEAD_DIM, base) for base in (0, D, 2 * D))
            query, key, value = qkv[m, :, at_q], qkv[m, :, at_k], qkv[m, :, at_v]
            d_out = d_att[:, cols(h, HEAD_DIM)]
            p_local = probs[m, h, :, :SEG]
            p_remote = probs[m, h, :, SEG:]
            d_local = by_rows(d_out, value)
            d_remote = by_rows(d_out, picked_v[m, :, cols(h, HEAD_DIM)])
            wide_local, wide_remote = to_f32(p_local), to_f32(p_remote)
            centre = jnp.sum(to_f32(d_out) * to_f32(kept[m, 1, :, cols(h, HEAD_DIM)]), axis=-1, keepdims=True)
            d_local = to_low(wide_local * (d_local - centre))
            d_remote = to_low(wide_remote * (d_remote - centre))
            d_query = (times(d_local, key) + times(d_remote, picked_k[m, :, cols(h, HEAD_DIM)])) * scale
            d_key = by_tokens(d_local, query) * scale
            qkv[m, :, at_v] = to_low(by_tokens(p_local, d_out))
            qkv[m, :, at_q] = to_low(rotate_back(d_query))
            qkv[m, :, at_k] = to_low(rotate_back(d_key))

        for i in range(HEADS):
            head_back(i)
        start_blocks(3, m)

        def qkv_back(n):
            wide[:, cols(n)] = by_rows(qkv[m], w_qkv[cols(n), :])

        for i in range(4):
            qkv_back(i)
        result, column = norm_back(wide[...], to_f32(xs[m]), gain_a[...], dh[...])
        gx[m] = to_low(result)
        gains[0:1, :] = column if m == 0 else gains[0:1, :] + column

        @pl.when(is_upper)
        def _():
            send_down(m).start()

        write_out(gx.at[m], igrad.at[rows(m)], 1, m).start()

    gains[...] = jnp.zeros_like(gains)
    for m in range(MICRO):
        forward(m)
    for m in range(MICRO):
        backward(m)

    for m in range(MICRO):
        write_out(y_low.at[m], act.at[rows(m)], 0, m).wait()
        write_out(gx.at[m], igrad.at[rows(m)], 1, m).wait()
        for which in range(4):
            wait_blocks(which, m)
    for copy in sent:
        copy.wait()
    for m in range(MICRO):
        for i in range(4):
            pltpu.make_async_remote_copy(
                src_ref=grads.at[m, :, cols(i)], dst_ref=e_p.at[i, rows(m)],
                send_sem=sem_xsend.at[14 + m * 4 + i], recv_sem=sem_xrecv.at[14 + m * 4 + i],
                device_id=near, device_id_type=MESH,
            ).wait()

    @pl.when(is_lower)
    def _():
        for m in range(MICRO):
            send_up(m).wait_send()

    @pl.when(is_upper)
    def _():
        for m in range(MICRO):
            send_down(m).wait_send()


def rotary_constants():
    half = HEAD_DIM // 2
    freqs = np.exp(-np.log(10000.0) * np.arange(half) * 2.0 / HEAD_DIM)
    angles = np.arange(SEG)[:, None] * freqs[None, :]
    cosine = np.concatenate([np.cos(angles), np.cos(angles)], axis=1)
    sine = np.concatenate([-np.sin(angles), np.sin(angles)], axis=1)
    return cosine.astype(np.float32), sine.astype(np.float32)


def run_layers(tokens, cotangent, mem_keys, mem_values, index, flags, gain_a, gain_f, w_qkv, w_o, w_gu, w_d):
    cosine, sine = rotary_constants()
    count = tokens.shape[0]
    low, wide = jnp.bfloat16, jnp.float32
    anywhere = pl.BlockSpec(memory_space=pl.ANY)
    near_by = pl.BlockSpec(memory_space=pltpu.VMEM)
    shape = jax.ShapeDtypeStruct
    outs = (
        shape((count, D), low),
        shape((count, D), low),
        shape((count, D), low),
        shape((count, D), low),
        shape((count, D), low),
        shape((count, FF), low),
        shape((22, count, BLOCK), low),
        shape((12, count, BLOCK), low),
        shape((4, count, BLOCK), low),
        shape((4, count, BLOCK), low),
        shape((count, D), low),
        shape((count, D), low),
        shape((count, D), low),
        shape((2, count, 768), low),
        shape((11, SEG, BLOCK), low),
        shape((4, count, BLOCK), low),
        shape((8, D), wide),
    )
    scratch = [
        pltpu.VMEM((D, 3 * D), low),
        pltpu.VMEM((D, D), low),
        pltpu.VMEM((D, 2 * FF), low),
        pltpu.VMEM((FF, D), low),
        pltpu.VMEM((MICRO, SEG, D), low),
        pltpu.VMEM((MICRO, SEG, 3 * D), low),
        pltpu.VMEM((MICRO, HEADS, SEG, SEG + TOPM), low),
        pltpu.VMEM((MICRO, SEG, D), wide),
        pltpu.VMEM((MICRO, SEG, 2 * FF), low),
        pltpu.VMEM((MICRO, SEG, D), low),
        pltpu.VMEM((MICRO, TOPM, D), low),
        pltpu.VMEM((MICRO, TOPM, D), low),
        pltpu.VMEM((MICRO, 3, SEG, D), low),
        pltpu.VMEM((MICRO, SEG, FF), low),
        pltpu.VMEM((MICRO, SEG, D), low),
        pltpu.VMEM((SEG, D), wide),
        pltpu.VMEM((SEG, D), wide),
        pltpu.VMEM((MICRO, SEG, D), low),
        pltpu.VMEM((SEG, D), low),
        pltpu.VMEM((MICRO, SEG, D), low),
        pltpu.SemaphoreType.DMA((4, 4)),
        pltpu.SemaphoreType.DMA((2, MICRO)),
        pltpu.SemaphoreType.DMA((2, MICRO)),
        pltpu.SemaphoreType.DMA((4, MICRO)),
        pltpu.SemaphoreType.DMA((6, MICRO)),
        pltpu.SemaphoreType.DMA((2, MICRO)),
        pltpu.SemaphoreType.DMA((2, MICRO)),
        pltpu.SemaphoreType.DMA((33,)),
        pltpu.SemaphoreType.DMA((33,)),
    ]
    return pl.pallas_call(
        layer_kernel,
        out_shape=outs,
        in_specs=[anywhere] * 4
        + [near_by, pl.BlockSpec(memory_space=pltpu.SMEM)]
        + [near_by] * 4
        + [anywhere] * 4,
        out_specs=(anywhere,) * 16 + (near_by,),
        scratch_shapes=scratch,
        compiler_params=pltpu.CompilerParams(
            collective_id=1, has_side_effects=True, vmem_limit_bytes=60 * 2**20
        ),
        cost_estimate=pl.CostEstimate(flops=27 * 10**9, bytes_accessed=50 * 10**6, transcendentals=0),
        name="relay_layers",
    )(tokens, cotangent, mem_keys, mem_values, index, flags, cosine, sine, gain_a, gain_f, w_qkv, w_o, w_gu, w_d)


def finish_kernel(*refs):
    (sq, down, gains, act, igrad) = refs[:5]
    (gu_out, o_out, qkv_out, d_out, ga_out, gf_out, act_out, igrad_out) = refs[5:13]
    (sq_v, d_v, gu_v, o_v, qkv_v, down_v, pass_v, sem_in, sem_out) = refs[13:]
    parts = (
        (gu_v, gu_out, 0, 11),
        (qkv_v, qkv_out, 13, 6),
        (o_v, o_out, 11, 2),
    )
    loads = [
        [
            pltpu.make_async_copy(
                sq.at[half, pl.ds(base, count)], sq_v.at[half, pl.ds(base, count)], sem_in.at[2 * i + half]
            )
            for half in range(2)
        ]
        for i, (_, _, base, count) in enumerate(parts)
    ]
    load_d = pltpu.make_async_copy(down, d_v, sem_in.at[6])
    passed = [
        (pltpu.make_async_copy(src, pass_v.at[i], sem_in.at[7 + i]), pltpu.make_async_copy(pass_v.at[i], dst, sem_out.at[8 + i]))
        for i, (src, dst) in enumerate(((act, act_out), (igrad, igrad_out)))
    ]
    for pair in loads:
        for copy in pair:
            copy.start()
    load_d.start()
    for load, _ in passed:
        load.start()
    stores = []
    mine = cols(lax.axis_index("dp"))
    ga_out[...] = gains[0:1, mine]
    gf_out[...] = gains[1:2, mine]
    for i, (view, out, base, count) in enumerate(parts):
        for half in range(2):
            loads[i][half].wait()
            for c in range(count):
                at = pl.ds((half * count + c) * BLOCK, BLOCK)
                view[:, at] = sq_v[half, base + c].astype(jnp.float32)
            span = pl.ds(half * count * BLOCK, count * BLOCK)
            stores.append(pltpu.make_async_copy(view.at[:, span], out.at[:, span], sem_out.at[2 * i + half]))
            stores[-1].start()
    for load, store in passed:
        load.wait()
        store.start()
        stores.append(store)
    load_d.wait()
    for half in range(2):
        for k in range(4):
            down_v[pl.ds(half * 352, 352), pl.ds(k * BLOCK, BLOCK)] = d_v[half, k].astype(jnp.float32)
        span = pl.ds(half * 352, 352)
        stores.append(pltpu.make_async_copy(down_v.at[span], d_out.at[span], sem_out.at[6 + half]))
        stores[-1].start()
    for copy in stores:
        copy.wait()


def finish_gradients(out_sq, out_d, out_gains, act, igrad):
    anywhere = pl.BlockSpec(memory_space=pl.ANY)
    near_by = pl.BlockSpec(memory_space=pltpu.VMEM)
    shapes = ((256, 2 * FF), (256, D), (256, 3 * D), (704, D))
    wide = jnp.float32
    return pl.pallas_call(
        finish_kernel,
        out_shape=tuple(jax.ShapeDtypeStruct(shape, wide) for shape in shapes + ((1, BLOCK),) * 2)
        + (jax.ShapeDtypeStruct(act.shape, act.dtype),) * 2,
        in_specs=[anywhere] * 2 + [near_by] + [anywhere] * 2,
        out_specs=(anywhere,) * 4 + (near_by,) * 2 + (anywhere,) * 2,
        scratch_shapes=[pltpu.VMEM(out_sq.shape, jnp.bfloat16), pltpu.VMEM(out_d.shape, jnp.bfloat16)]
        + [pltpu.VMEM(shape, wide) for shape in shapes]
        + [pltpu.VMEM((2,) + act.shape, act.dtype)]
        + [pltpu.SemaphoreType.DMA((9,)), pltpu.SemaphoreType.DMA((10,))],
        compiler_params=pltpu.CompilerParams(vmem_limit_bytes=60 * 2**20),
        name="finish_gradients",
    )(out_sq, out_d, out_gains, act, igrad)


def body(
    group_size,
    tokens,
    cotangent,
    mem_keys,
    mem_values,
    mem_index,
    mem_flags,
    norm_attn,
    w_qkv,
    w_out,
    norm_ffn,
    w_gate_up,
    w_down,
):
    (act, igrad, na_all, nf_all, o_all, z_all, dgu, dm, f_cols, e_cols, na_p, nf_p, o_p, z_p, dgu_p, e_p, gains) = run_layers(
        tokens,
        cotangent,
        mem_keys,
        mem_values,
        mem_index,
        mem_flags,
        norm_attn,
        norm_ffn,
        w_qkv[0],
        w_out[0],
        w_gate_up[0],
        w_down[0],
    )
    reduced = reduce_gradients(
        group_size,
        (nf_all, na_all, o_all, z_all, dgu, dm, f_cols, e_cols, nf_p, na_p, o_p, z_p, dgu_p, e_p),
        gains,
    )
    (grad_gu, grad_o, grad_qkv, grad_d, grad_na, grad_nf, act, igrad) = finish_gradients(*reduced, act, igrad)
    return (
        act[None],
        igrad[None],
        grad_na,
        grad_qkv[None],
        grad_o[None],
        grad_nf,
        grad_gu[None],
        grad_d[None],
    )


def solution(mesh):
    placed = (
        P(("dp", "group"), None),
        P(("dp", "group"), None),
        P(("dp", "group"), None, None),
        P(("dp", "group"), None, None),
        P(("dp", "group"), None),
        P(("dp", "group")),
        P("section", None),
        P("section", None, None),
        P("section", None, None),
        P("section", None),
        P("section", None, None),
        P("section", None, None),
    )
    return jax.shard_map(
        functools.partial(body, mesh.shape["group"]),
        mesh=mesh,
        in_specs=placed,
        out_specs=(
            P("section", ("dp", "group"), None),
            P("section", ("dp", "group"), None),
            P("section", "dp"),
            P("section", "dp", None),
            P("section", "dp", None),
            P("section", "dp"),
            P("section", "dp", None),
            P("section", "dp", None),
        ),
        check_vma=False,
    )
```

```python
import functools

import jax
import jax.numpy as jnp
import numpy as np
from jax import lax
from jax.experimental import pallas as pl
from jax.experimental.pallas import tpu as pltpu
from jax.sharding import PartitionSpec as P

D = 1024
HEADS = 8
HEAD_DIM = 128
FF = 2816
SEG = 256
TOPM = 128
MICRO = 2
EPS = 1e-05
NEG = -1e30
MESH = pl.DeviceIdType.MESH
BLOCK = 256
LAGS = (0, 3, 6, 9, 13)


def flip(value, mask):
    return value + mask * (1 - 2 * ((value // mask) % 2))


def down_span(j, bit):
    return pl.ds(pl.multiple_of(1408 * j + 640 * bit, 128), 768)


def summed(left, right):
    return (left.astype(jnp.float32) + right.astype(jnp.float32)).astype(jnp.bfloat16)


def reduce_kernel(extra, *refs):
    n_extra = len(extra)
    (nf_all, na_all, o_all, z_all, dgu, dm, f_cols, e_cols, nf_p, na_p, o_p, z_p, dgu_p, e_p, gains) = refs[:15]
    (out_sq, out_d, out_gains) = refs[15:18]
    refs = refs[18:]
    (a_own, a_in, z_own, z_in, b_own, b_in, e_own, e_in) = refs[:8]
    (g_sq, q0, q1, q2, g_d, d0, d1, d2, gain_out, gain_in) = refs[8:18]
    refs = refs[18:]
    n0, n1 = refs[:2]
    refs = refs[2:]
    x_sq, x_d, spread = refs[:3]
    (sem_load, sem_bload, sem_bsend, sem_brecv) = refs[3:7]
    (sem_send, sem_recv, sem_copy, gain_send, gain_recv) = refs[7:12]

    section, dpi, group = (lax.axis_index(name) for name in ("section", "dp", "group"))
    mask1 = 1 + section
    mask2 = 2 - section
    half = (group // mask1) % 2
    low2 = (group // mask2) % 2
    bit0 = dpi % 2
    bit1 = (dpi // 2) % 2
    first = (section, dpi, flip(group, mask1))
    second = (section, dpi, flip(group, mask2))
    near = (section, flip(dpi, 1), group)
    far = (section, flip(dpi, 2), group)
    others = [(section, dpi, flip(group, mask)) for mask in extra]
    partners = [first, second, near, far] + others

    barrier = pltpu.get_barrier_semaphore()
    for partner in partners:
        pl.semaphore_signal(barrier, inc=1, device_id=partner, device_id_type=MESH)
    pl.semaphore_wait(barrier, len(partners))

    def remote(src, dst, send, recv, device):
        return pltpu.make_async_remote_copy(
            src_ref=src, dst_ref=dst, send_sem=send, recv_sem=recv, device_id=device, device_id_type=MESH
        )

    def load_a(slot):
        return (
            pltpu.make_async_copy((nf_all, o_all, na_all)[slot], a_own.at[slot], sem_load.at[0, slot]),
            pltpu.make_async_copy((nf_p, o_p, na_p)[slot], a_in.at[slot], sem_load.at[1, slot]),
        )

    def load_z():
        own = [
            pltpu.make_async_copy(z_all.at[:, down_span(j, bit0)], z_own.at[j], sem_load.at[0, 3 + j])
            for j in range(2)
        ]
        return own + [pltpu.make_async_copy(z_p, z_in, sem_load.at[1, 3])]

    def load_gu(i):
        return (
            pltpu.make_async_copy(dgu.at[:, cols(half * 11 + i)], b_own.at[i], sem_bload.at[0, i]),
            pltpu.make_async_copy(dgu_p.at[:, cols(i)], b_in.at[i, pl.ds(0, SEG)], sem_bload.at[1, i]),
        )

    def send_gu(i):
        later = pl.ds(SEG, SEG)
        return remote(
            dgu.at[later, cols((1 - half) * 11 + i)], b_in.at[i, later], sem_bsend.at[i], sem_brecv.at[i], first
        )

    def load_e(k):
        return (
            pltpu.make_async_copy(e_cols.at[:, cols(k)], e_own.at[k], sem_bload.at[0, 19 + k]),
            pltpu.make_async_copy(e_p.at[:, cols(k)], e_in.at[k], sem_bload.at[1, 19 + k]),
        )

    def late(part, i):
        return f_cols.at[:, cols(part * 2 + i)] if i < 2 else dm.at[:, cols(part * 6 + i - 2)]

    def load_late(i):
        return pltpu.make_async_copy(late(half, i), b_own.at[11 + i], sem_bload.at[0, 11 + i])

    def send_late(i):
        return remote(late(1 - half, i), b_in.at[11 + i], sem_bsend.at[11 + i], sem_brecv.at[11 + i], first)

    def start(copies):
        for copy in copies:
            copy.start()

    def finish_copies(copies):
        for copy in copies:
            copy.wait()

    kinds = ((0, 0, 11), (1, 11, 2), (2, 13, 6))
    start(load_z())
    for i in range(3):
        send_gu(i).start()
    start(load_e(0))
    start(load_a(0))
    for i in range(3):
        start(load_gu(i))

    def load_rest():
        start(load_gu(3))
        for i in range(1, 4):
            start(load_e(i))
        for i in range(4, 11):
            start(load_gu(i))
        start(load_a(1))
        start(load_a(2))
        for i in range(8):
            load_late(i).start()

    def send_more(t):
        @pl.when(t < 8)
        def _():
            send_gu(t + 3).start()

        for i in range(8):

            @pl.when(t == 8 + i)
            def _():
                send_late(i).start()

    class Square:
        base, rows = 4, 256
        partial, recv0, recv1, recv2, xs, out = g_sq, q0, q1, q2, x_sq, out_sq

    class Early:
        base, rows = 4, 256
        partial, recv0, recv1, recv2, xs, out = g_sq, n0, n1, q2, x_sq, out_sq

    class Down:
        base, rows = 0, 352
        partial, recv0, recv1, recv2, xs, out = g_d, d0, d1, d2, x_d, out_d

    def rows_at(cls, part):
        size = cls.rows // 2
        return pl.ds(pl.multiple_of(part * size, 16), size)

    def half_rows(part):
        return pl.ds(pl.multiple_of(part * 352, 16), 352)

    def hop(cls, c, i, src, dst, device):
        k = cls.base + c
        return remote(src, dst, sem_send.at[i, k], sem_recv.at[i, k], device)

    def hops(cls, c):
        both = pl.ds(0, 2)
        if cls is Down:
            return (
                lambda: hop(cls, c, 0, cls.partial.at[c, 1 - bit1], cls.recv0.at[c], far),
                lambda: hop(cls, c, 1, cls.recv0.at[c, half_rows(1 - half)], cls.recv1.at[c], first),
                lambda: hop(cls, c, 2, cls.recv1.at[c, rows_at(cls, 1 - low2)], cls.recv2.at[c], second),
            )
        if cls is Early:
            slot = c // 4
            return (
                lambda: hop(cls, c, 0, cls.partial.at[c, both, 1 - bit0], cls.recv0.at[slot], near),
                lambda: hop(cls, c, 1, cls.recv0.at[slot, 1 - bit1], cls.recv1.at[slot], far),
                lambda: hop(cls, c, 2, cls.recv1.at[slot, rows_at(cls, 1 - low2)], cls.recv2.at[c], second),
            )
        return (
            lambda: hop(cls, c, 0, cls.partial.at[c, both, both, rows_at(cls, 1 - low2)], cls.recv0.at[c], second),
            lambda: hop(cls, c, 1, cls.recv0.at[c, both, 1 - bit0], cls.recv1.at[c], near),
            lambda: hop(cls, c, 2, cls.recv1.at[c, 1 - bit1], cls.recv2.at[c], far),
        )

    def combine(cls, c, i):
        if cls is Down:
            if i == 0:
                cls.recv0[c] = summed(cls.partial[c, bit1], cls.recv0[c])
            elif i == 1:
                cls.recv1[c] = summed(cls.recv0[c, half_rows(half)], cls.recv1[c])
            else:
                cls.recv2[c] = summed(cls.recv1[c, rows_at(cls, low2)], cls.recv2[c])
        elif cls is Early:
            slot = c // 4
            if i == 0:
                for j in range(2):
                    cls.recv0[slot, j] = summed(cls.partial[c, j, bit0], cls.recv0[slot, j])
            elif i == 1:
                cls.recv1[slot] = summed(cls.recv0[slot, bit1], cls.recv1[slot])
            else:
                cls.recv2[c] = summed(cls.recv1[slot, rows_at(cls, low2)], cls.recv2[c])
        elif i == 0:
            for j in range(4):
                cls.recv0[c, j // 2, j % 2] = summed(
                    cls.partial[c, j // 2, j % 2, rows_at(cls, low2)], cls.recv0[c, j // 2, j % 2]
                )
        elif i == 1:
            for j in range(2):
                cls.recv1[c, j] = summed(cls.recv0[c, j, bit0], cls.recv1[c, j])
        else:
            cls.recv2[c] = summed(cls.recv1[c, bit1], cls.recv2[c])

    def to_extra(cls, c, i):
        k = cls.base + c
        src = cls.recv2.at[c] if i == 0 else cls.xs.at[i - 1, c]
        return remote(src, cls.xs.at[i, c], sem_send.at[6 + i, k], sem_recv.at[6 + i, k], others[i])

    def final(cls, c):
        return cls.recv2.at[c] if n_extra == 0 else cls.xs.at[n_extra - 1, c]

    def share_second(cls, c):
        k = cls.base + c
        return remote(final(cls, c), cls.out.at[half, c, rows_at(cls, low2)], sem_send.at[3, k], sem_recv.at[3, k], second)

    def share_first(cls, c):
        k = cls.base + c
        return remote(final(cls, c), cls.out.at[half, c, rows_at(cls, low2)], sem_send.at[4, k], sem_recv.at[4, k], first)

    def pass_on(cls, c):
        k = cls.base + c
        block = cls.out.at[half, c, rows_at(cls, 1 - low2)]
        return remote(block, block, sem_send.at[5, k], sem_recv.at[5, k], first)

    def keep(cls, c):
        return pltpu.make_async_copy(final(cls, c), cls.out.at[half, c, rows_at(cls, low2)], sem_copy.at[cls.base + c])

    def multiply(left, right, left2, right2):
        return (by_tokens(left, right) + by_tokens(left2, right2)).astype(jnp.bfloat16)

    def partial_square(c):
        for kind, base, count in kinds:

            @pl.when(c == base)
            def _():
                finish_copies(load_a(kind))

        @pl.when(c < 11)
        def _():
            finish_copies(load_gu(c))
            send_gu(c).wait_recv()

        for i in range(8):

            @pl.when(c == 11 + i)
            def _():
                load_late(i).wait()
                send_late(i).wait_recv()

        for kind, base, count in kinds:

            @pl.when((c >= base) & (c < base + count))
            def _():
                for j in range(4):
                    rows = pl.ds(j * 256, 256)
                    g_sq[c, j // 2, j % 2] = multiply(
                        a_own[kind, :, rows], b_own[c], a_in[kind, :, rows], b_in[c]
                    )

        @pl.when(c % 4 == 1)
        def _():
            hops(Early, c)[0]().start()

        @pl.when(c % 4 != 1)
        def _():
            hops(Square, c)[0]().start()

    def partial_down(c):
        @pl.when(c == 0)
        def _():
            finish_copies(load_z())

        finish_copies(load_e(c))
        for j in range(2):
            spread[...] = multiply(z_own[j], e_own[c], z_in[j], e_in[c])
            g_d[c, j] = spread[pl.ds(pl.multiple_of(64 * bit0, 16), 704), :]
        hops(Down, c)[0]().start()

    def share(cls, c):
        share_second(cls, c).start()
        share_first(cls, c).start()
        keep(cls, c).start()

    def stage_hop(i, cls, c):
        hops(cls, c)[i]().wait_recv()
        combine(cls, c, i)
        if i < 2:
            hops(cls, c)[i + 1]().start()
        elif n_extra:
            to_extra(cls, c, 0).start()
        else:
            share(cls, c)

    def stage_extra(cls, c, i):
        to_extra(cls, c, i).wait()
        mine = cls.recv2[c] if i == 0 else cls.xs[i - 1, c]
        cls.xs[i, c] = summed(mine, cls.xs[i, c])
        if i + 1 < n_extra:
            to_extra(cls, c, i + 1).start()
        else:
            share(cls, c)

    def stage_pass(cls, c):
        share_second(cls, c).wait_recv()
        pass_on(cls, c).start()

    def partial(cls, c):
        if cls is Down:
            partial_down(c)
        else:
            partial_square(c)

    def by_order(stage, c):
        if stage is partial:
            stage(Square, c)
            return

        @pl.when(c % 4 == 1)
        def _():
            stage(Early, c)

        @pl.when(c % 4 != 1)
        def _():
            stage(Square, c)

    stages = [partial] + [functools.partial(stage_hop, i) for i in range(3)]
    stages += [functools.partial(lambda i, cls, c: stage_extra(cls, c, i), i) for i in range(n_extra)]

    stages += [stage_pass]

    def gain_exchange(i):
        return remote(gain_out.at[i], gain_in.at[i], gain_send.at[i], gain_recv.at[i], partners[i])

    lags = LAGS[:4] + tuple(LAGS[3] + 2 * (i + 1) for i in range(n_extra)) + (LAGS[4] + 2 * n_extra,)
    steps = 23 + lags[-1]

    @pl.loop(0, steps)
    def _(t):
        send_more(t)
        for i, stage in enumerate(stages):
            c = t - lags[i]
            turn = c // 5

            @pl.when((c >= 0) & (c < 20))
            def _():
                @pl.when(c % 5 == 0)
                def _():
                    stage(Down, turn)

                @pl.when(c % 5 != 0)
                def _():
                    by_order(stage, c - 1 - turn)

            @pl.when((c >= 20) & (c < 23))
            def _():
                by_order(stage, c - 4)

        @pl.when(t == 0)
        def _():
            load_rest()

        for i in range(len(partners)):

            @pl.when(t == 3 * i + 2)
            def _():
                if i == 0:
                    gain_out[0] = gains[...]
                else:
                    gain_exchange(i - 1).wait()
                    gain_out[i] = gain_out[i - 1] + gain_in[i - 1]
                gain_exchange(i).start()

    last = len(partners) - 1
    gain_exchange(last).wait()
    out_gains[...] = gain_out[last] + gain_in[last]

    for i in range(8):
        send_late(i).wait_send()
    for i in range(11):
        send_gu(i).wait_send()

    def finish(cls, c):
        for make in hops(cls, c):
            make().wait_send()
        share_second(cls, c).wait_send()
        share_first(cls, c).wait()
        pass_on(cls, c).wait()
        keep(cls, c).wait()

    @pl.loop(0, 4)
    def _(c):
        finish(Down, c)

    @pl.loop(0, 19)
    def _(c):
        @pl.when(c % 4 == 1)
        def _():
            finish(Early, c)

        @pl.when(c % 4 != 1)
        def _():
            finish(Square, c)


def reduce_gradients(group_size, activations, gains):
    extra = []
    mask = 4
    while mask < group_size:
        extra.append(mask)
        mask *= 2
    n_extra = len(extra)
    low = jnp.bfloat16
    tokens = activations[0].shape[0]
    scratch = [
        pltpu.VMEM((3, tokens, D), low),
        pltpu.VMEM((3, tokens, D), low),
        pltpu.VMEM((2, tokens, 768), low),
        pltpu.VMEM((2, tokens, 768), low),
        pltpu.VMEM((19, tokens, BLOCK), low),
        pltpu.VMEM((19, tokens, BLOCK), low),
        pltpu.VMEM((4, tokens, BLOCK), low),
        pltpu.VMEM((4, tokens, BLOCK), low),
        pltpu.VMEM((19, 2, 2, 256, BLOCK), low),
        pltpu.VMEM((19, 2, 2, 128, BLOCK), low),
        pltpu.VMEM((19, 2, 128, BLOCK), low),
        pltpu.VMEM((19, 128, BLOCK), low),
        pltpu.VMEM((4, 2, 704, BLOCK), low),
        pltpu.VMEM((4, 704, BLOCK), low),
        pltpu.VMEM((4, 352, BLOCK), low),
        pltpu.VMEM((4, 176, BLOCK), low),
        pltpu.VMEM((4 + n_extra, 8, D), jnp.float32),
        pltpu.VMEM((4 + n_extra, 8, D), jnp.float32),
        pltpu.VMEM((6, 2, 256, BLOCK), low),
        pltpu.VMEM((6, 256, BLOCK), low),
        pltpu.VMEM((max(n_extra, 1), 19 if n_extra else 1, 128, BLOCK), low),
        pltpu.VMEM((max(n_extra, 1), 4 if n_extra else 1, 176, BLOCK), low),
        pltpu.VMEM((768, BLOCK), low),
        pltpu.SemaphoreType.DMA((2, 5)),
        pltpu.SemaphoreType.DMA((2, 23)),
        pltpu.SemaphoreType.DMA((19,)),
        pltpu.SemaphoreType.DMA((19,)),
        pltpu.SemaphoreType.DMA((6 + n_extra, 23)),
        pltpu.SemaphoreType.DMA((6 + n_extra, 23)),
        pltpu.SemaphoreType.DMA((23,)),
        pltpu.SemaphoreType.DMA((4 + n_extra,)),
        pltpu.SemaphoreType.DMA((4 + n_extra,)),
    ]
    anywhere = pl.BlockSpec(memory_space=pl.ANY)
    near_by = pl.BlockSpec(memory_space=pltpu.VMEM)
    return pl.pallas_call(
        functools.partial(reduce_kernel, tuple(extra)),
        out_shape=(
            jax.ShapeDtypeStruct((2, 19, 256, BLOCK), low),
            jax.ShapeDtypeStruct((2, 4, 352, BLOCK), low),
            jax.ShapeDtypeStruct((8, D), jnp.float32),
        ),
        in_specs=[anywhere] * 14 + [near_by],
        out_specs=(anywhere, anywhere, near_by),
        scratch_shapes=scratch,
        compiler_params=pltpu.CompilerParams(
            collective_id=0, has_side_effects=True, vmem_limit_bytes=58 * 2**20
        ),
        cost_estimate=pl.CostEstimate(flops=13 * 10**9, bytes_accessed=30 * 10**6, transcendentals=0),
        name="reduce_gradients",
    )(*activations, gains)


def to_f32(value):
    return value.astype(jnp.float32)


def to_low(value):
    return value.astype(jnp.bfloat16)


def by_rows(left, right):
    return lax.dot_general(left, right, (((1,), (1,)), ((), ())), preferred_element_type=jnp.float32)


def by_tokens(left, right):
    return lax.dot_general(left, right, (((0,), (0,)), ((), ())), preferred_element_type=jnp.float32)


def times(left, right):
    return jnp.dot(left, right, preferred_element_type=jnp.float32)


def cols(index, size=BLOCK, base=0):
    if isinstance(index, int):
        return pl.ds(base + index * size, size)
    return pl.ds(pl.multiple_of(base + index * size, 128), size)


def inverse_rms(values):
    return lax.rsqrt(jnp.mean(values * values, axis=-1, keepdims=True) + EPS)


def layer_kernel(*refs):
    (tokens, cotangent, mem_k, mem_v, index, flags, cosine, sine, gain_a, gain_f) = refs[:10]
    (w_qkv_hbm, w_o_hbm, w_gu_hbm, w_d_hbm) = refs[10:14]
    (act, igrad, na_all, nf_all, o_all, z_all, dgu, dm, f_cols, e_cols) = refs[14:24]
    (na_p, nf_p, o_p, z_p, dgu_p, e_p, gains) = refs[24:31]
    refs = refs[31:]
    (w_qkv, w_o, w_gu, w_d, xs, qkv, probs, resid, factors, grads, picked_k, picked_v) = refs[:12]
    (kept, hidden, y_low, wide, dh, f_low, d_att, gx) = refs[12:20]
    (sem_w, sem_in, sem_mem, sem_t, sem_out, sem_send, sem_recv, sem_xsend, sem_xrecv) = refs[20:29]

    section, dpi, group = (lax.axis_index(name) for name in ("section", "dp", "group"))
    mask1 = 1 + section
    half = (group // mask1) % 2
    bit0 = dpi % 2
    twin = (1 - section, dpi, group)
    first = (section, dpi, flip(group, mask1))
    near = (section, flip(dpi, 1), group)
    is_lower = section == 0
    is_upper = section == 1
    scale = HEAD_DIM ** (-0.5)

    third = 3 * D // 4
    weights = [
        [
            pltpu.make_async_copy(w_qkv_hbm.at[:, cols(p, third)], w_qkv.at[:, cols(p, third)], sem_w.at[0, p])
            for p in range(4)
        ]
    ]
    for i, (src, dst, pieces) in enumerate(
        ((w_o_hbm, w_o, 1), (w_gu_hbm, w_gu, 4), (w_d_hbm, w_d, 2)), start=1
    ):
        size = src.shape[0] // pieces
        weights.append(
            [
                pltpu.make_async_copy(src.at[pl.ds(p * size, size)], dst.at[pl.ds(p * size, size)], sem_w.at[i, p])
                for p in range(pieces)
            ]
        )

    def rows(m):
        return pl.ds(m * SEG, SEG)

    def load_tokens(m):
        return pltpu.make_async_copy(tokens.at[rows(m)], xs.at[m], sem_in.at[0, m])

    def load_cotangent(m):
        return pltpu.make_async_copy(cotangent.at[rows(m)], grads.at[m], sem_in.at[1, m])

    def send_up(m):
        return pltpu.make_async_remote_copy(
            src_ref=y_low.at[m], dst_ref=xs.at[m], send_sem=sem_send.at[0, m], recv_sem=sem_recv.at[0, m],
            device_id=twin, device_id_type=MESH,
        )

    def send_down(m):
        return pltpu.make_async_remote_copy(
            src_ref=gx.at[m], dst_ref=grads.at[m], send_sem=sem_send.at[1, m], recv_sem=sem_recv.at[1, m],
            device_id=twin, device_id_type=MESH,
        )

    @pl.when(is_lower)
    def _():
        load_tokens(0).start()

    for copy in weights[0]:
        copy.start()

    @pl.when(is_lower)
    def _():
        load_tokens(1).start()

    memory_in = [
        pltpu.make_async_copy(src.at[m], factors.at[m, :, cols(i, D)], sem_mem.at[i, m])
        for m in range(MICRO)
        for i, src in enumerate((mem_k, mem_v))
    ]

    @pl.when(is_upper)
    def _():
        for copy in memory_in:
            copy.start()
        for m in range(MICRO):
            load_cotangent(m).start()

    for group_copies in weights[1:]:
        for copy in group_copies:
            copy.start()

    barrier = pltpu.get_barrier_semaphore()
    pl.semaphore_signal(barrier, inc=1, device_id=twin, device_id_type=MESH)
    pl.semaphore_signal(barrier, inc=1, device_id=first, device_id_type=MESH)
    pl.semaphore_signal(barrier, inc=1, device_id=near, device_id_type=MESH)
    @pl.when(is_lower)
    def _():
        picked_k[...] = jnp.zeros_like(picked_k)
        picked_v[...] = jnp.zeros_like(picked_v)

    @pl.when(is_upper)
    def _():
        for copy in memory_in:
            copy.wait()
        places = lax.broadcasted_iota(jnp.int32, (SEG, TOPM), 0)
        for m in range(MICRO):
            chosen = to_low(to_f32(index[m : m + 1, :] == places).T)
            for n in range(4):
                picked_k[m, :, cols(n)] = to_low(times(chosen, factors[m, :, cols(n)]))
                picked_v[m, :, cols(n)] = to_low(times(chosen, factors[m, :, cols(n, BLOCK, D)]))

    sent = []

    def exchange(src, dst, at, device=first):
        copy = pltpu.make_async_remote_copy(
            src_ref=src, dst_ref=dst, send_sem=sem_xsend.at[at], recv_sem=sem_xrecv.at[at],
            device_id=device, device_id_type=MESH,
        )
        copy.start()
        return copy

    def exchange_grads(src, m):
        return exchange(src, e_p.at[rows(m)], 10 + m, near)

    def meet():
        pl.semaphore_wait(barrier, 3)

        @pl.when(is_upper)
        def _():
            for m in range(MICRO):
                exchange_grads(cotangent.at[rows(m)], m)

    meet()

    def local(src, dst, sem):
        copy = pltpu.make_async_copy(src, dst, sem)
        copy.start()
        sent.append(copy)

    def share_kept(kind, out, partner_out, m):
        view = kept.at[m, kind]
        local(view, out.at[rows(m)], sem_t.at[kind, m])
        sent.append(exchange(view, partner_out.at[rows(m)], kind * MICRO + m))

    def forward(m):
        @pl.when(is_lower)
        def _():
            load_tokens(m).wait()

        @pl.when(is_upper)
        def _():
            send_up(m).wait_recv()

        x = to_f32(xs[m])
        normed = kept.at[m, 0]
        normed[...] = to_low(x * inverse_rms(x) * to_f32(gain_a[...]))
        def need_qkv(block):
            if m == 0 and block == 0:
                for copy in weights[0]:
                    copy.wait()

        def rotated(j):
            need_qkv(j)
            block = times(normed[...], w_qkv[:, cols(j)])
            for p in range(2):
                part = block[:, p * HEAD_DIM : (p + 1) * HEAD_DIM]
                part = part * cosine[...] + pltpu.roll(part, HEAD_DIM // 2, 1) * sine[...]
                qkv[m, :, cols(2 * j + p, HEAD_DIM)] = to_low(part)

        for i in range(8):
            rotated(i)

        def plain(j):
            need_qkv(8 + j)
            qkv[m, :, cols(j, BLOCK, 2 * D)] = to_low(times(normed[...], w_qkv[:, cols(j, BLOCK, 2 * D)]))

        for i in range(4):
            plain(i)
        share_kept(0, na_all, na_p, m)
        attended = kept.at[m, 1]
        steep = scale * 1.4426950408889634
        ones = jnp.ones((SEG, HEAD_DIM), jnp.bfloat16)
        bias = (1 - flags[m] * section).astype(jnp.float32) * NEG
        causal = lax.broadcasted_iota(jnp.int32, (SEG, SEG), 0) >= lax.broadcasted_iota(jnp.int32, (SEG, SEG), 1)

        def head(h):
            query = qkv[m, :, cols(h, HEAD_DIM)]
            local = by_rows(query, qkv[m, :, cols(h, HEAD_DIM, D)])
            local = jnp.where(causal, local, NEG)
            remote = by_rows(query, picked_k[m, :, cols(h, HEAD_DIM)]) + bias
            peak = jnp.maximum(
                jnp.max(local, axis=-1, keepdims=True), jnp.max(remote, axis=-1, keepdims=True)
            )
            local = jnp.exp2((local - peak) * steep)
            remote = jnp.exp2((remote - peak) * steep)
            value = jnp.concatenate([qkv[m, :, cols(h, HEAD_DIM, 2 * D)], ones], axis=1)
            value_m = jnp.concatenate([picked_v[m, :, cols(h, HEAD_DIM)], ones[:TOPM]], axis=1)
            result = times(to_low(local), value) + times(to_low(remote), value_m)
            share = 1.0 / result[:, HEAD_DIM:]
            attended[:, cols(h, HEAD_DIM)] = to_low(result[:, :HEAD_DIM] * share)
            probs[m, h, :, :HEAD_DIM] = to_low(local[:, :HEAD_DIM] * share)
            probs[m, h, :, HEAD_DIM:SEG] = to_low(local[:, HEAD_DIM:] * share)
            probs[m, h, :, SEG:] = to_low(remote * share)

        for i in range(HEADS):
            head(i)
        if m == 0:
            weights[1][0].wait()

        def project(n):
            resid[m, :, cols(n)] = to_f32(xs[m, :, cols(n)]) + times(attended[...], w_o[:, cols(n)])

        for i in range(4):
            project(i)
        share_kept(1, o_all, o_p, m)
        normed_ffn = kept.at[m, 2]
        h = resid[m]
        normed_ffn[...] = to_low(h * inverse_rms(h) * to_f32(gain_f[...]))
        if m == 0:
            for copy in weights[2]:
                copy.wait()

        def gate(j):
            a = times(normed_ffn[...], w_gu[:, cols(j)])
            u = times(normed_ffn[...], w_gu[:, cols(j, BLOCK, FF)])
            sg = jax.nn.sigmoid(a)
            silu = a * sg
            hidden[m, :, cols(j)] = to_low(silu * u)
            factors[m, :, cols(j)] = to_low(u * sg * (1.0 + a * (1.0 - sg)))
            factors[m, :, cols(j, BLOCK, FF)] = to_low(silu)

        for i in range(FF // BLOCK):
            gate(i)
        if m == 0:
            for copy in weights[3]:
                copy.wait()

        def down(n):
            y_low[m, :, cols(n)] = to_low(resid[m, :, cols(n)] + times(hidden[m], w_d[:, cols(n)]))

        for i in range(4):
            down(i)

        @pl.when(is_lower)
        def _():
            send_up(m).start()

        write_out(y_low.at[m], act.at[rows(m)], 0, m).start()
        share_kept(2, nf_all, nf_p, m)
        local(hidden.at[m], z_all.at[rows(m)], sem_t.at[3, m])
        for j in range(2):
            span = hidden.at[m, :, down_span(j, 1 - bit0)]
            sent.append(exchange(span, z_p.at[j, rows(m)], 3 * MICRO + 2 * m + j, near))

    def write_out(src, dst, kind, m):
        return pltpu.make_async_copy(src, dst, sem_out.at[kind, m])

    block_sets = ((grads, e_cols, 2), (factors, dgu, 3), (f_low, f_cols, 4), (qkv, dm, 5))

    def blocks_out(which, m):
        src, dst, kind = block_sets[which]
        return write_out(src.at[m], dst.at[rows(m)], kind, m)

    def norm_back(d_normed, values, gain, incoming):
        inverse = inverse_rms(values)
        scaled = d_normed * to_f32(gain)
        column = jnp.sum(d_normed * (values * inverse), axis=0, keepdims=True)
        centre = jnp.mean(scaled * values, axis=-1, keepdims=True)
        return incoming + inverse * scaled - values * (inverse * inverse * inverse * centre), column

    def backward(m):
        @pl.when(is_upper)
        def _():
            load_cotangent(m).wait()

        @pl.when(is_lower)
        def _():
            send_down(m).wait_recv()

        blocks_out(0, m).start()

        @pl.when(is_lower)
        def _():
            exchange_grads(grads.at[m], m)

        def gate_back(j):
            dz = by_rows(grads[m], w_d[cols(j), :])
            factors[m, :, cols(j)] = to_low(dz * to_f32(factors[m, :, cols(j)]))
            factors[m, :, cols(j, BLOCK, FF)] = to_low(dz * to_f32(factors[m, :, cols(j, BLOCK, FF)]))

        for i in range(FF // BLOCK):
            gate_back(i)
        blocks_out(1, m).start()
        if m == 0:
            sent.append(exchange(factors.at[m, :, cols(1 - half, FF)], dgu_p, 12))

        def gate_up_back(n):
            wide[:, cols(n)] = by_rows(factors[m], w_gu[cols(n), :])

        for i in range(4):
            gate_up_back(i)
        result, column = norm_back(wide[...], resid[m], gain_f[...], to_f32(grads[m]))
        dh[...] = result
        f_low[m] = to_low(result)
        gains[1:2, :] = column if m == 0 else gains[1:2, :] + column
        blocks_out(2, m).start()

        def out_back(n):
            d_att[:, cols(n)] = to_low(by_rows(f_low[m], w_o[cols(n), :]))

        for i in range(4):
            out_back(i)

        def rotate_back(part):
            return part * cosine[...] - pltpu.roll(part, HEAD_DIM // 2, 1) * sine[...]

        def head_back(h):
            at_q, at_k, at_v = (cols(h, HEAD_DIM, base) for base in (0, D, 2 * D))
            query, key, value = qkv[m, :, at_q], qkv[m, :, at_k], qkv[m, :, at_v]
            d_out = d_att[:, cols(h, HEAD_DIM)]
            p_local = probs[m, h, :, :SEG]
            p_remote = probs[m, h, :, SEG:]
            d_local = by_rows(d_out, value)
            d_remote = by_rows(d_out, picked_v[m, :, cols(h, HEAD_DIM)])
            wide_local, wide_remote = to_f32(p_local), to_f32(p_remote)
            centre = jnp.sum(to_f32(d_out) * to_f32(kept[m, 1, :, cols(h, HEAD_DIM)]), axis=-1, keepdims=True)
            d_local = to_low(wide_local * (d_local - centre))
            d_remote = to_low(wide_remote * (d_remote - centre))
            d_query = (times(d_local, key) + times(d_remote, picked_k[m, :, cols(h, HEAD_DIM)])) * scale
            d_key = by_tokens(d_local, query) * scale
            qkv[m, :, at_v] = to_low(by_tokens(p_local, d_out))
            qkv[m, :, at_q] = to_low(rotate_back(d_query))
            qkv[m, :, at_k] = to_low(rotate_back(d_key))

        for i in range(HEADS):
            head_back(i)
        blocks_out(3, m).start()

        def qkv_back(n):
            wide[:, cols(n)] = by_rows(qkv[m], w_qkv[cols(n), :])

        for i in range(4):
            qkv_back(i)
        result, column = norm_back(wide[...], to_f32(xs[m]), gain_a[...], dh[...])
        gx[m] = to_low(result)
        gains[0:1, :] = column if m == 0 else gains[0:1, :] + column

        @pl.when(is_upper)
        def _():
            send_down(m).start()

        write_out(gx.at[m], igrad.at[rows(m)], 1, m).start()

    gains[...] = jnp.zeros_like(gains)
    for m in range(MICRO):
        forward(m)
    for m in range(MICRO):
        backward(m)

    for m in range(MICRO):
        write_out(y_low.at[m], act.at[rows(m)], 0, m).wait()
        write_out(gx.at[m], igrad.at[rows(m)], 1, m).wait()
        for which in range(4):
            blocks_out(which, m).wait()
    for copy in sent:
        copy.wait()
    for m in range(MICRO):
        pltpu.make_async_remote_copy(
            src_ref=grads.at[m], dst_ref=e_p.at[rows(m)], send_sem=sem_xsend.at[10 + m],
            recv_sem=sem_xrecv.at[10 + m], device_id=near, device_id_type=MESH,
        ).wait()

    @pl.when(is_lower)
    def _():
        for m in range(MICRO):
            send_up(m).wait_send()

    @pl.when(is_upper)
    def _():
        for m in range(MICRO):
            send_down(m).wait_send()


def rotary_constants():
    half = HEAD_DIM // 2
    freqs = np.exp(-np.log(10000.0) * np.arange(half) * 2.0 / HEAD_DIM)
    angles = np.arange(SEG)[:, None] * freqs[None, :]
    cosine = np.concatenate([np.cos(angles), np.cos(angles)], axis=1)
    sine = np.concatenate([-np.sin(angles), np.sin(angles)], axis=1)
    return cosine.astype(np.float32), sine.astype(np.float32)


def run_layers(tokens, cotangent, mem_keys, mem_values, index, flags, gain_a, gain_f, w_qkv, w_o, w_gu, w_d):
    cosine, sine = rotary_constants()
    count = tokens.shape[0]
    low, wide = jnp.bfloat16, jnp.float32
    anywhere = pl.BlockSpec(memory_space=pl.ANY)
    near_by = pl.BlockSpec(memory_space=pltpu.VMEM)
    shape = jax.ShapeDtypeStruct
    outs = (
        shape((count, D), low),
        shape((count, D), low),
        shape((count, D), low),
        shape((count, D), low),
        shape((count, D), low),
        shape((count, FF), low),
        shape((count, 2 * FF), low),
        shape((count, 3 * D), low),
        shape((count, D), low),
        shape((count, D), low),
        shape((count, D), low),
        shape((count, D), low),
        shape((count, D), low),
        shape((2, count, 768), low),
        shape((SEG, FF), low),
        shape((count, D), low),
        shape((8, D), wide),
    )
    scratch = [
        pltpu.VMEM((D, 3 * D), low),
        pltpu.VMEM((D, D), low),
        pltpu.VMEM((D, 2 * FF), low),
        pltpu.VMEM((FF, D), low),
        pltpu.VMEM((MICRO, SEG, D), low),
        pltpu.VMEM((MICRO, SEG, 3 * D), low),
        pltpu.VMEM((MICRO, HEADS, SEG, SEG + TOPM), low),
        pltpu.VMEM((MICRO, SEG, D), wide),
        pltpu.VMEM((MICRO, SEG, 2 * FF), low),
        pltpu.VMEM((MICRO, SEG, D), low),
        pltpu.VMEM((MICRO, TOPM, D), low),
        pltpu.VMEM((MICRO, TOPM, D), low),
        pltpu.VMEM((MICRO, 3, SEG, D), low),
        pltpu.VMEM((MICRO, SEG, FF), low),
        pltpu.VMEM((MICRO, SEG, D), low),
        pltpu.VMEM((SEG, D), wide),
        pltpu.VMEM((SEG, D), wide),
        pltpu.VMEM((MICRO, SEG, D), low),
        pltpu.VMEM((SEG, D), low),
        pltpu.VMEM((MICRO, SEG, D), low),
        pltpu.SemaphoreType.DMA((4, 4)),
        pltpu.SemaphoreType.DMA((2, MICRO)),
        pltpu.SemaphoreType.DMA((2, MICRO)),
        pltpu.SemaphoreType.DMA((4, MICRO)),
        pltpu.SemaphoreType.DMA((6, MICRO)),
        pltpu.SemaphoreType.DMA((2, MICRO)),
        pltpu.SemaphoreType.DMA((2, MICRO)),
        pltpu.SemaphoreType.DMA((13,)),
        pltpu.SemaphoreType.DMA((13,)),
    ]
    return pl.pallas_call(
        layer_kernel,
        out_shape=outs,
        in_specs=[anywhere] * 4
        + [near_by, pl.BlockSpec(memory_space=pltpu.SMEM)]
        + [near_by] * 4
        + [anywhere] * 4,
        out_specs=(anywhere,) * 16 + (near_by,),
        scratch_shapes=scratch,
        compiler_params=pltpu.CompilerParams(
            collective_id=1, has_side_effects=True, vmem_limit_bytes=60 * 2**20
        ),
        cost_estimate=pl.CostEstimate(flops=27 * 10**9, bytes_accessed=50 * 10**6, transcendentals=0),
        name="relay_layers",
    )(tokens, cotangent, mem_keys, mem_values, index, flags, cosine, sine, gain_a, gain_f, w_qkv, w_o, w_gu, w_d)


def finish_kernel(*refs):
    (sq, down, gains, act, igrad) = refs[:5]
    (gu_out, o_out, qkv_out, d_out, ga_out, gf_out, act_out, igrad_out) = refs[5:13]
    (sq_v, d_v, gu_v, o_v, qkv_v, down_v, pass_v, sem_in, sem_out) = refs[13:]
    parts = (
        (gu_v, gu_out, 0, 11),
        (qkv_v, qkv_out, 13, 6),
        (o_v, o_out, 11, 2),
    )
    loads = [
        [
            pltpu.make_async_copy(
                sq.at[half, pl.ds(base, count)], sq_v.at[half, pl.ds(base, count)], sem_in.at[2 * i + half]
            )
            for half in range(2)
        ]
        for i, (_, _, base, count) in enumerate(parts)
    ]
    load_d = pltpu.make_async_copy(down, d_v, sem_in.at[6])
    passed = [
        (pltpu.make_async_copy(src, pass_v.at[i], sem_in.at[7 + i]), pltpu.make_async_copy(pass_v.at[i], dst, sem_out.at[8 + i]))
        for i, (src, dst) in enumerate(((act, act_out), (igrad, igrad_out)))
    ]
    for pair in loads:
        for copy in pair:
            copy.start()
    load_d.start()
    for load, _ in passed:
        load.start()
    stores = []
    mine = cols(lax.axis_index("dp"))
    ga_out[...] = gains[0:1, mine]
    gf_out[...] = gains[1:2, mine]
    for i, (view, out, base, count) in enumerate(parts):
        for half in range(2):
            loads[i][half].wait()
            for c in range(count):
                at = pl.ds((half * count + c) * BLOCK, BLOCK)
                view[:, at] = sq_v[half, base + c].astype(jnp.float32)
            span = pl.ds(half * count * BLOCK, count * BLOCK)
            stores.append(pltpu.make_async_copy(view.at[:, span], out.at[:, span], sem_out.at[2 * i + half]))
            stores[-1].start()
    for load, store in passed:
        load.wait()
        store.start()
        stores.append(store)
    load_d.wait()
    for half in range(2):
        for k in range(4):
            down_v[pl.ds(half * 352, 352), pl.ds(k * BLOCK, BLOCK)] = d_v[half, k].astype(jnp.float32)
        span = pl.ds(half * 352, 352)
        stores.append(pltpu.make_async_copy(down_v.at[span], d_out.at[span], sem_out.at[6 + half]))
        stores[-1].start()
    for copy in stores:
        copy.wait()


def finish_gradients(out_sq, out_d, out_gains, act, igrad):
    anywhere = pl.BlockSpec(memory_space=pl.ANY)
    near_by = pl.BlockSpec(memory_space=pltpu.VMEM)
    shapes = ((256, 2 * FF), (256, D), (256, 3 * D), (704, D))
    wide = jnp.float32
    return pl.pallas_call(
        finish_kernel,
        out_shape=tuple(jax.ShapeDtypeStruct(shape, wide) for shape in shapes + ((1, BLOCK),) * 2)
        + (jax.ShapeDtypeStruct(act.shape, act.dtype),) * 2,
        in_specs=[anywhere] * 2 + [near_by] + [anywhere] * 2,
        out_specs=(anywhere,) * 4 + (near_by,) * 2 + (anywhere,) * 2,
        scratch_shapes=[pltpu.VMEM(out_sq.shape, jnp.bfloat16), pltpu.VMEM(out_d.shape, jnp.bfloat16)]
        + [pltpu.VMEM(shape, wide) for shape in shapes]
        + [pltpu.VMEM((2,) + act.shape, act.dtype)]
        + [pltpu.SemaphoreType.DMA((9,)), pltpu.SemaphoreType.DMA((10,))],
        compiler_params=pltpu.CompilerParams(vmem_limit_bytes=60 * 2**20),
        name="finish_gradients",
    )(out_sq, out_d, out_gains, act, igrad)


def body(
    group_size,
    tokens,
    cotangent,
    mem_keys,
    mem_values,
    mem_index,
    mem_flags,
    norm_attn,
    w_qkv,
    w_out,
    norm_ffn,
    w_gate_up,
    w_down,
):
    (act, igrad, na_all, nf_all, o_all, z_all, dgu, dm, f_cols, e_cols, na_p, nf_p, o_p, z_p, dgu_p, e_p, gains) = run_layers(
        tokens,
        cotangent,
        mem_keys,
        mem_values,
        mem_index,
        mem_flags,
        norm_attn,
        norm_ffn,
        w_qkv[0],
        w_out[0],
        w_gate_up[0],
        w_down[0],
    )
    reduced = reduce_gradients(
        group_size,
        (nf_all, na_all, o_all, z_all, dgu, dm, f_cols, e_cols, nf_p, na_p, o_p, z_p, dgu_p, e_p),
        gains,
    )
    (grad_gu, grad_o, grad_qkv, grad_d, grad_na, grad_nf, act, igrad) = finish_gradients(*reduced, act, igrad)
    return (
        act[None],
        igrad[None],
        grad_na,
        grad_qkv[None],
        grad_o[None],
        grad_nf,
        grad_gu[None],
        grad_d[None],
    )


def solution(mesh):
    placed = (
        P(("dp", "group"), None),
        P(("dp", "group"), None),
        P(("dp", "group"), None, None),
        P(("dp", "group"), None, None),
        P(("dp", "group"), None),
        P(("dp", "group")),
        P("section", None),
        P("section", None, None),
        P("section", None, None),
        P("section", None),
        P("section", None, None),
        P("section", None, None),
    )
    return jax.shard_map(
        functools.partial(body, mesh.shape["group"]),
        mesh=mesh,
        in_specs=placed,
        out_specs=(
            P("section", ("dp", "group"), None),
            P("section", ("dp", "group"), None),
            P("section", "dp"),
            P("section", "dp", None),
            P("section", "dp", None),
            P("section", "dp"),
            P("section", "dp", None),
            P("section", "dp", None),
        ),
        check_vma=False,
    )
```
